32 devices in a mesh: section: 2 (over x), dp: 16 (over z, y, core).
Axes of the slice: x: 2, y: 2, z: 4, core: 2. Of those that a mesh axis runs over, the one named last changes fastest.
Arguments:
- start_state: bfloat16 [32, 1024, 256], P('dp'), may hold values from -6 to 6
- embedded: bfloat16 [32, 1024, 256], P('dp'), may hold values from -6 to 6
- cotangent: bfloat16 [32, 1024, 256], P('dp'), may hold values from -6 to 6
- segment_ids: int32 [32, 1024], P('dp'), may hold values from 0 to 7, never falling along the last dimension, each value on 1 to 512 neighbouring positions
- pad_lengths: int32 [32], P('dp'), may hold values from 0 to 128
- norm1_gain: float32 [256], replicated, may hold values from 0.1 to 1.9
- norm1_bias: float32 [256], replicated, may hold values from -1.5 to 1.5
- w_qkv: bfloat16 [256, 768], replicated, may hold values from -0.375 to 0.375
- q_bias: float32 [256], replicated, may hold values from -2.5 to 2.5
- v_bias: float32 [256], replicated, may hold values from -2.5 to 2.5
- w_out: bfloat16 [256, 256], replicated, may hold values from -2 to 2
- out_bias: float32 [256], replicated, may hold values from -1.5 to 1.5
- norm2_gain: float32 [256], replicated, may hold values from 0.1 to 1.9
- norm2_bias: float32 [256], replicated, may hold values from -1.5 to 1.5
- w_up: bfloat16 [256, 1024], replicated, may hold values from -0.375 to 0.375
- up_bias: float32 [1024], replicated, may hold values from -2.5 to 2.5
- w_down: bfloat16 [1024, 256], replicated, may hold values from -0.1875 to 0.1875
- down_bias: float32 [256], replicated, may hold values from -1.5 to 1.5
Outputs:
- loop_states: bfloat16 [2, 32, 1024, 256], P('section', 'dp')
- state_grads: float32 [2, 32, 1024, 256], P('section', 'dp')
- embed_grad: float32 [32, 1024, 256], P('dp', 'section')
- grad_norm1_gain: float32 [256], replicated
- grad_norm1_bias: float32 [256], replicated
- grad_w_qkv: float32 [256, 768], replicated
- grad_q_bias: float32 [256], replicated
- grad_v_bias: float32 [256], replicated
- grad_w_out: float32 [256, 256], replicated
- grad_out_bias: float32 [256], replicated
- grad_norm2_gain: float32 [256], replicated
- grad_norm2_bias: float32 [256], replicated
- grad_w_up: float32 [256, 1024], replicated
- grad_up_bias: float32 [1024], replicated
- grad_w_down: float32 [1024, 256], replicated
- grad_down_bias: float32 [256], replicated
The draws below stay inside these ranges and needn't reach their ends.
All inputs are finite; a program needn't handle non-finite values.
Results may differ from the reference program's by a relative error of at most 0.015.
Values may be sent and summed in bfloat16 or wider, within the bound.
A program may use at most 320 MiB of HBM per device.

```python
import math
import jax
import jax.numpy as jnp
import numpy as np
from jax import lax

D = 256
HEADS = 4
HEAD_DIM = 64
FF = 1024
SEQ = 1024
ROWS = 32


def plant(result, stream_key, least, high):
    extent = result.shape
    index_at = [jax.random.randint(jax.random.fold_in(stream_key, axis), (), 0, extent[axis]) for axis in range(len(extent))]
    result = result.at[tuple(index_at)].set(least)
    longest = extent.index(max(extent))
    index_at[longest] = (index_at[longest] + 1) % extent[longest]
    return result.at[tuple(index_at)].set(high)


def block_levels(key, extent, shards, smallest, largest):
    def one(dim, shards_of):
        steps = jax.random.uniform(jax.random.fold_in(jax.random.fold_in(key, 6), dim), (shards_of,), jnp.float32, smallest / len(shards), largest / len(shards))
        return jnp.repeat(jnp.exp(steps), extent[dim] // shards_of).reshape((-1,) + (1,) * (len(extent) - dim - 1))

    level = one(*shards[0])
    for cut in shards[1:]:
        level = level * one(*cut)
    return level


def profile(amount, total, limit, skew):
    loads = [(1 << 20) // math.isqrt(grade ** skew) + 1 for grade in range(2, amount + 1)]
    surplus, given = total - limit - (amount - 1), [1] * (amount - 1)
    while surplus > 0:
        candidates = [i for i in range(amount - 1) if given[i] < limit]
        mass, budget = sum([loads[i] for i in candidates]), surplus
        for i in candidates:
            more = min(limit - given[i], max(1, budget * loads[i] // mass), surplus)
            given[i] = given[i] + more
            surplus = surplus - more
    return np.array([limit] + given)


def ragged_sizes(key, count, total, reach, lean):
    if count == 2:
        one = jax.random.randint(key, (), max(1, total - reach), min(reach, total - 1) + 1)
        return jnp.stack([one, total - one])
    sizes = jnp.asarray(profile(count, total, reach, lean), jnp.int32)
    twos = (count - 1) // 2
    giver, receiver = sizes[1:1 + 2 * twos:2], sizes[2:2 + 2 * twos:2]
    margin = jnp.minimum(giver - 1, reach - receiver)
    shifted = jax.random.randint(jax.random.fold_in(key, 1), (twos,), 0, 1 << 20) % (margin + 1)
    sizes = sizes.at[1:1 + 2 * twos:2].set(giver - shifted).at[2:2 + 2 * twos:2].set(receiver + shifted)
    return sizes[jax.random.permutation(jax.random.fold_in(key, 2), count)]


def noise(rng, dims, scale, most, shards=(), held_as=jnp.bfloat16):
    result = jax.random.normal(rng, dims, jnp.float32) * scale
    if len(shards) > 0:
        result = block_levels(rng, dims, shards, -0.22, 0.18) * result
    return jnp.clip(result, min=-most, max=most).astype(held_as)


def setup_inputs(seed: int = 0) -> dict:
    keys = jax.random.split(jax.random.key(seed), 19)
    start_state = noise(keys[0], (ROWS, SEQ, D), 1.0, 6.0, ((0, 16),))
    embedded = noise(keys[1], (ROWS, SEQ, D), 1.0, 6.0, ((0, 16),))
    cotangent = noise(keys[2], (ROWS, SEQ, D), 1.0, 6.0, ((0, 16),))
    segment_ids = jax.vmap(lambda own: jnp.searchsorted(jnp.cumsum(ragged_sizes(own, max(SEQ // 128, 4), SEQ, SEQ // 2, 2)), jnp.arange(SEQ), side="right"))(jax.random.split(keys[3], ROWS)).reshape((ROWS, SEQ)).astype(jnp.int32)
    pad_lengths = plant(jax.random.randint(keys[4], (ROWS,), 0, SEQ // 8 + 1), jax.random.fold_in(keys[4], 1), 0, (SEQ // 8 + 1) - 1).astype(jnp.int32)
    norm1_gain = jnp.clip(1.0 + 0.18 * jax.random.normal(keys[5], (D,), jnp.float32), 0.1, 1.9)
    norm1_bias = noise(keys[6], (D,), 0.3, 1.5, (), jnp.float32)
    w_qkv = noise(keys[7], (D, 3 * D), D ** -0.5, 0.375)
    q_bias = noise(keys[8], (D,), 0.5, 2.5, (), jnp.float32)
    v_bias = noise(keys[9], (D,), 0.5, 2.5, (), jnp.float32)
    w_out = noise(keys[10], (D, D), (D // 32) ** -0.5, 2.0)
    out_bias = noise(keys[11], (D,), 0.3, 1.5, (), jnp.float32)
    norm2_gain = jnp.clip(1.0 + 0.18 * jax.random.normal(keys[12], (D,), jnp.float32), 0.1, 1.9)
    norm2_bias = noise(keys[13], (D,), 0.3, 1.5, (), jnp.float32)
    w_up = noise(keys[14], (D, FF), D ** -0.5, 0.375)
    up_bias = noise(keys[15], (FF,), 0.5, 2.5, (), jnp.float32)
    w_down = noise(keys[16], (FF, D), FF ** -0.5, 0.1875)
    down_bias = noise(keys[17], (D,), 0.3, 1.5, (), jnp.float32)
    return {"start_state": start_state, "embedded": embedded, "cotangent": cotangent, "segment_ids": segment_ids, "pad_lengths": pad_lengths, "norm1_gain": norm1_gain, "norm1_bias": norm1_bias, "w_qkv": w_qkv, "q_bias": q_bias, "v_bias": v_bias, "w_out": w_out, "out_bias": out_bias, "norm2_gain": norm2_gain, "norm2_bias": norm2_bias, "w_up": w_up, "up_bias": up_bias, "w_down": w_down, "down_bias": down_bias}


@jax.custom_vjp
def low(v):
    return lax.optimization_barrier(v.astype(jnp.bfloat16)).astype(jnp.float32)

@jax.custom_vjp
def low_back(v):
    return v

def low_keep(v):
    return (low(v), None)

def low_pass(kept, grad):
    return (grad,)

def back_keep(v):
    return (v, None)

def back_low(kept, grad):
    return (low(grad),)
low.defvjp(low_keep, low_pass)
low_back.defvjp(back_keep, back_low)
norm_eps = 1e-05
masked_score = -1e+30

def round_both(value):
    return low(low_back(value))

def matmul(left, right):
    return jnp.einsum('...i,ij->...j', left, right, precision=lax.Precision.HIGHEST)

def layer_norm(values, norm_gain, norm_shift):
    average = lax.optimization_barrier(jnp.mean(values, axis=-1, keepdims=True))
    centred = values - average
    spread = lax.optimization_barrier(jnp.mean(centred * centred, axis=-1, keepdims=True))
    return centred * lax.rsqrt(spread + norm_eps) * norm_gain + norm_shift

def allowed(segment_part, pad_part):
    places = jnp.arange(SEQ, dtype=jnp.int32)
    same_segment = segment_part[:, :, None] == segment_part[:, None, :]
    causal = places[:, None] >= places[None, :]
    key_live = places[None, None, :] < (SEQ - pad_part)[:, None, None]
    self_pair = places[:, None] == places[None, :]
    return same_segment & causal[None] & (key_live | self_pair[None])

def attend(queries, key_rows, value_rows, allowed_mask):
    row_count = queries.shape[0]
    queries = queries.reshape(row_count, SEQ, HEADS, HEAD_DIM)
    key_rows = key_rows.reshape(row_count, SEQ, HEADS, HEAD_DIM)
    value_rows = value_rows.reshape(row_count, SEQ, HEADS, HEAD_DIM)
    scores = jnp.einsum('rqhe,rkhe->rhqk', queries, key_rows, precision=lax.Precision.HIGHEST) * HEAD_DIM ** (-0.5)
    scores = low_back(scores)
    scores = jnp.where(allowed_mask[:, None], scores, masked_score)
    probabilities = low(jax.nn.softmax(scores, axis=-1))
    attended = jnp.einsum('rhqk,rkhe->rqhe', probabilities, value_rows, precision=lax.Precision.HIGHEST)
    return attended.reshape(row_count, SEQ, D)

def shared_block(inputs, weights, allowed_mask):
    norm1_gain, norm1_bias, w_qkv, q_bias, v_bias, w_out, out_bias, norm2_gain, norm2_bias, w_up, up_bias, w_down, down_bias = weights
    normed = low(layer_norm(inputs, norm1_gain, norm1_bias))
    projected = matmul(normed, w_qkv)
    queries = round_both(projected[..., :D] + q_bias)
    key_rows = round_both(projected[..., D:2 * D])
    value_rows = round_both(projected[..., 2 * D:] + v_bias)
    attended = round_both(attend(queries, key_rows, value_rows, allowed_mask))
    middle = inputs + low_back(matmul(attended, w_out) + out_bias)
    normed_two = low(layer_norm(middle, norm2_gain, norm2_bias))
    hidden = low_back(matmul(normed_two, w_up) + up_bias)
    active = low(jax.nn.gelu(hidden, approximate=False))
    return middle + low_back(matmul(active, w_down) + down_bias)

def forward(state_in, embed_in, shift_in, weights, allowed_mask):
    first_out = shared_block(state_in + embed_in, weights, allowed_mask)
    between = low_back(low(first_out)) + shift_in
    final_state = shared_block(between + embed_in, weights, allowed_mask)
    return (final_state, between)

def reference(start_state, embedded, cotangent, segment_ids, pad_lengths, norm1_gain, norm1_bias, w_qkv, q_bias, v_bias, w_out, out_bias, norm2_gain, norm2_bias, w_up, up_bias, w_down, down_bias):
    params = (norm1_gain, norm1_bias, w_qkv.astype(jnp.float32), q_bias, v_bias, w_out.astype(jnp.float32), out_bias, norm2_gain, norm2_bias, w_up.astype(jnp.float32), up_bias, w_down.astype(jnp.float32), down_bias)
    row_group = 4
    row_blocks = ROWS // row_group

    def regroup(array):
        return array.reshape((row_blocks, row_group) + array.shape[1:])
    row_pieces = (regroup(start_state), regroup(embedded), regroup(cotangent), regroup(segment_ids), regroup(pad_lengths))

    def visit_rows(totals, row_piece):
        state_part, embed_part, cot_part, segment_part, pad_part = row_piece
        allowed_mask = allowed(segment_part, pad_part)
        zero_shift = jnp.zeros(state_part.shape, jnp.float32)

        def run_layers(state_in, embed_in, shift_in, *weights):
            return forward(state_in, embed_in, shift_in, weights, allowed_mask)
        outputs, pullback = jax.vjp(run_layers, state_part.astype(jnp.float32), embed_part.astype(jnp.float32), zero_shift, *params)
        final_state, between = outputs
        gradients = pullback((cot_part.astype(jnp.float32), jnp.zeros_like(between)))
        totals = tuple((total + grad_term for total, grad_term in zip(totals, gradients[3:])))
        return (totals, (between.astype(jnp.bfloat16), final_state.astype(jnp.bfloat16), gradients[0], gradients[2], gradients[1]))
    initial = tuple((jnp.zeros(leaf_value.shape, jnp.float32) for leaf_value in params))
    totals, stacked = lax.scan(visit_rows, initial, row_pieces)

    def unstack(array):
        return array.reshape((ROWS,) + array.shape[2:])
    between_all = unstack(stacked[0])
    final_all = unstack(stacked[1])
    first_grads = unstack(stacked[2])
    second_grads = unstack(stacked[3])
    embed_all = unstack(stacked[4])
    loop_states = jnp.stack([between_all, final_all])
    state_grads = jnp.stack([first_grads, second_grads])
    return (loop_states, state_grads, embed_all, totals[0], totals[1], totals[2], totals[3], totals[4], totals[5], totals[6], totals[7], totals[8], totals[9], totals[10], totals[11], totals[12])
```

```python
from functools import partial

import jax
import jax.numpy as jnp
from jax import lax
from jax.experimental import pallas as pl
from jax.experimental.pallas import tpu as pltpu
from jax.sharding import PartitionSpec as P

HEADS = 4
HEAD_DIM = 64
BLOCK = 256
SPAN = 512
norm_eps = 1e-05
masked_score = -1e30
bf16 = jnp.bfloat16
f32 = jnp.float32


def mul(left, right):
    return jnp.dot(left, right, preferred_element_type=f32)


def mul_rows(left, right):
    return lax.dot_general(left, right, (((1,), (1,)), ((), ())), preferred_element_type=f32)


def mul_columns(left, right):
    return lax.dot_general(left, right, (((0,), (0,)), ((), ())), preferred_element_type=f32)


def row_of(ref):
    return ref[...].reshape(1, ref.shape[0])


def eight_sums(values):
    rows, width = values.shape
    return jnp.sum(values.reshape(rows // 8, 8, width), axis=0)


def normalise(x):
    average = jnp.mean(x, axis=-1, keepdims=True)
    centred = x - average
    spread = jnp.mean(centred * centred, axis=-1, keepdims=True)
    scale = lax.rsqrt(spread + norm_eps)
    return centred * scale, scale


def norm_back(cotangent, gain, hat, scale):
    scaled = cotangent * gain
    first = jnp.mean(scaled, axis=-1, keepdims=True)
    second = jnp.mean(scaled * hat, axis=-1, keepdims=True)
    return scale * (scaled - first - hat * second)


def blocks_of(length):
    result, store = [], 0
    for b in range(length // BLOCK):
        first = max(0, b - SPAN // BLOCK)
        result.append((b, first, store))
        store += (b + 1 - first) * BLOCK
    return result, store


N1G, N1B, QB, VB, OB, N2G, N2B, DB, UB = (256 * i for i in range(9))
SUMS = 256 * 12


def compute_kernel(
    start_hbm, emb_hbm, cot_hbm, seg_ref, pad_ref,
    g1_ref, b1_ref, wqkv_ref, qb_ref, vb_ref, wout_ref, ob_ref, g2_ref, b2_ref, wup_ref, ub_ref,
    wdown_ref, db_ref,
    state_ref, grad_ref, gqkv_ref, gout_ref, gup_ref, gdown_ref, sums_ref,
    start_v, emb_v, cot_v, qx, kx, xbuf, hat1, scale1, normed1, qa, qt, ka, va, expo, inverse,
    outcome, hat2, scale2, normed2, active, slope, hgrad, branch, mgrad, dout, goa, gt,
    dq, dkt, dvt, pgrad, gdown_t, in_sem,
):
    length, width = xbuf.shape
    count = length // BLOCK
    part = lax.axis_index("section")
    loads = [
        pltpu.make_async_copy(hbm.at[part], dest, in_sem.at[i])
        for i, (hbm, dest) in enumerate(((start_hbm, start_v), (emb_hbm, emb_v), (cot_hbm, cot_v)))
    ]
    for load in loads:
        load.start()

    lane = lax.broadcasted_iota(jnp.int32, (128, 128), 1) & 63
    for c in range(length // 128):
        tokens = slice(c * 128, c * 128 + 128)
        ids = jnp.where(part == 0, seg_ref[0:1, tokens], seg_ref[1:2, tokens]).astype(f32)
        ids = jnp.broadcast_to(ids, (128, 128)).T.astype(jnp.int32)
        same = ids == lane
        qx[tokens, :] = jnp.where((lane < 8) & jnp.logical_not(same), masked_score, 0.0).astype(bf16)
        kx[tokens, :] = jnp.where(same, 1.0, 0.0).astype(bf16)

    for load in loads:
        load.wait()
    xbuf[...] = start_v[...].astype(f32) + emb_v[...].astype(f32)

    low_half = lax.broadcasted_iota(jnp.int32, (BLOCK, 128), 1) < 64
    row_at = lax.broadcasted_iota(jnp.int32, (BLOCK, BLOCK), 0)
    col_at = lax.broadcasted_iota(jnp.int32, (BLOCK, BLOCK), 1)
    ones = jnp.ones((BLOCK, 128), bf16)

    def rows_at(b):
        return pl.ds(pl.multiple_of(b * BLOCK, BLOCK), BLOCK)

    def forward(t, _):
        def project(b, _):
            rows = rows_at(b)
            hat, scale = normalise(xbuf[rows, :])
            normed = (hat * row_of(g1_ref) + row_of(b1_ref)).astype(bf16)
            hat1[t, rows, :] = hat
            scale1[t, rows, :] = jnp.broadcast_to(scale, (BLOCK, 128))
            normed1[t, rows, :] = normed
            q = (mul(normed, wqkv_ref[:, :width]) + row_of(qb_ref)).astype(bf16)
            q = q * jnp.asarray(HEAD_DIM**-0.5, bf16)
            k = mul(normed, wqkv_ref[:, width : 2 * width]).astype(bf16)
            v = (mul(normed, wqkv_ref[:, 2 * width :]) + row_of(vb_ref)).astype(bf16)
            qt[t, :, rows] = q.T
            for pair in range(HEADS // 2):
                lanes = slice(pair * 128, pair * 128 + 128)
                for h, mine in ((2 * pair, low_half), (2 * pair + 1, jnp.logical_not(low_half))):
                    qa[h, rows, :] = jnp.where(mine, q[:, lanes], qx[rows, :])
                    ka[t, h, rows, :] = jnp.where(mine, k[:, lanes], kx[rows, :])
                    va[t, h, rows, :] = jnp.where(mine, v[:, lanes], ones)
            return 0

        lax.fori_loop(0, count, project, 0)

        def attend(pair, _):
            for b, first, store in blocks_of(length)[0]:
                rows = slice(b * BLOCK, b * BLOCK + BLOCK)
                keys = slice(first * BLOCK, b * BLOCK + BLOCK)
                wide = (b + 1 - first) * BLOCK
                live = col_at + b * BLOCK < length - pad_ref[part]
                diagonal = (row_at == col_at) | ((row_at > col_at) & live)
                results = []
                for parity in range(2):
                    h = 2 * pair + parity
                    scores = mul_rows(qa[h, rows, :], ka[t, h, keys, :])
                    last = jnp.where(diagonal, scores[:, wide - BLOCK :], masked_score)
                    if wide > BLOCK:
                        scores = jnp.concatenate([scores[:, : wide - BLOCK], last], axis=1)
                    else:
                        scores = last
                    peak = jnp.max(scores, axis=1, keepdims=True)
                    exps = jnp.exp(scores - peak).astype(bf16)
                    expo[t, h, :, store : store + wide] = exps
                    results.append(mul(exps, va[t, h, keys, :]))
                top = jnp.where(low_half, results[0], results[1])
                total = pltpu.roll(jnp.where(low_half, results[1], results[0]), 64, 1)
                inv = 1.0 / total
                inverse[t, pair, rows, :] = inv
                outcome[t, pair, rows, :] = top * inv
            return 0

        lax.fori_loop(0, HEADS // 2, attend, 0)

        def feed(b, _):
            rows = rows_at(b)
            middle = xbuf[rows, :] + row_of(ob_ref)
            for pair in range(HEADS // 2):
                middle = middle + mul(outcome[t, pair, rows, :].astype(bf16), wout_ref[pair * 128 : pair * 128 + 128, :])
            hat, scale = normalise(middle)
            normed = (hat * row_of(g2_ref) + row_of(b2_ref)).astype(bf16)
            hat2[t, rows, :] = hat
            scale2[t, rows, :] = jnp.broadcast_to(scale, (BLOCK, 128))
            normed2[t, rows, :] = normed
            total = middle + row_of(db_ref)
            for c in range(wup_ref.shape[1] // 256):
                columns = slice(c * 256, c * 256 + 256)
                hidden = mul(normed, wup_ref[:, columns]) + row_of(ub_ref)[:, columns]
                phi = 0.5 + 0.5 * lax.erf(hidden * 0.7071067811865476)
                density = 0.3989422804014327 * jnp.exp(-0.5 * hidden * hidden)
                act = (hidden * phi).astype(bf16)
                active[t, rows, columns] = act
                slope[t, rows, columns] = (phi + hidden * density).astype(bf16)
                total = total + mul(act, wdown_ref[columns, :])
            state = total.astype(bf16)
            state_ref[t, 0, rows, :] = state
            xbuf[rows, :] = state.astype(f32) + emb_v[rows, :].astype(f32)
            return 0

        lax.fori_loop(0, count, feed, 0)
        return 0

    lax.fori_loop(0, 2, forward, 0)

    sums_ref[...] = jnp.zeros_like(sums_ref)
    gqkv_ref[...] = jnp.zeros_like(gqkv_ref)
    gout_ref[...] = jnp.zeros_like(gout_ref)
    gup_ref[...] = jnp.zeros_like(gup_ref)
    gdown_t[...] = jnp.zeros_like(gdown_t)
    dout[...] = cot_v[...]

    def add_sums(at, values):
        columns = slice(at, at + values.shape[1])
        sums_ref[:, columns] += eight_sums(values)

    def backward(step, _):
        t = 1 - step

        def feed_back(b, _):
            rows = rows_at(b)
            down = dout[rows, :]
            down_wide = down.astype(f32)
            add_sums(DB, down_wide)
            cotangent = jnp.zeros((BLOCK, width), f32)
            for c in range(wup_ref.shape[1] // 256):
                columns = slice(c * 256, c * 256 + 256)
                up = mul_rows(down, wdown_ref[columns, :]) * slope[t, rows, columns].astype(f32)
                up = up.astype(bf16)
                hgrad[rows, columns] = up
                add_sums(UB + c * 256, up.astype(f32))
                cotangent = cotangent + mul_rows(up, wup_ref[:, columns])
            hat = hat2[t, rows, :]
            add_sums(N2G, cotangent * hat)
            add_sums(N2B, cotangent)
            middle = down_wide + norm_back(cotangent, row_of(g2_ref), hat, scale2[t, rows, 0:1])
            mgrad[rows, :] = middle
            low = middle.astype(bf16)
            branch[rows, :] = low
            add_sums(OB, low.astype(f32))
            attended_grad = mul_rows(low, wout_ref[...]).astype(bf16)
            for pair in range(HEADS // 2):
                grad = attended_grad[:, pair * 128 : pair * 128 + 128].astype(f32)
                scaled = (grad * inverse[t, pair, rows, :]).astype(bf16)
                product = scaled.astype(f32) * outcome[t, pair, rows, :]
                gt[pair * 128 : pair * 128 + 128, rows] = scaled.T
                lane_of = lax.broadcasted_iota(jnp.int32, (BLOCK, 128), 1)
                for parity in range(2):
                    mine = low_half if parity == 0 else jnp.logical_not(low_half)
                    inner = -jnp.sum(jnp.where(mine, product, 0.0), axis=1, keepdims=True)
                    high = inner.astype(bf16).astype(f32)
                    rest = inner - high
                    spot = lane_of - (64 - parity * 64)
                    extra = jnp.where(spot == 0, high, jnp.where(spot == 1, rest, 0.0))
                    goa[2 * pair + parity, rows, :] = jnp.where(mine, scaled, extra.astype(bf16))
            return 0

        lax.fori_loop(0, count, feed_back, 0)

        gdown_t[...] += mul_columns(dout[...], active[t])
        gup_ref[...] += mul_columns(normed2[t], hgrad[...])
        for pair in range(HEADS // 2):
            gout_ref[pair * 128 : pair * 128 + 128, :] += mul_columns(
                outcome[t, pair].astype(bf16), branch[...]
            )

        for b, first, store in reversed(blocks_of(length)[0]):
            rows = slice(b * BLOCK, b * BLOCK + BLOCK)
            keys = slice(first * BLOCK, b * BLOCK + BLOCK)
            wide = (b + 1 - first) * BLOCK

            def attend_back(pair, _):
                parts = []
                for parity in range(2):
                    h = 2 * pair + parity
                    head_rows = pl.ds(pl.multiple_of(h * HEAD_DIM, HEAD_DIM), HEAD_DIM)
                    exps = expo[t, h, :, store : store + wide]
                    slopes = mul_rows(goa[h, rows, :], va[t, h, keys, :])
                    score_grad = (exps.astype(f32) * slopes).astype(bf16)
                    parts.append(mul(score_grad, ka[t, h, keys, :]))
                    key_part = mul(qt[t, head_rows, rows], score_grad)
                    value_part = mul(gt[head_rows, rows], exps)
                    for kb in range(first, b + 1):
                        mine = slice((kb - first) * BLOCK, (kb - first) * BLOCK + BLOCK)
                        there = slice(kb * BLOCK, kb * BLOCK + BLOCK)
                        if b == min(count - 1, kb + SPAN // BLOCK):
                            dkt[head_rows, there] = key_part[:, mine]
                            dvt[head_rows, there] = value_part[:, mine]
                        else:
                            dkt[head_rows, there] += key_part[:, mine]
                            dvt[head_rows, there] += value_part[:, mine]
                dq[pair] = jnp.where(low_half, parts[0], parts[1])
                return 0

            lax.fori_loop(0, HEADS // 2, attend_back, 0)
            for pair in range(HEADS // 2):
                pgrad[rows, pair * 128 : pair * 128 + 128] = (dq[pair] * HEAD_DIM**-0.5).astype(bf16)
            pgrad[rows, width : 2 * width] = dkt[:, rows].T.astype(bf16)
            pgrad[rows, 2 * width :] = dvt[:, rows].T.astype(bf16)
            part_grad = pgrad[rows, :]
            add_sums(QB, part_grad[:, :width].astype(f32))
            add_sums(VB, part_grad[:, 2 * width :].astype(f32))
            cotangent = mul_rows(part_grad, wqkv_ref[...])
            hat = hat1[t, rows, :]
            add_sums(N1G, cotangent * hat)
            add_sums(N1B, cotangent)
            x_grad = mgrad[rows, :] + norm_back(cotangent, row_of(g1_ref), hat, scale1[t, rows, 0:1])
            grad_ref[t, 0, rows, :] = x_grad
            dout[rows, :] = x_grad.astype(bf16)

        gqkv_ref[...] += mul_columns(normed1[t], pgrad[...])
        return 0

    lax.fori_loop(0, 2, backward, 0)
    gdown_ref[...] = gdown_t[...].T


def local_part(args):
    start = args[0]
    _, length, width = start.shape
    hidden = args[15].shape[0]
    vmem = pl.BlockSpec(memory_space=pltpu.VMEM)
    smem = pl.BlockSpec(memory_space=pltpu.SMEM)
    hbm = pl.BlockSpec(memory_space=pl.ANY)
    count = length // BLOCK
    pairs = HEADS // 2

    def V(*shape, dtype=bf16):
        return pltpu.VMEM(shape, dtype)

    return pl.pallas_call(
        compute_kernel,
        name="block_both_ways",
        in_specs=[hbm, hbm, hbm, vmem, smem] + [vmem] * 13,
        out_specs=[vmem] * 7,
        out_shape=[
            jax.ShapeDtypeStruct((2, 1, length, width), bf16),
            jax.ShapeDtypeStruct((2, 1, length, width), f32),
            jax.ShapeDtypeStruct((width, 3 * width), f32),
            jax.ShapeDtypeStruct((width, width), f32),
            jax.ShapeDtypeStruct((width, hidden), f32),
            jax.ShapeDtypeStruct((hidden, width), f32),
            jax.ShapeDtypeStruct((8, SUMS), f32),
        ],
        scratch_shapes=[
            V(length, width),
            V(length, width),
            V(length, width),
            V(length, 128),
            V(length, 128),
            V(length, width, dtype=f32),
            V(2, length, width, dtype=f32),
            V(2, length, 128, dtype=f32),
            V(2, length, width),
            V(HEADS, length, 128),
            V(2, width, length),
            V(2, HEADS, length, 128),
            V(2, HEADS, length, 128),
            V(2, HEADS, BLOCK, blocks_of(length)[1]),
            V(2, pairs, length, 128, dtype=f32),
            V(2, pairs, length, 128, dtype=f32),
            V(2, length, width, dtype=f32),
            V(2, length, 128, dtype=f32),
            V(2, length, width),
            V(2, length, hidden),
            V(2, length, hidden),
            V(length, hidden),
            V(length, width),
            V(length, width, dtype=f32),
            V(length, width),
            V(HEADS, length, 128),
            V(width, length),
            V(pairs, BLOCK, 128, dtype=f32),
            V(width, length, dtype=f32),
            V(width, length, dtype=f32),
            V(length, 3 * width),
            V(width, hidden, dtype=f32),
            pltpu.SemaphoreType.DMA((3,)),
        ],
        compiler_params=pltpu.CompilerParams(vmem_limit_bytes=60 << 20),
    )(*args)


def body(*args):
    states, grads, gqkv, gout, gup, gdown, sums = local_part(args)
    sums = jnp.sum(sums, axis=0)

    def piece(at, size=256):
        return sums[at : at + size]

    totals = (
        piece(N1G), piece(N1B), gqkv, piece(QB), piece(VB), gout, piece(OB), piece(N2G), piece(N2B),
        gup, piece(UB, 1024), gdown, piece(DB),
    )
    embed = grads[0] + grads[1]
    loop_states = lax.all_to_all(states, "section", split_axis=0, concat_axis=1, tiled=True)
    state_grads = lax.all_to_all(
        grads.astype(bf16), "section", split_axis=0, concat_axis=1, tiled=True
    ).astype(f32)
    embed_grad = lax.all_to_all(
        embed.astype(bf16), "section", split_axis=1, concat_axis=0, tiled=True
    ).astype(f32)
    summed = lax.psum(totals, ("section", "dp"))
    return (loop_states, state_grads, embed_grad) + tuple(summed)


def solution(mesh):
    rows = P("dp", None, None)
    return jax.shard_map(
        body,
        mesh=mesh,
        in_specs=(rows, rows, rows, P("dp", None), P("dp")) + (P(),) * 13,
        out_specs=(
            P("section", "dp", None, None),
            P("section", "dp", None, None),
            P("dp", "section", None),
        )
        + (P(),) * 13,
        check_vma=False,
    )
```

```python
from functools import partial

import jax
import jax.numpy as jnp
from jax import lax
from jax.experimental import pallas as pl
from jax.experimental.pallas import tpu as pltpu
from jax.sharding import PartitionSpec as P

HEADS = 4
HEAD_DIM = 64
BLOCK = 256
SPAN = 512
norm_eps = 1e-05
masked_score = -1e30
bf16 = jnp.bfloat16
f32 = jnp.float32


def mul(left, right):
    return jnp.dot(left, right, preferred_element_type=f32)


def mul_rows(left, right):
    return lax.dot_general(left, right, (((1,), (1,)), ((), ())), preferred_element_type=f32)


def mul_columns(left, right):
    return lax.dot_general(left, right, (((0,), (0,)), ((), ())), preferred_element_type=f32)


def row_of(ref):
    return ref[...].reshape(1, ref.shape[0])


def eight_sums(values):
    rows, width = values.shape
    return jnp.sum(values.reshape(rows // 8, 8, width), axis=0)


def normalise(x):
    average = jnp.mean(x, axis=-1, keepdims=True)
    centred = x - average
    spread = jnp.mean(centred * centred, axis=-1, keepdims=True)
    scale = lax.rsqrt(spread + norm_eps)
    return centred * scale, scale


def norm_back(cotangent, gain, hat, scale):
    scaled = cotangent * gain
    first = jnp.mean(scaled, axis=-1, keepdims=True)
    second = jnp.mean(scaled * hat, axis=-1, keepdims=True)
    return scale * (scaled - first - hat * second)


def blocks_of(length):
    result, store = [], 0
    for b in range(length // BLOCK):
        first = max(0, b - SPAN // BLOCK)
        result.append((b, first, store))
        store += (b + 1 - first) * BLOCK
    return result, store


N1G, N1B, QB, VB, OB, N2G, N2B, DB, UB = (256 * i for i in range(9))
SUMS = 256 * 12
DOWN_AT, OUT_AT, BULK_ROWS = 2048, 4096, 4608
SUMS_AT, TAIL_ROWS = 1536, 1568
MESH = pl.DeviceIdType.MESH


def compute_kernel(
    far_count,
    start_hbm, emb_hbm, cot_hbm, seg_ref, pad_ref,
    g1_ref, b1_ref, wqkv_ref, qb_ref, vb_ref, wout_ref, ob_ref, g2_ref, b2_ref, wup_ref, ub_ref,
    wdown_ref, db_ref,
    states_hbm, grads_hbm, extra_hbm, bulk_hbm, tail_hbm,
    start_v, emb_v, qx, kx, xbuf, hat1, scales, normed1, qa, qt, ka, va, expo, inverse,
    outcome, hat2, normed2, active, slope, hgrad, branch, mgrad, grads, states, goa, gt,
    dq, dkt, dvt, pgrad, gqkv, gout, gup, gdown, sums,
    bulk, bulk_core, bulk_plane, bulk_far, bulk_all, tail, tail_core, tail_plane, tail_far, tail_all,
    in_sem, swap_send, swap_recv, sum_send, sum_recv,
):
    length, width = xbuf.shape
    count = length // BLOCK
    part = lax.axis_index("section")
    place = lax.axis_index("dp")
    core, middle_bit, far = place % 2, (place // 2) % 2, place // 4
    plane = 2 * part + middle_bit

    swap_peer = (1 - part, place)
    core_peer = (part, place + 1 - 2 * core)

    def plane_peer(step):
        there = (plane + step) % 4
        return (there // 2, 4 * far + 2 * (there % 2) + core)

    def far_peer(step):
        return (part, 4 * ((far + step) % far_count) + 2 * middle_bit + core)

    peers = [swap_peer, core_peer, plane_peer(1), plane_peer(3)]
    peers += [far_peer(step) for step in range(1, far_count)]
    barrier = pltpu.get_barrier_semaphore()
    for peer in peers:
        pl.semaphore_signal(barrier, inc=1, device_id=peer, device_id_type=MESH)

    def remote(src, dst, sems, at, peer):
        return pltpu.make_async_remote_copy(
            src_ref=src, dst_ref=dst, send_sem=sems[0].at[at], recv_sem=sems[1].at[at],
            device_id=peer, device_id_type=MESH,
        )

    class Sum:
        def __init__(self, first_sem, own, by_core, by_plane, by_far, result):
            self.own, self.by_core, self.by_plane, self.by_far = own, by_core, by_plane, by_far
            self.result, self.first_sem = result, first_sem
            self.half = own.shape[0] // 2
            self.quarter = self.half // 4
            self.piece = self.quarter // far_count
            self.core_at = core * self.half
            self.plane_at = self.core_at + plane * self.quarter
            self.far_at = self.plane_at + far * self.piece

        def rows(self, at, size):
            return pl.ds(pl.multiple_of(at, 16), size)

        def copy(self, at, src, dst, peer):
            return remote(src, dst, (sum_send, sum_recv), self.first_sem + at, peer)

        def core_out(self):
            rows = self.rows((1 - core) * self.half, self.half)
            return [self.copy(0, self.own.at[rows], self.by_core, core_peer)]

        def plane_out(self):
            copies = []
            for step in range(1, 4):
                there = (plane + step) % 4
                rows = self.rows(self.core_at + there * self.quarter, self.quarter)
                copies.append(
                    self.copy(step, self.own.at[rows], self.by_plane.at[step - 1], plane_peer(step))
                )
            return copies

        def far_out(self):
            copies = []
            for step in range(1, far_count):
                there = (far + step) % far_count
                rows = self.rows(self.plane_at + there * self.piece, self.piece)
                copies.append(
                    self.copy(3 + step, self.own.at[rows], self.by_far.at[step - 1], far_peer(step))
                )
            return copies

        def far_back(self):
            rows = self.rows(self.far_at, self.piece)
            return [
                self.copy(2 + far_count + step, self.result.at[rows], self.result.at[rows], far_peer(step))
                for step in range(1, far_count)
            ]

        def plane_back(self):
            rows = self.rows(self.plane_at, self.quarter)
            return [
                self.copy(1 + 2 * far_count + step, self.result.at[rows], self.result.at[rows], plane_peer(step))
                for step in range(1, 4)
            ]

        def core_back(self):
            rows = self.rows(self.core_at, self.half)
            return [self.copy(5 + 2 * far_count, self.result.at[rows], self.result.at[rows], core_peer)]

        def add_core(self):
            step_rows = self.quarter

            def add(i, _):
                rows = self.rows(self.core_at + i * step_rows, step_rows)
                theirs = self.rows(i * step_rows, step_rows)
                self.own[rows, :] = (self.own[rows, :].astype(f32) + self.by_core[theirs, :].astype(f32)).astype(bf16)
                return 0

            lax.fori_loop(0, 4, add, 0)

        def add_plane(self):
            rows = self.rows(self.plane_at, self.quarter)
            total = self.own[rows, :].astype(f32)
            for step in range(3):
                total = total + self.by_plane[step].astype(f32)
            self.own[rows, :] = total.astype(bf16)

        def add_far(self):
            rows = self.rows(self.far_at, self.piece)
            total = self.own[rows, :].astype(f32)
            for step in range(far_count - 1):
                total = total + self.by_far[step].astype(f32)
            self.result[rows, :] = total.astype(bf16)

    def start(copies):
        for copy in copies:
            copy.start()

    def finish(copies):
        for copy in copies:
            copy.wait()

    sum_bulk = Sum(0, bulk, bulk_core, bulk_plane, bulk_far, bulk_all)
    sum_tail = Sum(6 + 2 * far_count, tail, tail_core, tail_plane, tail_far, tail_all)

    def state_copy():
        return remote(states.at[1 - part], states_hbm.at[part], (swap_send, swap_recv), 0, swap_peer)

    def main_copy(t, b):
        rows = slice(b * BLOCK, b * BLOCK + BLOCK)
        return remote(grads.at[t, rows], grads_hbm.at[part, rows], (swap_send, swap_recv), 1 + b, swap_peer)

    def extra_copy(t, b):
        rows = slice(b * BLOCK, b * BLOCK + BLOCK)
        there = b % (count // 2)
        half_rows = slice(there * BLOCK, there * BLOCK + BLOCK)
        return remote(
            grads.at[t, rows], extra_hbm.at[part, half_rows], (swap_send, swap_recv), 1 + count + there, swap_peer
        )

    loads = [
        pltpu.make_async_copy(hbm.at[part], dest, in_sem.at[i])
        for i, (hbm, dest) in enumerate(((start_hbm, start_v), (emb_hbm, emb_v), (cot_hbm, grads.at[2])))
    ]
    for load in loads:
        load.start()

    lane = lax.broadcasted_iota(jnp.int32, (128, 128), 1) & 63
    for c in range(length // 128):
        tokens = slice(c * 128, c * 128 + 128)
        ids = jnp.where(part == 0, seg_ref[0:1, tokens], seg_ref[1:2, tokens]).astype(f32)
        ids = jnp.broadcast_to(ids, (128, 128)).T.astype(jnp.int32)
        same = ids == lane
        qx[tokens, :] = jnp.where((lane < 8) & jnp.logical_not(same), masked_score, 0.0).astype(bf16)
        kx[tokens, :] = jnp.where(same, 1.0, 0.0).astype(bf16)

    for load in loads:
        load.wait()
    xbuf[...] = start_v[...].astype(f32) + emb_v[...].astype(f32)

    low_half = lax.broadcasted_iota(jnp.int32, (BLOCK, 128), 1) < 64
    row_at = lax.broadcasted_iota(jnp.int32, (BLOCK, BLOCK), 0)
    col_at = lax.broadcasted_iota(jnp.int32, (BLOCK, BLOCK), 1)
    ones = jnp.ones((BLOCK, 128), bf16)

    def rows_at(b):
        return pl.ds(pl.multiple_of(b * BLOCK, BLOCK), BLOCK)

    def forward(t, _):
        def project(b, _):
            rows = rows_at(b)
            hat, scale = normalise(xbuf[rows, :])
            normed = (hat * row_of(g1_ref) + row_of(b1_ref)).astype(bf16)
            hat1[t, rows, :] = hat
            scales[t, rows, 0:1] = scale
            normed1[t, rows, :] = normed
            q = (mul(normed, wqkv_ref[:, :width]) + row_of(qb_ref)).astype(bf16)
            q = q * jnp.asarray(HEAD_DIM**-0.5, bf16)
            k = mul(normed, wqkv_ref[:, width : 2 * width]).astype(bf16)
            v = (mul(normed, wqkv_ref[:, 2 * width :]) + row_of(vb_ref)).astype(bf16)
            qt[t, :, rows] = q.T
            for pair in range(HEADS // 2):
                lanes = slice(pair * 128, pair * 128 + 128)
                for h, mine in ((2 * pair, low_half), (2 * pair + 1, jnp.logical_not(low_half))):
                    qa[h, rows, :] = jnp.where(mine, q[:, lanes], qx[rows, :])
                    ka[t, h, rows, :] = jnp.where(mine, k[:, lanes], kx[rows, :])
                    va[t, h, rows, :] = jnp.where(mine, v[:, lanes], ones)
            return 0

        lax.fori_loop(0, count, project, 0)

        def attend(pair, _):
            for b, first, store in blocks_of(length)[0]:
                rows = slice(b * BLOCK, b * BLOCK + BLOCK)
                keys = slice(first * BLOCK, b * BLOCK + BLOCK)
                wide = (b + 1 - first) * BLOCK
                live = col_at + b * BLOCK < length - pad_ref[part]
                diagonal = (row_at == col_at) | ((row_at > col_at) & live)
                results = []
                for parity in range(2):
                    h = 2 * pair + parity
                    scores = mul_rows(qa[h, rows, :], ka[t, h, keys, :])
                    last = jnp.where(diagonal, scores[:, wide - BLOCK :], masked_score)
                    if wide > BLOCK:
                        scores = jnp.concatenate([scores[:, : wide - BLOCK], last], axis=1)
                    else:
                        scores = last
                    peak = jnp.max(scores, axis=1, keepdims=True)
                    exps = jnp.exp(scores - peak).astype(bf16)
                    expo[t, h, :, store : store + wide] = exps
                    results.append(mul(exps, va[t, h, keys, :]))
                top = jnp.where(low_half, results[0], results[1])
                total = pltpu.roll(jnp.where(low_half, results[1], results[0]), 64, 1)
                inv = 1.0 / total
                inverse[t, pair, rows, :] = inv
                outcome[t, pair, rows, :] = top * inv
            return 0

        lax.fori_loop(0, HEADS // 2, attend, 0)

        def feed(b, _):
            rows = rows_at(b)
            middle = xbuf[rows, :] + row_of(ob_ref)
            for pair in range(HEADS // 2):
                middle = middle + mul(outcome[t, pair, rows, :].astype(bf16), wout_ref[pair * 128 : pair * 128 + 128, :])
            hat, scale = normalise(middle)
            normed = (hat * row_of(g2_ref) + row_of(b2_ref)).astype(bf16)
            hat2[t, rows, :] = hat
            scales[t, rows, 1:2] = scale
            normed2[t, rows, :] = normed
            total = middle + row_of(db_ref)
            for c in range(wup_ref.shape[1] // 256):
                columns = slice(c * 256, c * 256 + 256)
                hidden = mul(normed, wup_ref[:, columns]) + row_of(ub_ref)[:, columns]
                phi = 0.5 + 0.5 * lax.erf(hidden * 0.7071067811865476)
                density = 0.3989422804014327 * jnp.exp(-0.5 * hidden * hidden)
                act = (hidden * phi).astype(bf16)
                active[t, rows, columns] = act
                slope[t, rows, columns] = (phi + hidden * density).astype(bf16)
                total = total + mul(act, wdown_ref[columns, :])
            state = total.astype(bf16)
            states[t, rows, :] = state
            xbuf[rows, :] = state.astype(f32) + emb_v[rows, :].astype(f32)
            return 0

        lax.fori_loop(0, count, feed, 0)
        return 0

    lax.fori_loop(0, 2, forward, 0)

    for total in (sums, gqkv, gout, gup, gdown):
        total[...] = jnp.zeros_like(total)
    pl.semaphore_wait(barrier, len(peers))
    state_copy().start()
    keep_state = pltpu.make_async_copy(states.at[part], states_hbm.at[part], in_sem.at[0])
    keep_state.start()

    def add_sums(at, values):
        columns = slice(at, at + values.shape[1])
        sums[:, columns] += eight_sums(values)

    def backward(step, _):
        t = 1 - step

        def feed_back(b, _):
            rows = rows_at(b)
            down = grads[t + 1, rows, :]
            down_wide = down.astype(f32)
            add_sums(DB, down_wide)
            cotangent = jnp.zeros((BLOCK, width), f32)
            for c in range(wup_ref.shape[1] // 256):
                columns = slice(c * 256, c * 256 + 256)
                up = mul_rows(down, wdown_ref[columns, :]) * slope[t, rows, columns].astype(f32)
                up = up.astype(bf16)
                hgrad[rows, columns] = up
                add_sums(UB + c * 256, up.astype(f32))
                cotangent = cotangent + mul_rows(up, wup_ref[:, columns])
            hat = hat2[t, rows, :]
            add_sums(N2G, cotangent * hat)
            add_sums(N2B, cotangent)
            middle = down_wide + norm_back(cotangent, row_of(g2_ref), hat, scales[t, rows, 1:2])
            mgrad[rows, :] = middle
            low = middle.astype(bf16)
            branch[rows, :] = low
            add_sums(OB, low.astype(f32))
            attended_grad = mul_rows(low, wout_ref[...]).astype(bf16)
            for pair in range(HEADS // 2):
                grad = attended_grad[:, pair * 128 : pair * 128 + 128].astype(f32)
                scaled = (grad * inverse[t, pair, rows, :]).astype(bf16)
                product = scaled.astype(f32) * outcome[t, pair, rows, :]
                gt[pair * 128 : pair * 128 + 128, rows] = scaled.T
                lane_of = lax.broadcasted_iota(jnp.int32, (BLOCK, 128), 1)
                for parity in range(2):
                    mine = low_half if parity == 0 else jnp.logical_not(low_half)
                    inner = -jnp.sum(jnp.where(mine, product, 0.0), axis=1, keepdims=True)
                    high = inner.astype(bf16).astype(f32)
                    rest = inner - high
                    spot = lane_of - (64 - parity * 64)
                    extra = jnp.where(spot == 0, high, jnp.where(spot == 1, rest, 0.0))
                    goa[2 * pair + parity, rows, :] = jnp.where(mine, scaled, extra.astype(bf16))
            return 0

        lax.fori_loop(0, count, feed_back, 0)

        gdown[...] += mul_columns(grads[t + 1], active[t])
        gup[...] += mul_columns(normed2[t], hgrad[...])
        for pair in range(HEADS // 2):
            gout[pair * 128 : pair * 128 + 128, :] += mul_columns(
                outcome[t, pair].astype(bf16), branch[...]
            )

        @pl.when(t == 0)
        def _():
            for i in range(wup_ref.shape[1] // 128):
                lanes = slice(i * 128, i * 128 + 128)
                bulk[i * width : (i + 1) * width, :] = gup[:, lanes].astype(bf16)
                at = DOWN_AT + i * width
                bulk[at : at + width, :] = gdown[:, lanes].astype(bf16)
            for i in range(width // 128):
                at = OUT_AT + i * width
                bulk[at : at + width, :] = gout[:, i * 128 : i * 128 + 128].astype(bf16)
            if bulk.shape[0] > BULK_ROWS:
                bulk[BULK_ROWS:, :] = jnp.zeros((bulk.shape[0] - BULK_ROWS, 128), bf16)
            start(sum_bulk.core_out())

        for b, first, store in reversed(blocks_of(length)[0]):
            rows = slice(b * BLOCK, b * BLOCK + BLOCK)
            keys = slice(first * BLOCK, b * BLOCK + BLOCK)
            wide = (b + 1 - first) * BLOCK

            def attend_back(pair, _):
                parts = []
                for parity in range(2):
                    h = 2 * pair + parity
                    head_rows = pl.ds(pl.multiple_of(h * HEAD_DIM, HEAD_DIM), HEAD_DIM)
                    exps = expo[t, h, :, store : store + wide]
                    slopes = mul_rows(goa[h, rows, :], va[t, h, keys, :])
                    score_grad = (exps.astype(f32) * slopes).astype(bf16)
                    parts.append(mul(score_grad, ka[t, h, keys, :]))
                    key_part = mul(qt[t, head_rows, rows], score_grad)
                    value_part = mul(gt[head_rows, rows], exps)
                    for kb in range(first, b + 1):
                        mine = slice((kb - first) * BLOCK, (kb - first) * BLOCK + BLOCK)
                        there = slice(kb * BLOCK, kb * BLOCK + BLOCK)
                        if b == min(count - 1, kb + SPAN // BLOCK):
                            dkt[head_rows, there] = key_part[:, mine]
                            dvt[head_rows, there] = value_part[:, mine]
                        else:
                            dkt[head_rows, there] += key_part[:, mine]
                            dvt[head_rows, there] += value_part[:, mine]
                dq[pair] = jnp.where(low_half, parts[0], parts[1])
                return 0

            lax.fori_loop(0, HEADS // 2, attend_back, 0)
            for pair in range(HEADS // 2):
                pgrad[rows, pair * 128 : pair * 128 + 128] = (dq[pair] * HEAD_DIM**-0.5).astype(bf16)
            pgrad[rows, width : 2 * width] = dkt[:, rows].T.astype(bf16)
            pgrad[rows, 2 * width :] = dvt[:, rows].T.astype(bf16)
            part_grad = pgrad[rows, :]
            add_sums(QB, part_grad[:, :width].astype(f32))
            add_sums(VB, part_grad[:, 2 * width :].astype(f32))
            cotangent = mul_rows(part_grad, wqkv_ref[...])
            hat = hat1[t, rows, :]
            add_sums(N1G, cotangent * hat)
            add_sums(N1B, cotangent)
            x_grad = mgrad[rows, :] + norm_back(cotangent, row_of(g1_ref), hat, scales[t, rows, 0:1])
            grads[t, rows, :] = x_grad.astype(bf16)

            @pl.when(part == 1 - t)
            def _():
                main_copy(t, b).start()

            @pl.when((part == t) & (t == 1 - b // (count // 2)))
            def _():
                extra_copy(t, b).start()

            if b == count - 1:
                @pl.when(t == 0)
                def _():
                    finish(sum_bulk.core_out())
                    sum_bulk.add_core()
                    start(sum_bulk.plane_out())
            if b == 0:
                @pl.when(t == 0)
                def _():
                    finish(sum_bulk.plane_out())
                    sum_bulk.add_plane()
                    start(sum_bulk.far_out())

        gqkv[...] += mul_columns(normed1[t], pgrad[...])
        return 0

    lax.fori_loop(0, 2, backward, 0)

    for i in range(3 * width // 128):
        tail[i * width : (i + 1) * width, :] = gqkv[:, i * 128 : i * 128 + 128].astype(bf16)
    total = jnp.sum(sums[...], axis=0, keepdims=True)
    parts = [total[:, i * 128 : i * 128 + 128] for i in range(SUMS // 128)]
    parts.append(jnp.zeros((8, 128), f32))
    tail[SUMS_AT : SUMS_AT + 32, :] = jnp.concatenate(parts, axis=0).astype(bf16)
    tail[SUMS_AT + 32 :, :] = jnp.zeros((tail.shape[0] - SUMS_AT - 32, 128), bf16)
    start(sum_tail.core_out())
    half_rows = pl.ds(pl.multiple_of(part * (length // 2), BLOCK), length // 2)
    keep_grad = pltpu.make_async_copy(grads.at[part], grads_hbm.at[part], in_sem.at[1])
    keep_extra = pltpu.make_async_copy(grads.at[1 - part, half_rows], extra_hbm.at[part], in_sem.at[2])
    keep_grad.start()
    keep_extra.start()
    finish(sum_bulk.far_out())
    sum_bulk.add_far()
    start(sum_bulk.far_back())
    finish(sum_tail.core_out())
    sum_tail.add_core()
    start(sum_tail.plane_out())
    finish(sum_bulk.far_back())
    start(sum_bulk.plane_back())
    finish(sum_tail.plane_out())
    sum_tail.add_plane()
    start(sum_tail.far_out())
    finish(sum_tail.far_out())
    sum_tail.add_far()
    start(sum_tail.far_back())
    finish(sum_bulk.plane_back())
    start(sum_bulk.core_back())
    finish(sum_tail.far_back())
    start(sum_tail.plane_back())
    finish(sum_bulk.core_back())
    keep_bulk = pltpu.make_async_copy(bulk_all, bulk_hbm, in_sem.at[3])
    keep_bulk.start()
    finish(sum_tail.plane_back())
    start(sum_tail.core_back())
    finish(sum_tail.core_back())
    keep_tail = pltpu.make_async_copy(tail_all, tail_hbm, in_sem.at[4])
    keep_tail.start()

    state_copy().wait()
    for b in range(count):
        main_copy(0, b).wait()
    for b in range(count // 2):
        extra_copy(0, b).wait()
    for keep in (keep_state, keep_grad, keep_extra, keep_bulk, keep_tail):
        keep.wait()


def padded(rows, devices):
    unit = 16 * devices
    return (rows + unit - 1) // unit * unit


def finish_kernel(
    states_hbm, grads_hbm, extra_hbm, bulk_hbm, tail_hbm,
    loop_out, grad_out, embed_out, n1g, n1b, gqkv, qb, vb, gout, ob, n2g, n2b, gup, ub, gdown, db,
    grads, extra, bulk, tail, grad_v, embed_v, gqkv_v, gout_v, gup_v, gdown_v, sems,
):
    part = lax.axis_index("section")
    length, width = grads.shape[1:]

    def copy(at, src, dst):
        return pltpu.make_async_copy(src, dst, sems.at[at])

    passed = copy(0, states_hbm, loop_out.at[0])
    loads = [copy(1, grads_hbm, grads), copy(2, extra_hbm, extra), copy(3, bulk_hbm, bulk), copy(4, tail_hbm, tail)]
    passed.start()
    for load in loads:
        load.start()
    loads[0].wait()
    grad_v[...] = grads[...].astype(f32)
    stores = [copy(5, grad_v, grad_out.at[0])]
    stores[-1].start()
    loads[1].wait()
    half_rows = pl.ds(pl.multiple_of(part * (length // 2), BLOCK), length // 2)
    embed_v[...] = grads[:, half_rows, :].astype(f32) + extra[...].astype(f32)
    stores.append(copy(6, embed_v, embed_out))
    stores[-1].start()
    loads[2].wait()
    for i in range(gup_v.shape[1] // 128):
        lanes = slice(i * 128, i * 128 + 128)
        gup_v[:, lanes] = bulk[i * width : (i + 1) * width, :].astype(f32)
    stores.append(copy(7, gup_v, gup))
    stores[-1].start()
    for i in range(gup_v.shape[1] // 128):
        at = DOWN_AT + i * width
        gdown_v[i * 128 : i * 128 + 128, :] = bulk[at : at + width, :].T.astype(f32)
    stores.append(copy(8, gdown_v, gdown))
    stores[-1].start()
    for i in range(width // 128):
        at = OUT_AT + i * width
        gout_v[:, i * 128 : i * 128 + 128] = bulk[at : at + width, :].astype(f32)
    stores.append(copy(9, gout_v, gout))
    stores[-1].start()
    loads[3].wait()
    for i in range(3 * width // 128):
        gqkv_v[:, i * 128 : i * 128 + 128] = tail[i * width : (i + 1) * width, :].astype(f32)
    stores.append(copy(10, gqkv_v, gqkv))
    stores[-1].start()
    small = tail[SUMS_AT : SUMS_AT + 32, :].astype(f32)
    for at, ref in ((N1G, n1g), (N1B, n1b), (QB, qb), (VB, vb), (OB, ob), (N2G, n2g), (N2B, n2b), (DB, db), (UB, ub)):
        for i in range(ref.shape[0] // 128):
            ref[i * 128 : i * 128 + 128] = small[at // 128 + i]
    passed.wait()
    for store in stores:
        store.wait()


def whole_block(sections, places, *args):
    start = args[0]
    _, length, width = start.shape
    hidden = args[15].shape[0]
    vmem = pl.BlockSpec(memory_space=pltpu.VMEM)
    smem = pl.BlockSpec(memory_space=pltpu.SMEM)
    hbm = pl.BlockSpec(memory_space=pl.ANY)
    count = length // BLOCK
    pairs = HEADS // 2
    devices = sections * places
    far_count = places // 4
    bulk_rows, tail_rows = padded(BULK_ROWS, devices), padded(TAIL_ROWS, devices)

    def V(*shape, dtype=bf16):
        return pltpu.VMEM(shape, dtype)

    def O(*shape, dtype=f32):
        return jax.ShapeDtypeStruct(shape, dtype)

    def sum_buffers(rows):
        return [
            V(rows, 128),
            V(rows // 2, 128),
            V(3, rows // 8, 128),
            V(far_count - 1, rows // devices, 128),
            V(rows, 128),
        ]

    copies = 2 * (6 + 2 * far_count)
    between = pl.pallas_call(
        partial(compute_kernel, far_count),
        name="block_both_ways",
        in_specs=[hbm, hbm, hbm, vmem, smem] + [vmem] * 13,
        out_specs=[hbm] * 5,
        out_shape=[
            O(2, length, width, dtype=bf16),
            O(2, length, width, dtype=bf16),
            O(2, length // 2, width, dtype=bf16),
            O(bulk_rows, 128, dtype=bf16),
            O(tail_rows, 128, dtype=bf16),
        ],
        scratch_shapes=[
            V(length, width),
            V(length, width),
            V(length, 128),
            V(length, 128),
            V(length, width, dtype=f32),
            V(2, length, width, dtype=f32),
            V(2, length, 128, dtype=f32),
            V(2, length, width),
            V(HEADS, length, 128),
            V(2, width, length),
            V(2, HEADS, length, 128),
            V(2, HEADS, length, 128),
            V(2, HEADS, BLOCK, blocks_of(length)[1]),
            V(2, pairs, length, 128, dtype=f32),
            V(2, pairs, length, 128, dtype=f32),
            V(2, length, width, dtype=f32),
            V(2, length, width),
            V(2, length, hidden),
            V(2, length, hidden),
            V(length, hidden),
            V(length, width),
            V(length, width, dtype=f32),
            V(3, length, width),
            V(2, length, width),
            V(HEADS, length, 128),
            V(width, length),
            V(pairs, BLOCK, 128, dtype=f32),
            V(width, length, dtype=f32),
            V(width, length, dtype=f32),
            V(length, 3 * width),
            V(width, 3 * width, dtype=f32),
            V(width, width, dtype=f32),
            V(width, hidden, dtype=f32),
            V(width, hidden, dtype=f32),
            V(8, SUMS, dtype=f32),
        ]
        + sum_buffers(bulk_rows)
        + sum_buffers(tail_rows)
        + [
            pltpu.SemaphoreType.DMA((5,)),
            pltpu.SemaphoreType.DMA((1 + count + count // 2,)),
            pltpu.SemaphoreType.DMA((1 + count + count // 2,)),
            pltpu.SemaphoreType.DMA((copies,)),
            pltpu.SemaphoreType.DMA((copies,)),
        ],
        compiler_params=pltpu.CompilerParams(
            vmem_limit_bytes=63 << 20, collective_id=0, has_side_effects=True
        ),
    )(*args)
    return pl.pallas_call(
        finish_kernel,
        name="widen",
        in_specs=[hbm] * 5,
        out_specs=[hbm, hbm, hbm, vmem, vmem, hbm, vmem, vmem, hbm, vmem, vmem, vmem, hbm, vmem, hbm, vmem],
        out_shape=[
            O(1, 2, length, width, dtype=bf16),
            O(1, 2, length, width),
            O(2, length // 2, width),
            O(width), O(width), O(width, 3 * width), O(width), O(width), O(width, width), O(width),
            O(width), O(width), O(width, hidden), O(hidden), O(hidden, width), O(width),
        ],
        scratch_shapes=[
            V(2, length, width),
            V(2, length // 2, width),
            V(bulk_rows, 128),
            V(tail_rows, 128),
            V(2, length, width, dtype=f32),
            V(2, length // 2, width, dtype=f32),
            V(width, 3 * width, dtype=f32),
            V(width, width, dtype=f32),
            V(width, hidden, dtype=f32),
            V(hidden, width, dtype=f32),
            pltpu.SemaphoreType.DMA((11,)),
        ],
        compiler_params=pltpu.CompilerParams(vmem_limit_bytes=32 << 20),
    )(*between)


def solution(mesh):
    rows = P("dp", None, None)
    return jax.shard_map(
        partial(whole_block, mesh.shape["section"], mesh.shape["dp"]),
        mesh=mesh,
        in_specs=(rows, rows, rows, P("dp", None), P("dp")) + (P(),) * 13,
        out_specs=(
            P("section", "dp", None, None),
            P("section", "dp", None, None),
            P("dp", "section", None),
        )
        + (P(),) * 13,
        check_vma=False,
    )
```

```python
from functools import partial

import jax
import jax.numpy as jnp
from jax import lax
from jax.experimental import pallas as pl
from jax.experimental.pallas import tpu as pltpu
from jax.sharding import PartitionSpec as P

HEADS = 4
HEAD_DIM = 64
BLOCK = 256
SPAN = 512
norm_eps = 1e-05
masked_score = -1e30
bf16 = jnp.bfloat16
f32 = jnp.float32


def mul(left, right):
    return jnp.dot(left, right, preferred_element_type=f32)


def mul_rows(left, right):
    return lax.dot_general(left, right, (((1,), (1,)), ((), ())), preferred_element_type=f32)


def mul_columns(left, right):
    return lax.dot_general(left, right, (((0,), (0,)), ((), ())), preferred_element_type=f32)


def row_of(ref):
    return ref[...].reshape(1, ref.shape[0])


def eight_sums(values):
    rows, width = values.shape
    return jnp.sum(values.reshape(rows // 8, 8, width), axis=0)


def normalise(x):
    average = jnp.mean(x, axis=-1, keepdims=True)
    centred = x - average
    spread = jnp.mean(centred * centred, axis=-1, keepdims=True)
    scale = lax.rsqrt(spread + norm_eps)
    return centred * scale, scale


def norm_back(cotangent, gain, hat, scale):
    scaled = cotangent * gain
    first = jnp.mean(scaled, axis=-1, keepdims=True)
    second = jnp.mean(scaled * hat, axis=-1, keepdims=True)
    return scale * (scaled - first - hat * second)


def blocks_of(length):
    result, store = [], 0
    for b in range(length // BLOCK):
        first = max(0, b - SPAN // BLOCK)
        result.append((b, first, store))
        store += (b + 1 - first) * BLOCK
    return result, store


def reach(half, distance, wide):
    low = 128 if half == 1 and distance == SPAN // BLOCK else 0
    return low, wide - (128 if half == 0 else 0)


N1G, N1B, QB, VB, OB, N2G, N2B, DB, UB = (256 * i for i in range(9))
SUMS = 256 * 12
DOWN_ROWS, OUT_AT, UP_ROWS, QKV_ROWS = 2048, 2048, 2560, 1536
MESH = pl.DeviceIdType.MESH


def compute_kernel(
    far_count,
    start_hbm, emb_hbm, cot_hbm, seg_ref, pad_ref,
    g1_ref, b1_ref, wqkv_ref, qb_ref, vb_ref, wout_ref, ob_ref, g2_ref, b2_ref, wup_ref, ub_ref,
    wdown_ref, db_ref,
    states_hbm, grads_hbm, extra_hbm, down_hbm, up_hbm, qkv_hbm, small_hbm,
    start_v, emb_v, kx, wq_t, qb_t, edge, score_a, score_b, slope_a, slope_b,
    xbuf, hat1, scales, normed1, qa, ka, kt, va, vt, expo, inverse,
    outcome, hat2, normed2, active, slope, hgrad, branch, mgrad, grads, states, goa,
    dkt, dvt, pgrad, gqkv, gout, gup, gdown, sums, qv_sums,
    down, down_core, down_plane, down_far, down_all,
    up, up_core, up_plane, up_far, up_all,
    qkv, qkv_core, qkv_chip, qkv_all,
    small, small_there, in_sem, swap_send, swap_recv, sum_send, sum_recv,
):
    length, width = xbuf.shape
    count = length // BLOCK
    part = lax.axis_index("section")
    place = lax.axis_index("dp")
    core, near, far = place % 2, (place // 2) % 2, place // 4

    across_peer = (1 - part, place)
    core_peer = (part, place + 1 - 2 * core)
    near_peer = (part, place + 2 - 4 * near)

    plane = 2 * part + near

    def plane_peer(step):
        there = (plane + step) % 4
        return (there // 2, 4 * far + 2 * (there % 2) + core)

    def far_peer(step):
        return (part, 4 * ((far + step) % far_count) + 2 * near + core)

    chips = lax.axis_size("section") * lax.axis_size("dp") // 2
    chip = part * (chips // 2) + place // 2

    def chip_peer(step):
        there = (chip + step) % chips
        return (there // (chips // 2), 2 * (there % (chips // 2)) + core)

    peers = [core_peer] + [chip_peer(step) for step in range(1, chips)]
    barrier = pltpu.get_barrier_semaphore()
    for peer in peers:
        pl.semaphore_signal(barrier, inc=1, device_id=peer, device_id_type=MESH)

    def remote(src, dst, sems, at, peer):
        return pltpu.make_async_remote_copy(
            src_ref=src, dst_ref=dst, send_sem=sems[0].at[at], recv_sem=sems[1].at[at],
            device_id=peer, device_id_type=MESH,
        )

    class Sum:
        def __init__(self, first_sem, own, by_core, by_plane, by_far, result, result_hbm):
            self.first_sem, self.own, self.result = first_sem, own, result
            self.by_core, self.by_plane, self.by_far = by_core, by_plane, by_far
            half = own.shape[0] // 2
            quarter = half // 4
            piece = quarter // far_count
            core_at = core * half
            plane_at = core_at + plane * quarter
            self.sizes = (half, quarter, piece)
            self.starts = (core_at, plane_at, plane_at + far * piece)
            self.keep = pltpu.make_async_copy(result, result_hbm, in_sem.at[4 + (first_sem > 0)])
            self.stage = 0

        def rows(self, at, size):
            return pl.ds(pl.multiple_of(at, 16), size)

        def copy(self, at, src, dst, peer):
            return remote(src, dst, (sum_send, sum_recv), self.first_sem + at, peer)

        def out(self, level):
            if level == 0:
                rows = self.rows((1 - core) * self.sizes[0], self.sizes[0])
                return [self.copy(0, self.own.at[rows], self.by_core, core_peer)]
            copies = []
            size = self.sizes[level]
            if level == 1:
                for step in range(1, 4):
                    rows = self.rows(self.starts[0] + (plane + step) % 4 * size, size)
                    copies.append(self.copy(step, self.own.at[rows], self.by_plane.at[step - 1], plane_peer(step)))
            else:
                for step in range(1, far_count):
                    rows = self.rows(self.starts[1] + (far + step) % far_count * size, size)
                    copies.append(self.copy(3 + step, self.own.at[rows], self.by_far.at[step - 1], far_peer(step)))
            return copies

        def back(self, level):
            src = self.result.at[self.rows(self.starts[level], self.sizes[level])]
            first = 2 + far_count
            if level == 2:
                return [self.copy(first + step, src, src, far_peer(step)) for step in range(1, far_count)]
            if level == 1:
                return [self.copy(first + far_count - 1 + step, src, src, plane_peer(step)) for step in range(1, 4)]
            return [self.copy(first + far_count + 3, src, src, core_peer)]

        def add(self, level):
            rows = self.rows(self.starts[level], self.sizes[level])
            total = self.own[rows, :].astype(f32)
            if level == 0:
                total = total + self.by_core[...].astype(f32)
            else:
                others = self.by_plane if level == 1 else self.by_far
                for step in range(others.shape[0]):
                    total = total + others[step].astype(f32)
            target = self.result if level == 2 else self.own
            target[rows, :] = total.astype(bf16)

        def step(self):
            stage = self.stage
            self.stage += 1
            if 1 <= stage <= 3:
                finish(self.out(stage - 1))
                self.add(stage - 1)
            if stage >= 4:
                finish(self.back(6 - stage))
            if stage <= 2:
                start(self.out(stage))
            elif stage <= 5:
                start(self.back(5 - stage))
            else:
                self.keep.start()

    class ShortSum:
        def __init__(self, first_sem, own, by_core, by_chip, result, result_hbm):
            self.first_sem, self.own, self.result = first_sem, own, result
            self.by_core, self.by_chip = by_core, by_chip
            self.half = own.shape[0] // 2
            self.piece = self.half // chips
            self.core_at = core * self.half
            self.chip_at = self.core_at + chip * self.piece
            self.keep = pltpu.make_async_copy(result, result_hbm, in_sem.at[6])
            self.stage = 0

        def rows(self, at, size):
            return pl.ds(pl.multiple_of(at, 16), size)

        def copy(self, at, src, dst, peer):
            return remote(src, dst, (sum_send, sum_recv), self.first_sem + at, peer)

        def core_out(self):
            rows = self.rows((1 - core) * self.half, self.half)
            return [self.copy(0, self.own.at[rows], self.by_core, core_peer)]

        def chip_out(self):
            copies = []
            for step in range(1, chips):
                rows = self.rows(self.core_at + (chip + step) % chips * self.piece, self.piece)
                copies.append(self.copy(step, self.own.at[rows], self.by_chip.at[step - 1], chip_peer(step)))
            return copies

        def chip_back(self):
            src = self.result.at[self.rows(self.chip_at, self.piece)]
            return [self.copy(chips - 1 + step, src, src, chip_peer(step)) for step in range(1, chips)]

        def core_back(self):
            src = self.result.at[self.rows(self.core_at, self.half)]
            return [self.copy(2 * chips - 1, src, src, core_peer)]

        def step(self):
            stage = self.stage
            self.stage += 1
            if stage == 0:
                start(self.core_out())
            elif stage == 1:
                finish(self.core_out())
                rows = self.rows(self.core_at, self.half)
                total = self.own[rows, :].astype(f32) + self.by_core[...].astype(f32)
                self.own[rows, :] = total.astype(bf16)
                start(self.chip_out())
            elif stage == 2:
                finish(self.chip_out())
                rows = self.rows(self.chip_at, self.piece)
                total = self.own[rows, :].astype(f32)
                for step in range(chips - 1):
                    total = total + self.by_chip[step].astype(f32)
                self.result[rows, :] = total.astype(bf16)
                start(self.chip_back())
            elif stage == 3:
                finish(self.chip_back())
                start(self.core_back())
            else:
                finish(self.core_back())
                self.keep.start()

    class Small:
        def __init__(self, first_sem):
            self.first_sem, self.stage = first_sem, 0
            self.keep = pltpu.make_async_copy(small, small_hbm, in_sem.at[3])

        def copies(self, level):
            first = (0, 1, 2, 1 + far_count)[level]
            peers = ([core_peer], [near_peer], [far_peer(step) for step in range(1, far_count)], [across_peer])[level]
            return [
                remote(small, small_there.at[first + i], (sum_send, sum_recv), self.first_sem + first + i, peer)
                for i, peer in enumerate(peers)
            ]

        def step(self):
            stage = self.stage
            self.stage += 1
            if stage > 0:
                copies = self.copies(stage - 1)
                finish(copies)
                first = (0, 1, 2, 1 + far_count)[stage - 1]
                total = small[...]
                for i in range(len(copies)):
                    total = total + small_there[first + i]
                small[...] = total
            if stage < 4:
                start(self.copies(stage))
            else:
                self.keep.start()

    def start(copies):
        for copy in copies:
            copy.start()

    def finish(copies):
        for copy in copies:
            copy.wait()

    sems = 6 + 2 * far_count
    sum_down = Sum(0, down, down_core, down_plane, down_far, down_all, down_hbm)
    sum_up = Sum(sems, up, up_core, up_plane, up_far, up_all, up_hbm)
    sum_qkv = ShortSum(2 * sems, qkv, qkv_core, qkv_chip, qkv_all, qkv_hbm)
    sum_small = Small(2 * sems + 2 * chips)

    def pack(target, at, source):
        height = source.shape[0]
        for i in range(source.shape[1] // 128):
            target[at + i * height : at + (i + 1) * height, :] = source[:, i * 128 : i * 128 + 128].astype(bf16)

    def clear(target, used):
        if target.shape[0] > used:
            target[used:, :] = jnp.zeros((target.shape[0] - used, 128), bf16)

    def state_copy():
        return remote(states.at[1 - part], states_hbm.at[part], (swap_send, swap_recv), 0, across_peer)

    def main_copy(t, b):
        rows = slice(b * BLOCK, b * BLOCK + BLOCK)
        return remote(grads.at[t, rows], grads_hbm.at[part, rows], (swap_send, swap_recv), 1 + b, across_peer)

    def extra_copy(t, b):
        rows = slice(b * BLOCK, b * BLOCK + BLOCK)
        there = b % (count // 2)
        half_rows = slice(there * BLOCK, there * BLOCK + BLOCK)
        return remote(
            grads.at[t, rows], extra_hbm.at[part, half_rows], (swap_send, swap_recv), 1 + count + there, across_peer
        )

    loads = [
        pltpu.make_async_copy(hbm.at[part], dest, in_sem.at[i])
        for i, (hbm, dest) in enumerate(((start_hbm, start_v), (emb_hbm, emb_v), (cot_hbm, grads.at[2])))
    ]
    for load in loads:
        load.start()

    lane = lax.broadcasted_iota(jnp.int32, (128, 128), 1) & 63
    ids = jnp.where(part == 0, seg_ref[0:1, :], seg_ref[1:2, :])
    for c in range(length // 128):
        tokens = slice(c * 128, c * 128 + 128)
        turned = jnp.broadcast_to(ids[:, tokens].astype(f32), (128, 128)).T.astype(jnp.int32)
        kx[tokens, :] = jnp.where(turned == lane, 1.0, 0.0).astype(bf16)
    code = lax.broadcasted_iota(jnp.int32, (16, length), 0)
    unlike = jnp.where((code < 8) & (code != ids), masked_score, 0.0).astype(bf16)
    for h in range(HEADS):
        spare = 64 - h % 2 * 64
        for t in range(2):
            qa[t, h, spare : spare + 64, :] = jnp.zeros((64, length), bf16)
            qa[t, h, spare : spare + 16, :] = unlike
        goa[h, spare : spare + 64, :] = jnp.zeros((64, length), bf16)
        vt[h, 64:80, :] = jnp.ones((16, length), bf16)
    key_at = lax.broadcasted_iota(jnp.int32, (128, 128), 0)
    query_at = lax.broadcasted_iota(jnp.int32, (128, 128), 1)
    edge[0] = jnp.where(key_at <= query_at, 0.0, masked_score)
    live = key_at + (length - 128) < length - pad_ref[part]
    edge[1] = jnp.where((key_at == query_at) | ((key_at < query_at) & live), 0.0, masked_score)
    wq_t[...] = wqkv_ref[:, :width].T
    qb_t[...] = jnp.broadcast_to(row_of(qb_ref), (128, width)).T

    for load in loads:
        load.wait()
    xbuf[...] = start_v[...].astype(f32) + emb_v[...].astype(f32)

    low_half = lax.broadcasted_iota(jnp.int32, (BLOCK, 128), 1) < 64
    ones = jnp.ones((BLOCK, 128), bf16)

    def rows_at(b):
        return pl.ds(pl.multiple_of(b * BLOCK, BLOCK), BLOCK)

    def forward(t, _):
        def project(b, _):
            rows = rows_at(b)
            hat, scale = normalise(xbuf[rows, :])
            normed = (hat * row_of(g1_ref) + row_of(b1_ref)).astype(bf16)
            hat1[t, rows, :] = hat
            scales[t, rows, 0:1] = scale
            normed1[t, rows, :] = normed
            bias = jnp.concatenate([qb_t[...], qb_t[...]], axis=1)
            q = (mul_rows(wq_t[...], normed) + bias).astype(bf16) * jnp.asarray(HEAD_DIM**-0.5, bf16)
            k = mul(normed, wqkv_ref[:, width : 2 * width]).astype(bf16)
            v = (mul(normed, wqkv_ref[:, 2 * width :]) + row_of(vb_ref)).astype(bf16)
            kt[t, :, rows] = k.T
            turned = v.T
            for h in range(HEADS):
                lanes = slice(h // 2 * 128, h // 2 * 128 + 128)
                own = h % 2 * 64
                head = slice(h * HEAD_DIM, h * HEAD_DIM + HEAD_DIM)
                mine = low_half if h % 2 == 0 else jnp.logical_not(low_half)
                qa[t, h, own : own + 64, rows] = q[head]
                ka[h, rows, :] = jnp.where(mine, k[:, lanes], kx[rows, :])
                va[t, h, rows, :] = jnp.where(mine, v[:, lanes], ones)
                vt[h, 0:64, rows] = turned[head]
            return 0

        lax.fori_loop(0, count, project, 0)

        def attend(pair, _):
            units = [(parity, *block) for block in blocks_of(length)[0] for parity in range(2)]
            buffers = (score_a, score_b)

            def score(i):
                parity, b, first, store = units[i]
                h, wide = 2 * pair + parity, (b + 1 - first) * BLOCK
                rows = slice(b * BLOCK, b * BLOCK + BLOCK)
                keys = slice(first * BLOCK, b * BLOCK + BLOCK)
                buffers[i % 2][0:wide, :] = mul(ka[h, keys, :], qa[t, h, :, rows])

            def weigh(i):
                parity, b, first, store = units[i]
                h, wide = 2 * pair + parity, (b + 1 - first) * BLOCK
                rows = slice(b * BLOCK, b * BLOCK + BLOCK)
                keys = slice(first * BLOCK, b * BLOCK + BLOCK)
                for half in range(2):
                    low, high = reach(half, b - first, wide)
                    lanes = slice(half * 128, half * 128 + 128)
                    last = edge[1 if b == count - 1 and half == 1 else 0]
                    scores = buffers[i % 2][low : high - 128, lanes]
                    border = buffers[i % 2][high - 128 : high, lanes] + last
                    peak = jnp.max(border, axis=0, keepdims=True)
                    if high - 128 > low:
                        peak = jnp.maximum(peak, jnp.max(scores, axis=0, keepdims=True))
                        expo[t, h, store + low : store + high - 128, lanes] = jnp.exp(scores - peak).astype(bf16)
                    expo[t, h, store + high - 128 : store + high, lanes] = jnp.exp(border - peak).astype(bf16)
                    if low > 0:
                        expo[t, h, store : store + low, lanes] = jnp.zeros((low, 128), bf16)
                    if high < wide:
                        expo[t, h, store + high : store + wide, lanes] = jnp.zeros((wide - high, 128), bf16)
                result = mul(vt[h, :, keys], expo[t, h, store : store + wide, :])
                inv = 1.0 / result[64:72]
                inverse[t, h, :, rows] = inv
                head_rows = pl.ds(pl.multiple_of(h * HEAD_DIM, HEAD_DIM), HEAD_DIM)
                outcome[t, head_rows, rows] = result[0:64] * inv[0:1]

            score(0)
            for i in range(len(units)):
                if i + 1 < len(units):
                    score(i + 1)
                weigh(i)
            return 0

        lax.fori_loop(0, HEADS // 2, attend, 0)

        def feed(b, _):
            rows = rows_at(b)
            turned = outcome[t, :, rows].astype(bf16).T
            middle = xbuf[rows, :] + row_of(ob_ref) + mul(turned, wout_ref[...])
            hat, scale = normalise(middle)
            normed = (hat * row_of(g2_ref) + row_of(b2_ref)).astype(bf16)
            hat2[t, rows, :] = hat
            scales[t, rows, 1:2] = scale
            normed2[t, rows, :] = normed
            total = middle + row_of(db_ref)
            for c in range(wup_ref.shape[1] // 256):
                columns = slice(c * 256, c * 256 + 256)
                hidden = mul(normed, wup_ref[:, columns]) + row_of(ub_ref)[:, columns]
                phi = 0.5 + 0.5 * lax.erf(hidden * 0.7071067811865476)
                density = 0.3989422804014327 * jnp.exp(-0.5 * hidden * hidden)
                act = (hidden * phi).astype(bf16)
                active[t, rows, columns] = act
                slope[t, rows, columns] = (phi + hidden * density).astype(bf16)
                total = total + mul(act, wdown_ref[columns, :])
            state = total.astype(bf16)
            states[t, rows, :] = state
            xbuf[rows, :] = state.astype(f32) + emb_v[rows, :].astype(f32)
            return 0

        lax.fori_loop(0, count, feed, 0)
        return 0

    lax.fori_loop(0, 2, forward, 0)

    for total in (sums, qv_sums, gqkv, gout, gup, gdown):
        total[...] = jnp.zeros_like(total)
    pl.semaphore_wait(barrier, len(peers))
    state_copy().start()
    keep_state = pltpu.make_async_copy(states.at[part], states_hbm.at[part], in_sem.at[0])
    keep_state.start()

    def add_sums(at, values):
        columns = slice(at, at + values.shape[1])
        sums[:, columns] += eight_sums(values)

    def backward(t):
        def feed_back(b, _):
            rows = rows_at(b)
            down = grads[t + 1, rows, :]
            down_wide = down.astype(f32)
            add_sums(DB, down_wide)
            cotangent = jnp.zeros((BLOCK, width), f32)
            for c in range(wup_ref.shape[1] // 256):
                columns = slice(c * 256, c * 256 + 256)
                up = mul_rows(down, wdown_ref[columns, :]) * slope[t, rows, columns].astype(f32)
                up = up.astype(bf16)
                hgrad[rows, columns] = up
                add_sums(UB + c * 256, up.astype(f32))
                cotangent = cotangent + mul_rows(up, wup_ref[:, columns])
            hat = hat2[t, rows, :]
            add_sums(N2G, cotangent * hat)
            add_sums(N2B, cotangent)
            middle = down_wide + norm_back(cotangent, row_of(g2_ref), hat, scales[t, rows, 1:2])
            mgrad[rows, :] = middle
            low = middle.astype(bf16)
            branch[rows, :] = low
            add_sums(OB, low.astype(f32))
            attended_grad = mul_rows(wout_ref[...], low).astype(bf16).astype(f32)
            line = lax.broadcasted_iota(jnp.int32, (16, BLOCK), 0)
            for h in range(HEADS):
                own = h % 2 * 64
                head = slice(h * HEAD_DIM, h * HEAD_DIM + HEAD_DIM)
                scaled = (attended_grad[head] * inverse[t, h, 0:1, rows]).astype(bf16)
                inner = -jnp.sum(scaled.astype(f32) * outcome[t, head, rows], axis=0, keepdims=True)
                high = inner.astype(bf16).astype(f32)
                extra = jnp.where(line == 0, high, jnp.where(line == 1, inner - high, 0.0))
                goa[h, own : own + 64, rows] = scaled
                goa[h, 64 - own : 80 - own, rows] = extra.astype(bf16)
            return 0

        lax.fori_loop(0, count, feed_back, 0)

        gdown[...] += mul_columns(grads[t + 1], active[t])

        if t == 0:
            pack(down, 0, gdown)
            clear(down, DOWN_ROWS)
            sum_down.step()

        gup[...] += mul_columns(normed2[t], hgrad[...])
        gout[...] += mul(outcome[t].astype(bf16), branch[...])

        if t == 0:
            pack(up, 0, gup)
            pack(up, OUT_AT, gout)
            clear(up, UP_ROWS)
            sum_up.step()

        def attend_back(b, first, store):
            rows = slice(b * BLOCK, b * BLOCK + BLOCK)
            keys = slice(first * BLOCK, b * BLOCK + BLOCK)
            wide = (b + 1 - first) * BLOCK
            buffers = (slope_a, slope_b)

            def slopes(h):
                values = mul(va[t, h, keys, :], goa[h, :, rows])
                values = expo[t, h, store : store + wide, :].astype(f32) * values
                buffers[h % 2][0:wide, :] = values.astype(bf16)

            def spread(h):
                head = slice(h * HEAD_DIM, h * HEAD_DIM + HEAD_DIM)
                own = slice(h % 2 * 64, h % 2 * 64 + 64)
                score_grad = buffers[h % 2][0:wide, :]
                query_part = mul(kt[t, head, keys], score_grad)
                pgrad[head, rows] = (query_part * HEAD_DIM**-0.5).astype(bf16)
                key_part = mul_rows(qa[t, h, own, rows], score_grad)
                value_part = mul_rows(goa[h, own, rows], expo[t, h, store : store + wide, :])
                for kb in range(first, b + 1):
                    mine = slice((kb - first) * BLOCK, (kb - first) * BLOCK + BLOCK)
                    there = slice(kb * BLOCK, kb * BLOCK + BLOCK)
                    if b == min(count - 1, kb + SPAN // BLOCK):
                        dkt[head, there] = key_part[:, mine]
                        dvt[head, there] = value_part[:, mine]
                    else:
                        dkt[head, there] += key_part[:, mine]
                        dvt[head, there] += value_part[:, mine]

            slopes(0)
            for h in range(HEADS):
                if h + 1 < HEADS:
                    slopes(h + 1)
                spread(h)

        def input_back(b):
            rows = slice(b * BLOCK, b * BLOCK + BLOCK)
            pgrad[width : 2 * width, rows] = dkt[:, rows].astype(bf16)
            pgrad[2 * width :, rows] = dvt[:, rows].astype(bf16)
            part_grad = pgrad[:, rows]
            for lanes in (slice(0, 128), slice(128, 256)):
                qv_sums[0:width, :] += part_grad[:width, lanes].astype(f32)
                qv_sums[width:, :] += part_grad[2 * width :, lanes].astype(f32)
            cotangent = mul(wqkv_ref[...], part_grad).T
            hat = hat1[t, rows, :]
            add_sums(N1G, cotangent * hat)
            add_sums(N1B, cotangent)
            x_grad = mgrad[rows, :] + norm_back(cotangent, row_of(g1_ref), hat, scales[t, rows, 0:1])
            grads[t, rows, :] = x_grad.astype(bf16)

        def send(now, blocks):
            @pl.when(part == 1 - now)
            def _():
                for b in blocks:
                    main_copy(now, b).start()

            extra = [b for b in blocks if b // (count // 2) == 1 - now]
            if extra:
                @pl.when(part == now)
                def _():
                    for b in extra:
                        extra_copy(now, b).start()

        for b, first, store in reversed(blocks_of(length)[0]):
            attend_back(b, first, store)
            if b + 1 < count:
                input_back(b + 1)
            if t == 0 and b == count - 1:
                sum_down.step()
                sum_up.step()
            if t == 0 and b == count // 2 - 1:
                send(0, range(count // 2, count))

        pgrad[width : 2 * width, 0:BLOCK] = dkt[:, 0:BLOCK].astype(bf16)
        pgrad[2 * width :, 0:BLOCK] = dvt[:, 0:BLOCK].astype(bf16)
        gqkv[...] += mul(pgrad[...], normed1[t])

        if t == 0:
            pack(qkv, 0, gqkv)
            clear(qkv, QKV_ROWS)
            sum_qkv.step()
        input_back(0)
        send(t, range(count // 2 if t == 0 else count))

    backward(1)
    backward(0)

    sums[0:1, QB : QB + width] = jnp.sum(qv_sums[0:width, :].T, axis=0, keepdims=True)
    sums[0:1, VB : VB + width] = jnp.sum(qv_sums[width:, :].T, axis=0, keepdims=True)
    total = jnp.sum(sums[...], axis=0, keepdims=True)
    small[...] = jnp.concatenate([total[:, i * 128 : i * 128 + 128] for i in range(SUMS // 128)], axis=0)
    sum_small.step()
    half_rows = pl.ds(pl.multiple_of(part * (length // 2), BLOCK), length // 2)
    keep_grad = pltpu.make_async_copy(grads.at[part], grads_hbm.at[part], in_sem.at[1])
    keep_extra = pltpu.make_async_copy(grads.at[1 - part, half_rows], extra_hbm.at[part], in_sem.at[2])
    keep_grad.start()
    keep_extra.start()
    for total in (
        sum_qkv, sum_down, sum_up, sum_small,
        sum_down, sum_up, sum_small,
        sum_qkv, sum_down, sum_up, sum_small,
        sum_qkv, sum_down, sum_up, sum_small, sum_qkv, sum_down, sum_up,
    ):
        total.step()

    state_copy().wait()
    for b in range(count):
        main_copy(0, b).wait()
    for b in range(count // 2):
        extra_copy(0, b).wait()
    for keep in (keep_state, keep_grad, keep_extra, sum_small.keep, sum_down.keep, sum_up.keep, sum_qkv.keep):
        keep.wait()


def padded(rows, devices):
    unit = 16 * devices
    return (rows + unit - 1) // unit * unit


def finish_kernel(
    states_hbm, grads_hbm, extra_hbm, down_hbm, up_hbm, qkv_hbm, small_hbm,
    loop_out, grad_out, embed_out, n1g, n1b, gqkv, qb, vb, gout, ob, n2g, n2b, gup, ub, gdown, db,
    states, grads, extra, down, up, qkv, small, grad_v, embed_v, gqkv_v, gout_v, gup_v, gdown_v, sems,
):
    part = lax.axis_index("section")
    length, width = grads.shape[1:]

    def copy(at, src, dst):
        return pltpu.make_async_copy(src, dst, sems.at[at])

    passed = copy(0, states_hbm, states)
    loads = [
        copy(1, grads_hbm, grads), copy(2, extra_hbm, extra), copy(3, up_hbm, up), copy(4, down_hbm, down),
        copy(12, qkv_hbm, qkv), copy(13, small_hbm, small),
    ]
    passed.start()
    for load in loads:
        load.start()
    passed.wait()
    stores = [copy(11, states, loop_out.at[0])]
    stores[-1].start()
    loads[0].wait()
    grad_v[...] = grads[...].astype(f32)
    stores.append(copy(5, grad_v, grad_out.at[0]))
    stores[-1].start()
    loads[1].wait()
    half_rows = pl.ds(pl.multiple_of(part * (length // 2), BLOCK), length // 2)
    embed_v[...] = grads[:, half_rows, :].astype(f32) + extra[...].astype(f32)
    stores.append(copy(6, embed_v, embed_out))
    stores[-1].start()
    loads[2].wait()
    for i in range(gup_v.shape[1] // 128):
        lanes = slice(i * 128, i * 128 + 128)
        gup_v[:, lanes] = up[i * width : (i + 1) * width, :].astype(f32)
    stores.append(copy(7, gup_v, gup))
    stores[-1].start()
    for i in range(width // 128):
        at = OUT_AT + i * width
        gout_v[:, i * 128 : i * 128 + 128] = up[at : at + width, :].astype(f32)
    stores.append(copy(9, gout_v, gout))
    stores[-1].start()
    loads[3].wait()
    for i in range(gup_v.shape[1] // 128):
        gdown_v[i * 128 : i * 128 + 128, :] = down[i * width : (i + 1) * width, :].T.astype(f32)
    stores.append(copy(8, gdown_v, gdown))
    stores[-1].start()
    loads[4].wait()
    for i in range(width // 128):
        turned = qkv[i * 3 * width : (i + 1) * 3 * width, :].T
        gqkv_v[i * 128 : i * 128 + 128, :] = turned.astype(f32)
    stores.append(copy(10, gqkv_v, gqkv))
    stores[-1].start()
    loads[5].wait()
    for at, ref in ((N1G, n1g), (N1B, n1b), (QB, qb), (VB, vb), (OB, ob), (N2G, n2g), (N2B, n2b), (DB, db), (UB, ub)):
        for i in range(ref.shape[0] // 128):
            ref[i * 128 : i * 128 + 128] = small[at // 128 + i]
    for store in stores:
        store.wait()


def whole_block(sections, places, *args):
    start = args[0]
    _, length, width = start.shape
    hidden = args[15].shape[0]
    vmem = pl.BlockSpec(memory_space=pltpu.VMEM)
    smem = pl.BlockSpec(memory_space=pltpu.SMEM)
    hbm = pl.BlockSpec(memory_space=pl.ANY)
    count = length // BLOCK
    devices = sections * places
    far_count = places // 4
    payloads = [padded(rows, devices) for rows in (DOWN_ROWS, UP_ROWS, QKV_ROWS)]

    def V(*shape, dtype=bf16):
        return pltpu.VMEM(shape, dtype)

    def O(*shape, dtype=f32):
        return jax.ShapeDtypeStruct(shape, dtype)

    def sum_buffers(rows):
        return [
            V(rows, 128),
            V(rows // 2, 128),
            V(3, rows // 8, 128),
            V(far_count - 1, rows // devices, 128),
            V(rows, 128),
        ]

    copies = 2 * (6 + 2 * far_count) + devices + 2 + far_count
    between = pl.pallas_call(
        partial(compute_kernel, far_count),
        name="block_both_ways",
        in_specs=[hbm, hbm, hbm, vmem, smem] + [vmem] * 13,
        out_specs=[hbm] * 7,
        out_shape=[
            O(2, length, width, dtype=bf16),
            O(2, length, width, dtype=bf16),
            O(2, length // 2, width, dtype=bf16),
            *(O(rows, 128, dtype=bf16) for rows in payloads),
            O(SUMS // 128, 128),
        ],
        scratch_shapes=[
            V(length, width),
            V(length, width),
            V(length, 128),
            V(width, width),
            V(width, 128, dtype=f32),
            V(2, 128, 128, dtype=f32),
            V(SPAN + BLOCK, BLOCK, dtype=f32),
            V(SPAN + BLOCK, BLOCK, dtype=f32),
            V(SPAN + BLOCK, BLOCK),
            V(SPAN + BLOCK, BLOCK),
            V(length, width, dtype=f32),
            V(2, length, width, dtype=f32),
            V(2, length, 128, dtype=f32),
            V(2, length, width),
            V(2, HEADS, 128, length),
            V(HEADS, length, 128),
            V(2, width, length),
            V(2, HEADS, length, 128),
            V(HEADS, 80, length),
            V(2, HEADS, blocks_of(length)[1], BLOCK),
            V(2, HEADS, 8, length, dtype=f32),
            V(2, width, length, dtype=f32),
            V(2, length, width, dtype=f32),
            V(2, length, width),
            V(2, length, hidden),
            V(2, length, hidden),
            V(length, hidden),
            V(length, width),
            V(length, width, dtype=f32),
            V(3, length, width),
            V(2, length, width),
            V(HEADS, 128, length),
            V(width, length, dtype=f32),
            V(width, length, dtype=f32),
            V(3 * width, length),
            V(3 * width, width, dtype=f32),
            V(width, width, dtype=f32),
            V(width, hidden, dtype=f32),
            V(width, hidden, dtype=f32),
            V(8, SUMS, dtype=f32),
            V(2 * width, 128, dtype=f32),
        ]
        + sum_buffers(payloads[0])
        + sum_buffers(payloads[1])
        + [
            V(payloads[2], 128),
            V(payloads[2] // 2, 128),
            V(devices // 2 - 1, payloads[2] // devices, 128),
            V(payloads[2], 128),
        ]
        + [
            V(SUMS // 128, 128, dtype=f32),
            V(2 + far_count, SUMS // 128, 128, dtype=f32),
            pltpu.SemaphoreType.DMA((7,)),
            pltpu.SemaphoreType.DMA((1 + count + count // 2,)),
            pltpu.SemaphoreType.DMA((1 + count + count // 2,)),
            pltpu.SemaphoreType.DMA((copies,)),
            pltpu.SemaphoreType.DMA((copies,)),
        ],
        compiler_params=pltpu.CompilerParams(
            vmem_limit_bytes=63 << 20, collective_id=0, has_side_effects=True
        ),
    )(*args)
    return pl.pallas_call(
        finish_kernel,
        name="widen",
        in_specs=[hbm] * 7,
        out_specs=[hbm, hbm, hbm, vmem, vmem, hbm, vmem, vmem, hbm, vmem, vmem, vmem, hbm, vmem, hbm, vmem],
        out_shape=[
            O(1, 2, length, width, dtype=bf16),
            O(1, 2, length, width),
            O(2, length // 2, width),
            O(width), O(width), O(width, 3 * width), O(width), O(width), O(width, width), O(width),
            O(width), O(width), O(width, hidden), O(hidden), O(hidden, width), O(width),
        ],
        scratch_shapes=[
            V(2, length, width),
            V(2, length, width),
            V(2, length // 2, width),
            V(payloads[0], 128),
            V(payloads[1], 128),
            V(payloads[2], 128),
            V(SUMS // 128, 128, dtype=f32),
            V(2, length, width, dtype=f32),
            V(2, length // 2, width, dtype=f32),
            V(width, 3 * width, dtype=f32),
            V(width, width, dtype=f32),
            V(width, hidden, dtype=f32),
            V(hidden, width, dtype=f32),
            pltpu.SemaphoreType.DMA((14,)),
        ],
        compiler_params=pltpu.CompilerParams(vmem_limit_bytes=63 << 20),
    )(*between)


def solution(mesh):
    rows = P("dp", None, None)
    return jax.shard_map(
        partial(whole_block, mesh.shape["section"], mesh.shape["dp"]),
        mesh=mesh,
        in_specs=(rows, rows, rows, P("dp", None), P("dp")) + (P(),) * 13,
        out_specs=(
            P("section", "dp", None, None),
            P("section", "dp", None, None),
            P("dp", "section", None),
        )
        + (P(),) * 13,
        check_vma=False,
    )
```

```python
from functools import partial

import jax
import jax.numpy as jnp
from jax import lax
from jax.experimental import pallas as pl
from jax.experimental.pallas import tpu as pltpu
from jax.sharding import PartitionSpec as P

HEADS = 4
HEAD_DIM = 64
BLOCK = 256
SPAN = 512
norm_eps = 1e-05
masked_score = -1e30
bf16 = jnp.bfloat16
f32 = jnp.float32


def mul(left, right):
    return jnp.dot(left, right, preferred_element_type=f32)


def mul_rows(left, right):
    return lax.dot_general(left, right, (((1,), (1,)), ((), ())), preferred_element_type=f32)


def mul_columns(left, right):
    return lax.dot_general(left, right, (((0,), (0,)), ((), ())), preferred_element_type=f32)


def row_of(ref):
    return ref[...].reshape(1, ref.shape[0])


def eight_sums(values):
    rows, width = values.shape
    return jnp.sum(values.reshape(rows // 8, 8, width), axis=0)


def normalise(x):
    average = jnp.mean(x, axis=-1, keepdims=True)
    centred = x - average
    spread = jnp.mean(centred * centred, axis=-1, keepdims=True)
    scale = lax.rsqrt(spread + norm_eps)
    return centred * scale, scale


def norm_back(cotangent, gain, hat, scale):
    scaled = cotangent * gain
    first = jnp.mean(scaled, axis=-1, keepdims=True)
    second = jnp.mean(scaled * hat, axis=-1, keepdims=True)
    return scale * (scaled - first - hat * second)


def blocks_of(length):
    result, store = [], 0
    for b in range(length // BLOCK):
        first = max(0, b - SPAN // BLOCK)
        result.append((b, first, store))
        store += (b + 1 - first) * BLOCK
    return result, store


def reach(half, distance, wide):
    low = 128 if half == 1 and distance == SPAN // BLOCK else 0
    return low, wide - (128 if half == 0 else 0)


N1G, N1B, QB, VB, OB, N2G, N2B, DB, UB = (256 * i for i in range(9))
SUMS = 256 * 12
DOWN_ROWS, OUT_AT, UP_ROWS, QKV_ROWS = 2048, 2048, 2560, 1536
MESH = pl.DeviceIdType.MESH


def compute_kernel(
    far_count,
    start_hbm, emb_hbm, cot_hbm, seg_ref, pad_ref,
    g1_ref, b1_ref, wqkv_ref, qb_ref, vb_ref, wout_ref, ob_ref, g2_ref, b2_ref, wup_ref, ub_ref,
    wdown_ref, db_ref,
    states_hbm, grads_hbm, extra_hbm, down_hbm, up_hbm, qkv_hbm, small_hbm,
    start_v, emb_v, kx, wq_t, qb_t, edge, score_a, score_b, score_c, score_d, slope_a, slope_b,
    xbuf, hat1, scales, normed1, qa, ka, kt, va, vt, expo, inverse,
    outcome, hat2, normed2, active, slope, hgrad, branch, mgrad, grads, states, goa,
    dkt, dvt, pgrad, gqkv, gout, gup, gdown, sums, qv_sums,
    down, down_core, down_plane, down_far, down_all,
    up, up_core, up_plane, up_far, up_all,
    qkv, qkv_core, qkv_chip, qkv_all,
    small, small_there, in_sem, swap_send, swap_recv, sum_send, sum_recv,
):
    length, width = xbuf.shape
    count = length // BLOCK
    part = lax.axis_index("section")
    place = lax.axis_index("dp")
    core, near, far = place % 2, (place // 2) % 2, place // 4

    across_peer = (1 - part, place)
    core_peer = (part, place + 1 - 2 * core)
    near_peer = (part, place + 2 - 4 * near)

    plane = 2 * part + near

    def plane_peer(step):
        there = (plane + step) % 4
        return (there // 2, 4 * far + 2 * (there % 2) + core)

    def far_peer(step):
        return (part, 4 * ((far + step) % far_count) + 2 * near + core)

    chips = lax.axis_size("section") * lax.axis_size("dp") // 2
    chip = part * (chips // 2) + place // 2

    def chip_peer(step):
        there = (chip + step) % chips
        return (there // (chips // 2), 2 * (there % (chips // 2)) + core)

    peers = [core_peer] + [chip_peer(step) for step in range(1, chips)]
    barrier = pltpu.get_barrier_semaphore()
    for peer in peers:
        pl.semaphore_signal(barrier, inc=1, device_id=peer, device_id_type=MESH)

    def remote(src, dst, sems, at, peer):
        return pltpu.make_async_remote_copy(
            src_ref=src, dst_ref=dst, send_sem=sems[0].at[at], recv_sem=sems[1].at[at],
            device_id=peer, device_id_type=MESH,
        )

    class Sum:
        def __init__(self, first_sem, own, by_core, by_plane, by_far, result, result_hbm):
            self.first_sem, self.own, self.result = first_sem, own, result
            self.by_core, self.by_plane, self.by_far = by_core, by_plane, by_far
            half = own.shape[0] // 2
            quarter = half // 4
            piece = quarter // far_count
            core_at = core * half
            plane_at = core_at + plane * quarter
            self.sizes = (half, quarter, piece)
            self.starts = (core_at, plane_at, plane_at + far * piece)
            self.keep = pltpu.make_async_copy(result, result_hbm, in_sem.at[4 + (first_sem > 0)])
            self.stage = 0

        def rows(self, at, size):
            return pl.ds(pl.multiple_of(at, 16), size)

        def copy(self, at, src, dst, peer):
            return remote(src, dst, (sum_send, sum_recv), self.first_sem + at, peer)

        def out(self, level):
            if level == 0:
                rows = self.rows((1 - core) * self.sizes[0], self.sizes[0])
                return [self.copy(0, self.own.at[rows], self.by_core, core_peer)]
            copies = []
            size = self.sizes[level]
            if level == 1:
                for step in range(1, 4):
                    rows = self.rows(self.starts[0] + (plane + step) % 4 * size, size)
                    copies.append(self.copy(step, self.own.at[rows], self.by_plane.at[step - 1], plane_peer(step)))
            else:
                for step in range(1, far_count):
                    rows = self.rows(self.starts[1] + (far + step) % far_count * size, size)
                    copies.append(self.copy(3 + step, self.own.at[rows], self.by_far.at[step - 1], far_peer(step)))
            return copies

        def back(self, level):
            src = self.result.at[self.rows(self.starts[level], self.sizes[level])]
            first = 2 + far_count
            if level == 2:
                return [self.copy(first + step, src, src, far_peer(step)) for step in range(1, far_count)]
            if level == 1:
                return [self.copy(first + far_count - 1 + step, src, src, plane_peer(step)) for step in range(1, 4)]
            return [self.copy(first + far_count + 3, src, src, core_peer)]

        def add(self, level):
            rows = self.rows(self.starts[level], self.sizes[level])
            total = self.own[rows, :].astype(f32)
            if level == 0:
                total = total + self.by_core[...].astype(f32)
            else:
                others = self.by_plane if level == 1 else self.by_far
                for step in range(others.shape[0]):
                    total = total + others[step].astype(f32)
            target = self.result if level == 2 else self.own
            target[rows, :] = total.astype(bf16)

        def step(self):
            stage = self.stage
            self.stage += 1
            if 1 <= stage <= 3:
                finish(self.out(stage - 1))
                self.add(stage - 1)
            if stage >= 4:
                finish(self.back(6 - stage))
            if stage <= 2:
                start(self.out(stage))
            elif stage <= 5:
                start(self.back(5 - stage))
            else:
                self.keep.start()

    class ShortSum:
        def __init__(self, first_sem, own, by_core, by_chip, result, result_hbm):
            self.first_sem, self.own, self.result = first_sem, own, result
            self.by_core, self.by_chip = by_core, by_chip
            self.half = own.shape[0] // 2
            self.piece = self.half // chips
            self.core_at = core * self.half
            self.chip_at = self.core_at + chip * self.piece
            self.keep = pltpu.make_async_copy(result, result_hbm, in_sem.at[6])
            self.stage = 0

        def rows(self, at, size):
            return pl.ds(pl.multiple_of(at, 16), size)

        def copy(self, at, src, dst, peer):
            return remote(src, dst, (sum_send, sum_recv), self.first_sem + at, peer)

        def core_out(self):
            rows = self.rows((1 - core) * self.half, self.half)
            return [self.copy(0, self.own.at[rows], self.by_core, core_peer)]

        def chip_out(self):
            copies = []
            for step in range(1, chips):
                rows = self.rows(self.core_at + (chip + step) % chips * self.piece, self.piece)
                copies.append(self.copy(step, self.own.at[rows], self.by_chip.at[step - 1], chip_peer(step)))
            return copies

        def chip_back(self):
            src = self.result.at[self.rows(self.chip_at, self.piece)]
            return [self.copy(chips - 1 + step, src, src, chip_peer(step)) for step in range(1, chips)]

        def core_back(self):
            src = self.result.at[self.rows(self.core_at, self.half)]
            return [self.copy(2 * chips - 1, src, src, core_peer)]

        def step(self):
            stage = self.stage
            self.stage += 1
            if stage == 0:
                start(self.core_out())
            elif stage == 1:
                finish(self.core_out())
                rows = self.rows(self.core_at, self.half)
                total = self.own[rows, :].astype(f32) + self.by_core[...].astype(f32)
                self.own[rows, :] = total.astype(bf16)
                start(self.chip_out())
            elif stage == 2:
                finish(self.chip_out())
                rows = self.rows(self.chip_at, self.piece)
                total = self.own[rows, :].astype(f32)
                for step in range(chips - 1):
                    total = total + self.by_chip[step].astype(f32)
                self.result[rows, :] = total.astype(bf16)
                start(self.chip_back())
            elif stage == 3:
                finish(self.chip_back())
                start(self.core_back())
            else:
                finish(self.core_back())
                self.keep.start()

    class Small:
        def __init__(self, first_sem):
            self.first_sem, self.stage = first_sem, 0
            self.keep = pltpu.make_async_copy(small, small_hbm, in_sem.at[3])

        def copies(self, level):
            first = (0, 1, 2, 1 + far_count)[level]
            peers = ([core_peer], [near_peer], [far_peer(step) for step in range(1, far_count)], [across_peer])[level]
            return [
                remote(small, small_there.at[first + i], (sum_send, sum_recv), self.first_sem + first + i, peer)
                for i, peer in enumerate(peers)
            ]

        def step(self):
            stage = self.stage
            self.stage += 1
            if stage > 0:
                copies = self.copies(stage - 1)
                finish(copies)
                first = (0, 1, 2, 1 + far_count)[stage - 1]
                total = small[...]
                for i in range(len(copies)):
                    total = total + small_there[first + i]
                small[...] = total
            if stage < 4:
                start(self.copies(stage))
            else:
                self.keep.start()

    def start(copies):
        for copy in copies:
            copy.start()

    def finish(copies):
        for copy in copies:
            copy.wait()

    sems = 6 + 2 * far_count
    sum_down = Sum(0, down, down_core, down_plane, down_far, down_all, down_hbm)
    sum_up = Sum(sems, up, up_core, up_plane, up_far, up_all, up_hbm)
    sum_qkv = ShortSum(2 * sems, qkv, qkv_core, qkv_chip, qkv_all, qkv_hbm)
    sum_small = Small(2 * sems + 2 * chips)

    def pack(target, at, source):
        height = source.shape[0]
        for i in range(source.shape[1] // 128):
            target[at + i * height : at + (i + 1) * height, :] = source[:, i * 128 : i * 128 + 128].astype(bf16)

    def clear(target, used):
        if target.shape[0] > used:
            target[used:, :] = jnp.zeros((target.shape[0] - used, 128), bf16)

    def state_copy():
        return remote(states.at[1 - part], states_hbm.at[part], (swap_send, swap_recv), 0, across_peer)

    def main_copy(t, b):
        rows = slice(b * BLOCK, b * BLOCK + BLOCK)
        return remote(grads.at[t, rows], grads_hbm.at[part, rows], (swap_send, swap_recv), 1 + b, across_peer)

    def extra_copy(t, b):
        rows = slice(b * BLOCK, b * BLOCK + BLOCK)
        there = b % (count // 2)
        half_rows = slice(there * BLOCK, there * BLOCK + BLOCK)
        return remote(
            grads.at[t, rows], extra_hbm.at[part, half_rows], (swap_send, swap_recv), 1 + count + there, across_peer
        )

    loads = [
        pltpu.make_async_copy(hbm.at[part], dest, in_sem.at[i])
        for i, (hbm, dest) in enumerate(((start_hbm, start_v), (emb_hbm, emb_v), (cot_hbm, grads.at[2])))
    ]
    for load in loads:
        load.start()

    lane = lax.broadcasted_iota(jnp.int32, (128, 128), 1) & 63
    ids = jnp.where(part == 0, seg_ref[0:1, :], seg_ref[1:2, :])
    for c in range(length // 128):
        tokens = slice(c * 128, c * 128 + 128)
        turned = jnp.broadcast_to(ids[:, tokens].astype(f32), (128, 128)).T.astype(jnp.int32)
        kx[tokens, :] = jnp.where(turned == lane, 1.0, 0.0).astype(bf16)
    code = lax.broadcasted_iota(jnp.int32, (16, length), 0)
    unlike = jnp.where((code < 8) & (code != ids), masked_score, 0.0).astype(bf16)
    for h in range(HEADS):
        spare = 64 - h % 2 * 64
        for t in range(2):
            qa[t, h, spare : spare + 64, :] = jnp.zeros((64, length), bf16)
            qa[t, h, spare : spare + 16, :] = unlike
        goa[h, spare : spare + 64, :] = jnp.zeros((64, length), bf16)
        vt[h, 64:80, :] = jnp.ones((16, length), bf16)
    key_at = lax.broadcasted_iota(jnp.int32, (128, 128), 0)
    query_at = lax.broadcasted_iota(jnp.int32, (128, 128), 1)
    edge[0] = jnp.where(key_at <= query_at, 0.0, masked_score)
    live = key_at + (length - 128) < length - pad_ref[part]
    edge[1] = jnp.where((key_at == query_at) | ((key_at < query_at) & live), 0.0, masked_score)
    wq_t[...] = wqkv_ref[:, :width].T
    qb_t[...] = jnp.broadcast_to(row_of(qb_ref), (128, width)).T

    for load in loads:
        load.wait()
    xbuf[...] = start_v[...].astype(f32) + emb_v[...].astype(f32)

    low_half = lax.broadcasted_iota(jnp.int32, (BLOCK, 128), 1) < 64
    ones = jnp.ones((BLOCK, 128), bf16)

    def rows_at(b):
        return pl.ds(pl.multiple_of(b * BLOCK, BLOCK), BLOCK)

    def forward(t, _):
        def project(b, _):
            rows = rows_at(b)
            hat, scale = normalise(xbuf[rows, :])
            normed = (hat * row_of(g1_ref) + row_of(b1_ref)).astype(bf16)
            hat1[t, rows, :] = hat
            scales[t, rows, 0:1] = scale
            normed1[t, rows, :] = normed
            bias = jnp.concatenate([qb_t[...], qb_t[...]], axis=1)
            q = (mul_rows(wq_t[...], normed) + bias).astype(bf16) * jnp.asarray(HEAD_DIM**-0.5, bf16)
            k = mul(normed, wqkv_ref[:, width : 2 * width]).astype(bf16)
            v = (mul(normed, wqkv_ref[:, 2 * width :]) + row_of(vb_ref)).astype(bf16)
            kt[t, :, rows] = k.T
            turned = v.T
            for h in range(HEADS):
                lanes = slice(h // 2 * 128, h // 2 * 128 + 128)
                own = h % 2 * 64
                head = slice(h * HEAD_DIM, h * HEAD_DIM + HEAD_DIM)
                mine = low_half if h % 2 == 0 else jnp.logical_not(low_half)
                qa[t, h, own : own + 64, rows] = q[head]
                ka[h, rows, :] = jnp.where(mine, k[:, lanes], kx[rows, :])
                va[t, h, rows, :] = jnp.where(mine, v[:, lanes], ones)
                vt[h, 0:64, rows] = turned[head]
            return 0

        lax.fori_loop(0, count, project, 0, unroll=4)

        def attend(pair, _):
            units = [(parity, *block) for block in blocks_of(length)[0] for parity in range(2)]
            buffers = (score_a, score_b, score_c, score_d)

            def score(i):
                parity, b, first, store = units[i]
                h, wide = 2 * pair + parity, (b + 1 - first) * BLOCK
                rows = slice(b * BLOCK, b * BLOCK + BLOCK)
                keys = slice(first * BLOCK, b * BLOCK + BLOCK)
                buffers[i % 4][0:wide, :] = mul(ka[h, keys, :], qa[t, h, :, rows])

            def weigh(i):
                parity, b, first, store = units[i]
                h, wide = 2 * pair + parity, (b + 1 - first) * BLOCK
                rows = slice(b * BLOCK, b * BLOCK + BLOCK)
                keys = slice(first * BLOCK, b * BLOCK + BLOCK)
                for half in range(2):
                    low, high = reach(half, b - first, wide)
                    lanes = slice(half * 128, half * 128 + 128)
                    last = edge[1 if b == count - 1 and half == 1 else 0]
                    scores = buffers[i % 4][low : high - 128, lanes]
                    border = buffers[i % 4][high - 128 : high, lanes] + last
                    peak = jnp.max(border, axis=0, keepdims=True)
                    if high - 128 > low:
                        peak = jnp.maximum(peak, jnp.max(scores, axis=0, keepdims=True))
                        expo[t, h, store + low : store + high - 128, lanes] = jnp.exp(scores - peak).astype(bf16)
                    expo[t, h, store + high - 128 : store + high, lanes] = jnp.exp(border - peak).astype(bf16)
                    if low > 0:
                        expo[t, h, store : store + low, lanes] = jnp.zeros((low, 128), bf16)
                    if high < wide:
                        expo[t, h, store + high : store + wide, lanes] = jnp.zeros((wide - high, 128), bf16)
                result = mul(vt[h, :, keys], expo[t, h, store : store + wide, :])
                inv = 1.0 / result[64:72]
                inverse[t, h, :, rows] = inv
                head_rows = pl.ds(pl.multiple_of(h * HEAD_DIM, HEAD_DIM), HEAD_DIM)
                outcome[t, head_rows, rows] = result[0:64] * inv[0:1]

            score(0)
            score(1)
            for i in range(0, len(units), 2):
                if i + 2 < len(units):
                    score(i + 2)
                    score(i + 3)
                weigh(i)
                weigh(i + 1)
            return 0

        lax.fori_loop(0, HEADS // 2, attend, 0, unroll=2)

        def feed(b, _):
            rows = rows_at(b)
            turned = outcome[t, :, rows].astype(bf16).T
            middle = xbuf[rows, :] + row_of(ob_ref) + mul(turned, wout_ref[...])
            hat, scale = normalise(middle)
            normed = (hat * row_of(g2_ref) + row_of(b2_ref)).astype(bf16)
            hat2[t, rows, :] = hat
            scales[t, rows, 1:2] = scale
            normed2[t, rows, :] = normed
            for c in range(wup_ref.shape[1] // 256):
                columns = slice(c * 256, c * 256 + 256)
                hidden = mul(normed, wup_ref[:, columns]) + row_of(ub_ref)[:, columns]
                inner = hidden * 0.7071067811865476
                phi = 0.5 * lax.erf(inner) + 0.5
                bell = jnp.exp2(inner * -1.4426950408889634 * inner)
                active[t, rows, columns] = (hidden * phi).astype(bf16)
                slope[t, rows, columns] = (phi + hidden * bell * 0.3989422804014327).astype(bf16)
            total = middle + row_of(db_ref) + mul(active[t, rows, :], wdown_ref[...])
            state = total.astype(bf16)
            states[t, rows, :] = state
            xbuf[rows, :] = state.astype(f32) + emb_v[rows, :].astype(f32)
            return 0

        lax.fori_loop(0, count, feed, 0, unroll=4)
        return 0

    lax.fori_loop(0, 2, forward, 0)

    for total in (sums, qv_sums, gqkv, gout, gup, gdown):
        total[...] = jnp.zeros_like(total)
    pl.semaphore_wait(barrier, len(peers))
    state_copy().start()
    keep_state = pltpu.make_async_copy(states.at[part], states_hbm.at[part], in_sem.at[0])
    keep_state.start()

    def add_sums(at, values):
        columns = slice(at, at + values.shape[1])
        sums[:, columns] += eight_sums(values)

    def backward(t):
        def feed_back(b, _):
            rows = rows_at(b)
            down = grads[t + 1, rows, :]
            down_wide = down.astype(f32)
            add_sums(DB, down_wide)
            for c in range(wup_ref.shape[1] // 256):
                columns = slice(c * 256, c * 256 + 256)
                up_grad = mul_rows(down, wdown_ref[columns, :]) * slope[t, rows, columns].astype(f32)
                up_grad = up_grad.astype(bf16)
                hgrad[rows, columns] = up_grad
                add_sums(UB + c * 256, up_grad.astype(f32))
            cotangent = mul_rows(hgrad[rows, :], wup_ref[...])
            hat = hat2[t, rows, :]
            add_sums(N2G, cotangent * hat)
            add_sums(N2B, cotangent)
            middle = down_wide + norm_back(cotangent, row_of(g2_ref), hat, scales[t, rows, 1:2])
            mgrad[rows, :] = middle
            low = middle.astype(bf16)
            branch[rows, :] = low
            add_sums(OB, low.astype(f32))
            attended_grad = mul_rows(wout_ref[...], low).astype(bf16).astype(f32)
            line = lax.broadcasted_iota(jnp.int32, (16, BLOCK), 0)
            for h in range(HEADS):
                own = h % 2 * 64
                head = slice(h * HEAD_DIM, h * HEAD_DIM + HEAD_DIM)
                scaled = (attended_grad[head] * inverse[t, h, 0:1, rows]).astype(bf16)
                inner = -jnp.sum(scaled.astype(f32) * outcome[t, head, rows], axis=0, keepdims=True)
                high = inner.astype(bf16).astype(f32)
                extra = jnp.where(line == 0, high, jnp.where(line == 1, inner - high, 0.0))
                goa[h, own : own + 64, rows] = scaled
                goa[h, 64 - own : 80 - own, rows] = extra.astype(bf16)
            return 0

        lax.fori_loop(0, count, feed_back, 0, unroll=4)

        gdown[...] += mul_columns(grads[t + 1], active[t])

        if t == 0:
            pack(down, 0, gdown)
            clear(down, DOWN_ROWS)
            sum_down.step()

        gup[...] += mul_columns(normed2[t], hgrad[...])
        gout[...] += mul(outcome[t].astype(bf16), branch[...])

        if t == 0:
            pack(up, 0, gup)
            pack(up, OUT_AT, gout)
            clear(up, UP_ROWS)
            sum_up.step()

        def attend_back(b, first, store):
            rows = slice(b * BLOCK, b * BLOCK + BLOCK)
            keys = slice(first * BLOCK, b * BLOCK + BLOCK)
            wide = (b + 1 - first) * BLOCK
            buffers = (slope_a, slope_b)

            def slopes(h):
                values = mul(va[t, h, keys, :], goa[h, :, rows])
                values = expo[t, h, store : store + wide, :].astype(f32) * values
                buffers[h % 2][0:wide, :] = values.astype(bf16)

            def spread(h):
                head = slice(h * HEAD_DIM, h * HEAD_DIM + HEAD_DIM)
                own = slice(h % 2 * 64, h % 2 * 64 + 64)
                score_grad = buffers[h % 2][0:wide, :]
                query_part = mul(kt[t, head, keys], score_grad)
                pgrad[head, rows] = (query_part * HEAD_DIM**-0.5).astype(bf16)
                key_part = mul_rows(qa[t, h, own, rows], score_grad)
                value_part = mul_rows(goa[h, own, rows], expo[t, h, store : store + wide, :])
                for kb in range(first, b + 1):
                    mine = slice((kb - first) * BLOCK, (kb - first) * BLOCK + BLOCK)
                    there = slice(kb * BLOCK, kb * BLOCK + BLOCK)
                    if b == min(count - 1, kb + SPAN // BLOCK):
                        dkt[head, there] = key_part[:, mine]
                        dvt[head, there] = value_part[:, mine]
                    else:
                        dkt[head, there] += key_part[:, mine]
                        dvt[head, there] += value_part[:, mine]

            slopes(0)
            for h in range(HEADS):
                if h + 1 < HEADS:
                    slopes(h + 1)
                spread(h)

        def input_back(b):
            rows = slice(b * BLOCK, b * BLOCK + BLOCK)
            pgrad[width : 2 * width, rows] = dkt[:, rows].astype(bf16)
            pgrad[2 * width :, rows] = dvt[:, rows].astype(bf16)
            part_grad = pgrad[:, rows]
            for lanes in (slice(0, 128), slice(128, 256)):
                qv_sums[0:width, :] += part_grad[:width, lanes].astype(f32)
                qv_sums[width:, :] += part_grad[2 * width :, lanes].astype(f32)
            cotangent = mul(wqkv_ref[...], part_grad).T
            hat = hat1[t, rows, :]
            add_sums(N1G, cotangent * hat)
            add_sums(N1B, cotangent)
            x_grad = mgrad[rows, :] + norm_back(cotangent, row_of(g1_ref), hat, scales[t, rows, 0:1])
            grads[t, rows, :] = x_grad.astype(bf16)

        def send(now, blocks):
            @pl.when(part == 1 - now)
            def _():
                for b in blocks:
                    main_copy(now, b).start()

            extra = [b for b in blocks if b // (count // 2) == 1 - now]
            if extra:
                @pl.when(part == now)
                def _():
                    for b in extra:
                        extra_copy(now, b).start()

        for b, first, store in reversed(blocks_of(length)[0]):
            attend_back(b, first, store)
            if b + 1 < count:
                input_back(b + 1)
            if t == 0 and b == count - 1:
                sum_down.step()
                sum_up.step()
            if t == 0 and b == count // 2 - 1:
                send(0, range(count // 2, count))

        pgrad[width : 2 * width, 0:BLOCK] = dkt[:, 0:BLOCK].astype(bf16)
        pgrad[2 * width :, 0:BLOCK] = dvt[:, 0:BLOCK].astype(bf16)
        gqkv[...] += mul(pgrad[...], normed1[t])

        if t == 0:
            pack(qkv, 0, gqkv)
            clear(qkv, QKV_ROWS)
            sum_qkv.step()
        input_back(0)
        send(t, range(count // 2 if t == 0 else count))

    backward(1)
    backward(0)

    sums[0:1, QB : QB + width] = jnp.sum(qv_sums[0:width, :].T, axis=0, keepdims=True)
    sums[0:1, VB : VB + width] = jnp.sum(qv_sums[width:, :].T, axis=0, keepdims=True)
    total = jnp.sum(sums[...], axis=0, keepdims=True)
    small[...] = jnp.concatenate([total[:, i * 128 : i * 128 + 128] for i in range(SUMS // 128)], axis=0)
    sum_small.step()
    half_rows = pl.ds(pl.multiple_of(part * (length // 2), BLOCK), length // 2)
    keep_grad = pltpu.make_async_copy(grads.at[part], grads_hbm.at[part], in_sem.at[1])
    keep_extra = pltpu.make_async_copy(grads.at[1 - part, half_rows], extra_hbm.at[part], in_sem.at[2])
    keep_grad.start()
    keep_extra.start()
    for total in (
        sum_qkv, sum_down, sum_up, sum_small,
        sum_down, sum_up, sum_small,
        sum_qkv, sum_down, sum_up, sum_small,
        sum_qkv, sum_down, sum_up, sum_small, sum_qkv, sum_down, sum_up,
    ):
        total.step()

    state_copy().wait()
    for b in range(count):
        main_copy(0, b).wait()
    for b in range(count // 2):
        extra_copy(0, b).wait()
    for keep in (keep_state, keep_grad, keep_extra, sum_small.keep, sum_down.keep, sum_up.keep, sum_qkv.keep):
        keep.wait()


def padded(rows, devices):
    unit = 16 * devices
    return (rows + unit - 1) // unit * unit


def finish_kernel(
    states_hbm, grads_hbm, extra_hbm, down_hbm, up_hbm, qkv_hbm, small_hbm,
    loop_out, grad_out, embed_out, n1g, n1b, gqkv, qb, vb, gout, ob, n2g, n2b, gup, ub, gdown, db,
    states, grads, extra, down, up, qkv, small, grad_v, embed_v, gqkv_v, gout_v, gup_v, gdown_v, sems,
):
    part = lax.axis_index("section")
    length, width = grads.shape[1:]

    def copy(at, src, dst):
        return pltpu.make_async_copy(src, dst, sems.at[at])

    passed = copy(0, states_hbm, states)
    loads = [
        copy(1, grads_hbm, grads), copy(2, extra_hbm, extra), copy(3, up_hbm, up), copy(4, down_hbm, down),
        copy(12, qkv_hbm, qkv), copy(13, small_hbm, small),
    ]
    passed.start()
    for load in loads:
        load.start()
    passed.wait()
    stores = [copy(11, states, loop_out.at[0])]
    stores[-1].start()
    loads[0].wait()
    grad_v[...] = grads[...].astype(f32)
    stores.append(copy(5, grad_v, grad_out.at[0]))
    stores[-1].start()
    loads[1].wait()
    half_rows = pl.ds(pl.multiple_of(part * (length // 2), BLOCK), length // 2)
    embed_v[...] = grads[:, half_rows, :].astype(f32) + extra[...].astype(f32)
    stores.append(copy(6, embed_v, embed_out))
    stores[-1].start()
    loads[2].wait()
    for i in range(gup_v.shape[1] // 128):
        lanes = slice(i * 128, i * 128 + 128)
        gup_v[:, lanes] = up[i * width : (i + 1) * width, :].astype(f32)
    stores.append(copy(7, gup_v, gup))
    stores[-1].start()
    for i in range(width // 128):
        at = OUT_AT + i * width
        gout_v[:, i * 128 : i * 128 + 128] = up[at : at + width, :].astype(f32)
    stores.append(copy(9, gout_v, gout))
    stores[-1].start()
    loads[3].wait()
    for i in range(gup_v.shape[1] // 128):
        gdown_v[i * 128 : i * 128 + 128, :] = down[i * width : (i + 1) * width, :].T.astype(f32)
    stores.append(copy(8, gdown_v, gdown))
    stores[-1].start()
    loads[4].wait()
    for i in range(width // 128):
        turned = qkv[i * 3 * width : (i + 1) * 3 * width, :].T
        gqkv_v[i * 128 : i * 128 + 128, :] = turned.astype(f32)
    stores.append(copy(10, gqkv_v, gqkv))
    stores[-1].start()
    loads[5].wait()
    for at, ref in ((N1G, n1g), (N1B, n1b), (QB, qb), (VB, vb), (OB, ob), (N2G, n2g), (N2B, n2b), (DB, db), (UB, ub)):
        for i in range(ref.shape[0] // 128):
            ref[i * 128 : i * 128 + 128] = small[at // 128 + i]
    for store in stores:
        store.wait()


def whole_block(sections, places, *args):
    start = args[0]
    _, length, width = start.shape
    hidden = args[15].shape[0]
    vmem = pl.BlockSpec(memory_space=pltpu.VMEM)
    smem = pl.BlockSpec(memory_space=pltpu.SMEM)
    hbm = pl.BlockSpec(memory_space=pl.ANY)
    count = length // BLOCK
    devices = sections * places
    far_count = places // 4
    payloads = [padded(rows, devices) for rows in (DOWN_ROWS, UP_ROWS, QKV_ROWS)]

    def V(*shape, dtype=bf16):
        return pltpu.VMEM(shape, dtype)

    def O(*shape, dtype=f32):
        return jax.ShapeDtypeStruct(shape, dtype)

    def sum_buffers(rows):
        return [
            V(rows, 128),
            V(rows // 2, 128),
            V(3, rows // 8, 128),
            V(far_count - 1, rows // devices, 128),
            V(rows, 128),
        ]

    copies = 2 * (6 + 2 * far_count) + devices + 2 + far_count
    between = pl.pallas_call(
        partial(compute_kernel, far_count),
        name="block_both_ways",
        in_specs=[hbm, hbm, hbm, vmem, smem] + [vmem] * 13,
        out_specs=[hbm] * 7,
        out_shape=[
            O(2, length, width, dtype=bf16),
            O(2, length, width, dtype=bf16),
            O(2, length // 2, width, dtype=bf16),
            *(O(rows, 128, dtype=bf16) for rows in payloads),
            O(SUMS // 128, 128),
        ],
        scratch_shapes=[
            V(length, width),
            V(length, width),
            V(length, 128),
            V(width, width),
            V(width, 128, dtype=f32),
            V(2, 128, 128, dtype=f32),
            V(SPAN + BLOCK, BLOCK, dtype=f32),
            V(SPAN + BLOCK, BLOCK, dtype=f32),
            V(SPAN + BLOCK, BLOCK, dtype=f32),
            V(SPAN + BLOCK, BLOCK, dtype=f32),
            V(SPAN + BLOCK, BLOCK),
            V(SPAN + BLOCK, BLOCK),
            V(length, width, dtype=f32),
            V(2, length, width, dtype=f32),
            V(2, length, 128, dtype=f32),
            V(2, length, width),
            V(2, HEADS, 128, length),
            V(HEADS, length, 128),
            V(2, width, length),
            V(2, HEADS, length, 128),
            V(HEADS, 80, length),
            V(2, HEADS, blocks_of(length)[1], BLOCK),
            V(2, HEADS, 8, length, dtype=f32),
            V(2, width, length, dtype=f32),
            V(2, length, width, dtype=f32),
            V(2, length, width),
            V(2, length, hidden),
            V(2, length, hidden),
            V(length, hidden),
            V(length, width),
            V(length, width, dtype=f32),
            V(3, length, width),
            V(2, length, width),
            V(HEADS, 128, length),
            V(width, length, dtype=f32),
            V(width, length, dtype=f32),
            V(3 * width, length),
            V(3 * width, width, dtype=f32),
            V(width, width, dtype=f32),
            V(width, hidden, dtype=f32),
            V(width, hidden, dtype=f32),
            V(8, SUMS, dtype=f32),
            V(2 * width, 128, dtype=f32),
        ]
        + sum_buffers(payloads[0])
        + sum_buffers(payloads[1])
        + [
            V(payloads[2], 128),
            V(payloads[2] // 2, 128),
            V(devices // 2 - 1, payloads[2] // devices, 128),
            V(payloads[2], 128),
        ]
        + [
            V(SUMS // 128, 128, dtype=f32),
            V(2 + far_count, SUMS // 128, 128, dtype=f32),
            pltpu.SemaphoreType.DMA((7,)),
            pltpu.SemaphoreType.DMA((1 + count + count // 2,)),
            pltpu.SemaphoreType.DMA((1 + count + count // 2,)),
            pltpu.SemaphoreType.DMA((copies,)),
            pltpu.SemaphoreType.DMA((copies,)),
        ],
        compiler_params=pltpu.CompilerParams(
            vmem_limit_bytes=63 << 20, collective_id=0, has_side_effects=True
        ),
    )(*args)
    return pl.pallas_call(
        finish_kernel,
        name="widen",
        in_specs=[hbm] * 7,
        out_specs=[hbm, hbm, hbm, vmem, vmem, hbm, vmem, vmem, hbm, vmem, vmem, vmem, hbm, vmem, hbm, vmem],
        out_shape=[
            O(1, 2, length, width, dtype=bf16),
            O(1, 2, length, width),
            O(2, length // 2, width),
            O(width), O(width), O(width, 3 * width), O(width), O(width), O(width, width), O(width),
            O(width), O(width), O(width, hidden), O(hidden), O(hidden, width), O(width),
        ],
        scratch_shapes=[
            V(2, length, width),
            V(2, length, width),
            V(2, length // 2, width),
            V(payloads[0], 128),
            V(payloads[1], 128),
            V(payloads[2], 128),
            V(SUMS // 128, 128, dtype=f32),
            V(2, length, width, dtype=f32),
            V(2, length // 2, width, dtype=f32),
            V(width, 3 * width, dtype=f32),
            V(width, width, dtype=f32),
            V(width, hidden, dtype=f32),
            V(hidden, width, dtype=f32),
            pltpu.SemaphoreType.DMA((14,)),
        ],
        compiler_params=pltpu.CompilerParams(vmem_limit_bytes=63 << 20),
    )(*between)


def solution(mesh):
    rows = P("dp", None, None)
    return jax.shard_map(
        partial(whole_block, mesh.shape["section"], mesh.shape["dp"]),
        mesh=mesh,
        in_specs=(rows, rows, rows, P("dp", None), P("dp")) + (P(),) * 13,
        out_specs=(
            P("section", "dp", None, None),
            P("section", "dp", None, None),
            P("dp", "section", None),
        )
        + (P(),) * 13,
        check_vma=False,
    )
```

```python
from functools import partial

import jax
import jax.numpy as jnp
from jax import lax
from jax.experimental import pallas as pl
from jax.experimental.pallas import tpu as pltpu
from jax.sharding import PartitionSpec as P

HEADS = 4
HEAD_DIM = 64
BLOCK = 256
SPAN = 512
norm_eps = 1e-05
masked_score = -1e30
bf16 = jnp.bfloat16
f32 = jnp.float32


def mul(left, right):
    return jnp.dot(left, right, preferred_element_type=f32)


def mul_rows(left, right):
    return lax.dot_general(left, right, (((1,), (1,)), ((), ())), preferred_element_type=f32)


def mul_columns(left, right):
    return lax.dot_general(left, right, (((0,), (0,)), ((), ())), preferred_element_type=f32)


def row_of(ref):
    return ref[...].reshape(1, ref.shape[0])


def eight_sums(values):
    rows, width = values.shape
    return jnp.sum(values.reshape(rows // 8, 8, width), axis=0)


def normalise(x):
    average = jnp.mean(x, axis=-1, keepdims=True)
    centred = x - average
    spread = jnp.mean(centred * centred, axis=-1, keepdims=True)
    scale = lax.rsqrt(spread + norm_eps)
    return centred * scale, scale


def norm_back(cotangent, gain, hat, scale):
    scaled = cotangent * gain
    first = jnp.mean(scaled, axis=-1, keepdims=True)
    second = jnp.mean(scaled * hat, axis=-1, keepdims=True)
    return scale * (scaled - first - hat * second)


def blocks_of(length):
    result, store = [], 0
    for b in range(length // BLOCK):
        first = max(0, b - SPAN // BLOCK)
        result.append((b, first, store))
        store += (b + 1 - first) * BLOCK
    return result, store


def reach(half, distance, wide):
    low = 128 if half == 1 and distance == SPAN // BLOCK else 0
    return low, wide - (128 if half == 0 else 0)


HOOKS = {"a3": "DU", "f2": "Q32", "f0": "10"}
N1G, N1B, QB, VB, OB, N2G, N2B, DB, UB = (256 * i for i in range(9))
SUMS = 256 * 12
DOWN_ROWS, OUT_AT, UP_ROWS, QKV_ROWS = 2048, 2048, 2560, 1536
MESH = pl.DeviceIdType.MESH


def compute_kernel(
    far_count,
    start_hbm, emb_hbm, cot_hbm, seg_ref, pad_ref,
    g1_ref, b1_ref, wqkv_ref, qb_ref, vb_ref, wout_ref, ob_ref, g2_ref, b2_ref, wup_ref, ub_ref,
    wdown_ref, db_ref,
    states_hbm, grads_hbm, extra_hbm, down_hbm, up_hbm, qkv_hbm, small_hbm,
    start_v, emb_v, kx, wq_t, qb_t, edge, score_a, score_b, score_c, score_d, slope_a, slope_b,
    xbuf, hat1, scales, normed1, qa, ka, kt, va, vt, expo, inverse,
    outcome, hat2, normed2, active, slope, hgrad, branch, mgrad, grads, states, goa,
    dkt, dvt, pgrad, gqkv, gout, gup, gdown, sums, qv_sums,
    down, down_core, down_plane, down_far, down_all,
    up, up_core, up_plane, up_far, up_all,
    qkv, qkv_core, qkv_chip, qkv_all,
    small, small_there, in_sem, swap_send, swap_recv, sum_send, sum_recv,
):
    length, width = xbuf.shape
    count = length // BLOCK
    part = lax.axis_index("section")
    place = lax.axis_index("dp")
    core, near, far = place % 2, (place // 2) % 2, place // 4

    across_peer = (1 - part, place)
    core_peer = (part, place + 1 - 2 * core)
    near_peer = (part, place + 2 - 4 * near)

    plane = 2 * part + near

    def plane_peer(step):
        there = (plane + step) % 4
        return (there // 2, 4 * far + 2 * (there % 2) + core)

    def far_peer(step):
        return (part, 4 * ((far + step) % far_count) + 2 * near + core)

    chips = lax.axis_size("section") * lax.axis_size("dp") // 2
    chip = part * (chips // 2) + place // 2

    def chip_peer(step):
        there = (chip + step) % chips
        return (there // (chips // 2), 2 * (there % (chips // 2)) + core)

    peers = [core_peer] + [chip_peer(step) for step in range(1, chips)]
    barrier = pltpu.get_barrier_semaphore()
    for peer in peers:
        pl.semaphore_signal(barrier, inc=1, device_id=peer, device_id_type=MESH)

    def remote(src, dst, sems, at, peer):
        return pltpu.make_async_remote_copy(
            src_ref=src, dst_ref=dst, send_sem=sems[0].at[at], recv_sem=sems[1].at[at],
            device_id=peer, device_id_type=MESH,
        )

    class Sum:
        def __init__(self, first_sem, own, by_core, by_plane, by_far, result, result_hbm):
            self.first_sem, self.own, self.result = first_sem, own, result
            self.by_core, self.by_plane, self.by_far = by_core, by_plane, by_far
            half = own.shape[0] // 2
            quarter = half // 4
            piece = quarter // far_count
            core_at = core * half
            plane_at = core_at + plane * quarter
            self.sizes = (half, quarter, piece)
            self.starts = (core_at, plane_at, plane_at + far * piece)
            self.result_hbm = result_hbm
            rows = self.rows(core_at, half)
            self.keep = pltpu.make_async_copy(result.at[rows], result_hbm.at[rows], in_sem.at[4 + (first_sem > 0)])
            self.stage = 0

        def rows(self, at, size):
            return pl.ds(pl.multiple_of(at, 16), size)

        def copy(self, at, src, dst, peer):
            return remote(src, dst, (sum_send, sum_recv), self.first_sem + at, peer)

        def out(self, level):
            if level == 0:
                rows = self.rows((1 - core) * self.sizes[0], self.sizes[0])
                return [self.copy(0, self.own.at[rows], self.by_core, core_peer)]
            copies = []
            size = self.sizes[level]
            if level == 1:
                for step in range(1, 4):
                    rows = self.rows(self.starts[0] + (plane + step) % 4 * size, size)
                    copies.append(self.copy(step, self.own.at[rows], self.by_plane.at[step - 1], plane_peer(step)))
            else:
                for step in range(1, far_count):
                    rows = self.rows(self.starts[1] + (far + step) % far_count * size, size)
                    copies.append(self.copy(3 + step, self.own.at[rows], self.by_far.at[step - 1], far_peer(step)))
            return copies

        def back(self, level):
            src = self.result.at[self.rows(self.starts[level], self.sizes[level])]
            first = 2 + far_count
            if level == 2:
                return [self.copy(first + step, src, src, far_peer(step)) for step in range(1, far_count)]
            if level == 1:
                return [self.copy(first + far_count - 1 + step, src, src, plane_peer(step)) for step in range(1, 4)]
            rows = self.rows(self.starts[0], self.sizes[0])
            return [self.copy(first + far_count + 3, src, self.result_hbm.at[rows], core_peer)]

        def add(self, level):
            rows = self.rows(self.starts[level], self.sizes[level])
            total = self.own[rows, :].astype(f32)
            if level == 0:
                total = total + self.by_core[...].astype(f32)
            else:
                others = self.by_plane if level == 1 else self.by_far
                for step in range(others.shape[0]):
                    total = total + others[step].astype(f32)
            target = self.result if level == 2 else self.own
            target[rows, :] = total.astype(bf16)

        def step(self):
            stage = self.stage
            self.stage += 1
            if 1 <= stage <= 3:
                finish(self.out(stage - 1))
                self.add(stage - 1)
            if stage >= 4:
                finish(self.back(6 - stage))
            if stage <= 2:
                start(self.out(stage))
            elif stage <= 5:
                start(self.back(5 - stage))
            if stage == 5:
                self.keep.start()

    class ShortSum:
        def __init__(self, first_sem, own, by_core, by_chip, result, result_hbm):
            self.first_sem, self.own, self.result = first_sem, own, result
            self.by_core, self.by_chip = by_core, by_chip
            self.half = own.shape[0] // 2
            self.piece = self.half // chips
            self.core_at = core * self.half
            self.chip_at = self.core_at + chip * self.piece
            self.result_hbm = result_hbm
            rows = self.rows(self.core_at, self.half)
            self.keep = pltpu.make_async_copy(result.at[rows], result_hbm.at[rows], in_sem.at[6])
            self.stage = 0

        def rows(self, at, size):
            return pl.ds(pl.multiple_of(at, 16), size)

        def copy(self, at, src, dst, peer):
            return remote(src, dst, (sum_send, sum_recv), self.first_sem + at, peer)

        def core_out(self):
            rows = self.rows((1 - core) * self.half, self.half)
            return [self.copy(0, self.own.at[rows], self.by_core, core_peer)]

        def chip_out(self):
            copies = []
            for step in range(1, chips):
                rows = self.rows(self.core_at + (chip + step) % chips * self.piece, self.piece)
                copies.append(self.copy(step, self.own.at[rows], self.by_chip.at[step - 1], chip_peer(step)))
            return copies

        def chip_back(self):
            src = self.result.at[self.rows(self.chip_at, self.piece)]
            return [self.copy(chips - 1 + step, src, src, chip_peer(step)) for step in range(1, chips)]

        def core_back(self):
            rows = self.rows(self.core_at, self.half)
            return [self.copy(2 * chips - 1, self.result.at[rows], self.result_hbm.at[rows], core_peer)]

        def step(self):
            stage = self.stage
            self.stage += 1
            if stage == 0:
                start(self.core_out())
            elif stage == 1:
                finish(self.core_out())
                rows = self.rows(self.core_at, self.half)
                total = self.own[rows, :].astype(f32) + self.by_core[...].astype(f32)
                self.own[rows, :] = total.astype(bf16)
                start(self.chip_out())
            elif stage == 2:
                finish(self.chip_out())
                rows = self.rows(self.chip_at, self.piece)
                total = self.own[rows, :].astype(f32)
                for step in range(chips - 1):
                    total = total + self.by_chip[step].astype(f32)
                self.result[rows, :] = total.astype(bf16)
                start(self.chip_back())
            elif stage == 3:
                finish(self.chip_back())
                start(self.core_back())
                self.keep.start()
            else:
                finish(self.core_back())

    class Small:
        def __init__(self, first_sem):
            self.first_sem, self.stage = first_sem, 0
            self.keep = pltpu.make_async_copy(small, small_hbm, in_sem.at[3])

        def copies(self, level):
            first = (0, 1, 2, 1 + far_count)[level]
            peers = ([core_peer], [near_peer], [far_peer(step) for step in range(1, far_count)], [across_peer])[level]
            return [
                remote(small, small_there.at[first + i], (sum_send, sum_recv), self.first_sem + first + i, peer)
                for i, peer in enumerate(peers)
            ]

        def step(self):
            stage = self.stage
            self.stage += 1
            if stage > 0:
                copies = self.copies(stage - 1)
                finish(copies)
                first = (0, 1, 2, 1 + far_count)[stage - 1]
                total = small[...]
                for i in range(len(copies)):
                    total = total + small_there[first + i]
                small[...] = total
            if stage < 4:
                start(self.copies(stage))
            else:
                self.keep.start()

    def start(copies):
        for copy in copies:
            copy.start()

    def finish(copies):
        for copy in copies:
            copy.wait()

    sems = 6 + 2 * far_count
    sum_down = Sum(0, down, down_core, down_plane, down_far, down_all, down_hbm)
    sum_up = Sum(sems, up, up_core, up_plane, up_far, up_all, up_hbm)
    sum_qkv = ShortSum(2 * sems, qkv, qkv_core, qkv_chip, qkv_all, qkv_hbm)
    sum_small = Small(2 * sems + 2 * chips)

    def pack(target, at, source):
        height = source.shape[0]
        for i in range(source.shape[1] // 128):
            target[at + i * height : at + (i + 1) * height, :] = source[:, i * 128 : i * 128 + 128].astype(bf16)

    def clear(target, used):
        if target.shape[0] > used:
            target[used:, :] = jnp.zeros((target.shape[0] - used, 128), bf16)

    def state_copy():
        return remote(states.at[1 - part], states_hbm.at[part], (swap_send, swap_recv), 0, across_peer)

    def main_copy(t, b):
        rows = slice(b * BLOCK, b * BLOCK + BLOCK)
        return remote(grads.at[t, rows], grads_hbm.at[part, rows], (swap_send, swap_recv), 1 + b, across_peer)

    def extra_copy(t, b):
        rows = slice(b * BLOCK, b * BLOCK + BLOCK)
        there = b % (count // 2)
        half_rows = slice(there * BLOCK, there * BLOCK + BLOCK)
        return remote(
            grads.at[t, rows], extra_hbm.at[part, half_rows], (swap_send, swap_recv), 1 + count + there, across_peer
        )

    loads = [
        pltpu.make_async_copy(hbm.at[part], dest, in_sem.at[i])
        for i, (hbm, dest) in enumerate(((start_hbm, start_v), (emb_hbm, emb_v), (cot_hbm, grads.at[2])))
    ]
    for load in loads:
        load.start()

    lane = lax.broadcasted_iota(jnp.int32, (128, 128), 1) & 63
    ids = jnp.where(part == 0, seg_ref[0:1, :], seg_ref[1:2, :])
    for c in range(length // 128):
        tokens = slice(c * 128, c * 128 + 128)
        turned = jnp.broadcast_to(ids[:, tokens].astype(f32), (128, 128)).T.astype(jnp.int32)
        kx[tokens, :] = jnp.where(turned == lane, 1.0, 0.0).astype(bf16)
    code = lax.broadcasted_iota(jnp.int32, (16, length), 0)
    unlike = jnp.where((code < 8) & (code != ids), masked_score, 0.0).astype(bf16)
    for h in range(HEADS):
        spare = 64 - h % 2 * 64
        for t in range(2):
            qa[t, h, spare : spare + 64, :] = jnp.zeros((64, length), bf16)
            qa[t, h, spare : spare + 16, :] = unlike
        goa[h, spare : spare + 64, :] = jnp.zeros((64, length), bf16)
        vt[h, 64:80, :] = jnp.ones((16, length), bf16)
    key_at = lax.broadcasted_iota(jnp.int32, (128, 128), 0)
    query_at = lax.broadcasted_iota(jnp.int32, (128, 128), 1)
    edge[0] = jnp.where(key_at <= query_at, 0.0, masked_score)
    live = key_at + (length - 128) < length - pad_ref[part]
    edge[1] = jnp.where((key_at == query_at) | ((key_at < query_at) & live), 0.0, masked_score)
    wq_t[...] = wqkv_ref[:, :width].T
    qb_t[...] = jnp.broadcast_to(row_of(qb_ref), (128, width)).T

    for load in loads:
        load.wait()
    xbuf[...] = start_v[...].astype(f32) + emb_v[...].astype(f32)

    low_half = lax.broadcasted_iota(jnp.int32, (BLOCK, 128), 1) < 64
    ones = jnp.ones((BLOCK, 128), bf16)

    def rows_at(b):
        return pl.ds(pl.multiple_of(b * BLOCK, BLOCK), BLOCK)

    def forward(t):
        def project(b, _):
            rows = rows_at(b)
            hat, scale = normalise(xbuf[rows, :])
            normed = (hat * row_of(g1_ref) + row_of(b1_ref)).astype(bf16)
            hat1[t, rows, :] = hat
            scales[t, rows, 0:1] = scale
            normed1[t, rows, :] = normed
            bias = jnp.concatenate([qb_t[...], qb_t[...]], axis=1)
            q = (mul_rows(wq_t[...], normed) + bias).astype(bf16) * jnp.asarray(HEAD_DIM**-0.5, bf16)
            k = mul(normed, wqkv_ref[:, width : 2 * width]).astype(bf16)
            v = (mul(normed, wqkv_ref[:, 2 * width :]) + row_of(vb_ref)).astype(bf16)
            kt[t, :, rows] = k.T
            turned = v.T
            for h in range(HEADS):
                lanes = slice(h // 2 * 128, h // 2 * 128 + 128)
                own = h % 2 * 64
                head = slice(h * HEAD_DIM, h * HEAD_DIM + HEAD_DIM)
                mine = low_half if h % 2 == 0 else jnp.logical_not(low_half)
                qa[t, h, own : own + 64, rows] = q[head]
                ka[h, rows, :] = jnp.where(mine, k[:, lanes], kx[rows, :])
                va[t, h, rows, :] = jnp.where(mine, v[:, lanes], ones)
                vt[h, 0:64, rows] = turned[head]
            return 0

        lax.fori_loop(0, count, project, 0, unroll=4)

        def attend(pair, _):
            units = [(parity, *block) for block in blocks_of(length)[0] for parity in range(2)]
            buffers = (score_a, score_b, score_c, score_d)

            def score(i):
                parity, b, first, store = units[i]
                h, wide = 2 * pair + parity, (b + 1 - first) * BLOCK
                rows = slice(b * BLOCK, b * BLOCK + BLOCK)
                keys = slice(first * BLOCK, b * BLOCK + BLOCK)
                buffers[i % 4][0:wide, :] = mul(ka[h, keys, :], qa[t, h, :, rows])

            def weigh(i):
                parity, b, first, store = units[i]
                h, wide = 2 * pair + parity, (b + 1 - first) * BLOCK
                rows = slice(b * BLOCK, b * BLOCK + BLOCK)
                keys = slice(first * BLOCK, b * BLOCK + BLOCK)
                for half in range(2):
                    low, high = reach(half, b - first, wide)
                    lanes = slice(half * 128, half * 128 + 128)
                    last = edge[1 if b == count - 1 and half == 1 else 0]
                    scores = buffers[i % 4][low : high - 128, lanes]
                    border = buffers[i % 4][high - 128 : high, lanes] + last
                    peak = jnp.max(border, axis=0, keepdims=True)
                    if high - 128 > low:
                        peak = jnp.maximum(peak, jnp.max(scores, axis=0, keepdims=True))
                        expo[t, h, store + low : store + high - 128, lanes] = jnp.exp(scores - peak).astype(bf16)
                    expo[t, h, store + high - 128 : store + high, lanes] = jnp.exp(border - peak).astype(bf16)
                    if low > 0:
                        expo[t, h, store : store + low, lanes] = jnp.zeros((low, 128), bf16)
                    if high < wide:
                        expo[t, h, store + high : store + wide, lanes] = jnp.zeros((wide - high, 128), bf16)
                result = mul(vt[h, :, keys], expo[t, h, store : store + wide, :])
                inv = 1.0 / result[64:72]
                inverse[t, h, :, rows] = inv
                head_rows = pl.ds(pl.multiple_of(h * HEAD_DIM, HEAD_DIM), HEAD_DIM)
                outcome[t, head_rows, rows] = result[0:64] * inv[0:1]

            score(0)
            score(1)
            for i in range(0, len(units), 2):
                if i + 2 < len(units):
                    score(i + 2)
                    score(i + 3)
                weigh(i)
                weigh(i + 1)
            return 0

        lax.fori_loop(0, HEADS // 2, attend, 0, unroll=2)

        def feed(b, _):
            rows = rows_at(b)
            turned = outcome[t, :, rows].astype(bf16).T
            middle = xbuf[rows, :] + row_of(ob_ref) + mul(turned, wout_ref[...])
            hat, scale = normalise(middle)
            normed = (hat * row_of(g2_ref) + row_of(b2_ref)).astype(bf16)
            hat2[t, rows, :] = hat
            scales[t, rows, 1:2] = scale
            normed2[t, rows, :] = normed
            for c in range(wup_ref.shape[1] // 256):
                columns = slice(c * 256, c * 256 + 256)
                hidden = mul(normed, wup_ref[:, columns]) + row_of(ub_ref)[:, columns]
                inner = hidden * 0.7071067811865476
                phi = 0.5 * lax.erf(inner) + 0.5
                bell = jnp.exp2(inner * -1.4426950408889634 * inner)
                active[t, rows, columns] = (hidden * phi).astype(bf16)
                slope[t, rows, columns] = (phi + hidden * bell * 0.3989422804014327).astype(bf16)
            total = middle + row_of(db_ref) + mul(active[t, rows, :], wdown_ref[...])
            state = total.astype(bf16)
            states[t, rows, :] = state
            xbuf[rows, :] = state.astype(f32) + emb_v[rows, :].astype(f32)
            return 0

        lax.fori_loop(0, count, feed, 0, unroll=4)
    forward(0)
    forward(1)

    for total in (sums, qv_sums):
        total[...] = jnp.zeros_like(total)
    pl.semaphore_wait(barrier, len(peers))
    state_copy().start()
    keep_state = pltpu.make_async_copy(states.at[part], states_hbm.at[part], in_sem.at[0])
    keep_state.start()

    def add_to(total, term, t):
        if t == 1:
            total[...] = term
        else:
            total[...] += term

    def add_sums(at, values):
        columns = slice(at, at + values.shape[1])
        sums[:, columns] += eight_sums(values)

    def send(now, blocks):
        @pl.when(part == 1 - now)
        def _():
            for b in blocks:
                main_copy(now, b).start()

        extra = [b for b in blocks if b // (count // 2) == 1 - now]
        if extra:
            @pl.when(part == now)
            def _():
                for b in extra:
                    extra_copy(now, b).start()

    totals = {"D": sum_down, "U": sum_up, "Q": sum_qkv, "S": sum_small}

    def perform(action):
        if action in totals:
            totals[action].step()
        else:
            send(0, [int(action)])

    def backward(t):
        def hook(point):
            if t == 0:
                for action in HOOKS.get(point, ()):
                    perform(action)

        def feed_back(b, _):
            rows = rows_at(b)
            down = grads[t + 1, rows, :]
            down_wide = down.astype(f32)
            add_sums(DB, down_wide)
            for c in range(wup_ref.shape[1] // 256):
                columns = slice(c * 256, c * 256 + 256)
                up_grad = mul_rows(down, wdown_ref[columns, :]) * slope[t, rows, columns].astype(f32)
                up_grad = up_grad.astype(bf16)
                hgrad[rows, columns] = up_grad
                add_sums(UB + c * 256, up_grad.astype(f32))
            cotangent = mul_rows(hgrad[rows, :], wup_ref[...])
            hat = hat2[t, rows, :]
            add_sums(N2G, cotangent * hat)
            add_sums(N2B, cotangent)
            middle = down_wide + norm_back(cotangent, row_of(g2_ref), hat, scales[t, rows, 1:2])
            mgrad[rows, :] = middle
            low = middle.astype(bf16)
            branch[rows, :] = low
            add_sums(OB, low.astype(f32))
            attended_grad = mul_rows(wout_ref[...], low).astype(bf16).astype(f32)
            line = lax.broadcasted_iota(jnp.int32, (16, BLOCK), 0)
            for h in range(HEADS):
                own = h % 2 * 64
                head = slice(h * HEAD_DIM, h * HEAD_DIM + HEAD_DIM)
                scaled = (attended_grad[head] * inverse[t, h, 0:1, rows]).astype(bf16)
                inner = -jnp.sum(scaled.astype(f32) * outcome[t, head, rows], axis=0, keepdims=True)
                high = inner.astype(bf16).astype(f32)
                extra = jnp.where(line == 0, high, jnp.where(line == 1, inner - high, 0.0))
                goa[h, own : own + 64, rows] = scaled
                goa[h, 64 - own : 80 - own, rows] = extra.astype(bf16)
            return 0

        lax.fori_loop(0, count, feed_back, 0, unroll=4)

        add_to(gdown, mul_columns(grads[t + 1], active[t]), t)
        if t == 0:
            pack(down, 0, gdown)
            clear(down, DOWN_ROWS)
            sum_down.step()

        add_to(gup, mul_columns(normed2[t], hgrad[...]), t)
        add_to(gout, mul(outcome[t].astype(bf16), branch[...]), t)

        if t == 0:
            pack(up, 0, gup)
            pack(up, OUT_AT, gout)
            clear(up, UP_ROWS)
            sum_up.step()

        def attend_back(b, first, store):
            rows = slice(b * BLOCK, b * BLOCK + BLOCK)
            keys = slice(first * BLOCK, b * BLOCK + BLOCK)
            wide = (b + 1 - first) * BLOCK
            buffers = (slope_a, slope_b)

            def slopes(h):
                values = mul(va[t, h, keys, :], goa[h, :, rows])
                values = expo[t, h, store : store + wide, :].astype(f32) * values
                buffers[h % 2][0:wide, :] = values.astype(bf16)

            def spread(h):
                head = slice(h * HEAD_DIM, h * HEAD_DIM + HEAD_DIM)
                own = slice(h % 2 * 64, h % 2 * 64 + 64)
                score_grad = buffers[h % 2][0:wide, :]
                query_part = mul(kt[t, head, keys], score_grad)
                pgrad[head, rows] = (query_part * HEAD_DIM**-0.5).astype(bf16)
                key_part = mul_rows(qa[t, h, own, rows], score_grad)
                value_part = mul_rows(goa[h, own, rows], expo[t, h, store : store + wide, :])
                for kb in range(first, b + 1):
                    mine = slice((kb - first) * BLOCK, (kb - first) * BLOCK + BLOCK)
                    there = slice(kb * BLOCK, kb * BLOCK + BLOCK)
                    if b == min(count - 1, kb + SPAN // BLOCK):
                        dkt[head, there] = key_part[:, mine]
                        dvt[head, there] = value_part[:, mine]
                    else:
                        dkt[head, there] += key_part[:, mine]
                        dvt[head, there] += value_part[:, mine]

            slopes(0)
            for h in range(HEADS):
                if h + 1 < HEADS:
                    slopes(h + 1)
                spread(h)

        def input_back(b):
            rows = slice(b * BLOCK, b * BLOCK + BLOCK)
            if t == 1:
                pgrad[width : 2 * width, rows] = dkt[:, rows].astype(bf16)
                pgrad[2 * width :, rows] = dvt[:, rows].astype(bf16)
            part_grad = pgrad[:, rows]
            for lanes in (slice(0, 128), slice(128, 256)):
                qv_sums[0:width, :] += part_grad[:width, lanes].astype(f32)
                qv_sums[width:, :] += part_grad[2 * width :, lanes].astype(f32)
            cotangent = mul(wqkv_ref[...], part_grad).T
            hat = hat1[t, rows, :]
            add_sums(N1G, cotangent * hat)
            add_sums(N1B, cotangent)
            x_grad = mgrad[rows, :] + norm_back(cotangent, row_of(g1_ref), hat, scales[t, rows, 0:1])
            grads[t, rows, :] = x_grad.astype(bf16)

        last = t == 0
        for b, first, store in reversed(blocks_of(length)[0]):
            attend_back(b, first, store)
            if b + 1 < count and (False or not last):
                input_back(b + 1)
                if not last and True:
                    send(1, [b + 1])
            hook(f"a{b}")
        pgrad[width : 2 * width, 0:BLOCK] = dkt[:, 0:BLOCK].astype(bf16)
        pgrad[2 * width :, 0:BLOCK] = dvt[:, 0:BLOCK].astype(bf16)
        if last and not False:
            for b in range(1, count):
                rows = slice(b * BLOCK, b * BLOCK + BLOCK)
                pgrad[width : 2 * width, rows] = dkt[:, rows].astype(bf16)
                pgrad[2 * width :, rows] = dvt[:, rows].astype(bf16)
        add_to(gqkv, mul(pgrad[...], normed1[t]), t)
        if last:
            pack(qkv, 0, gqkv)
            clear(qkv, QKV_ROWS)
            sum_qkv.step()
            hook("q")
        for b in reversed(range(1 if False or not last else count)):
            input_back(b)
            hook(f"f{b}")
        if not last:
            send(1, [0] if True else range(count))

    backward(1)
    backward(0)

    sums[0:1, QB : QB + width] = jnp.sum(qv_sums[0:width, :].T, axis=0, keepdims=True)
    sums[0:1, VB : VB + width] = jnp.sum(qv_sums[width:, :].T, axis=0, keepdims=True)
    total = jnp.sum(sums[...], axis=0, keepdims=True)
    small[...] = jnp.concatenate([total[:, i * 128 : i * 128 + 128] for i in range(SUMS // 128)], axis=0)
    sum_small.step()
    half_rows = pl.ds(pl.multiple_of(part * (length // 2), BLOCK), length // 2)
    keep_grad = pltpu.make_async_copy(grads.at[part], grads_hbm.at[part], in_sem.at[1])
    keep_extra = pltpu.make_async_copy(grads.at[1 - part, half_rows], extra_hbm.at[part], in_sem.at[2])
    keep_grad.start()
    keep_extra.start()
    for action in "DUSDUSQDUSQDUSQDU":
        perform(action)

    state_copy().wait()
    for b in range(count):
        main_copy(0, b).wait()
    for b in range(count // 2):
        extra_copy(0, b).wait()
    for keep in (keep_state, keep_grad, keep_extra, sum_small.keep, sum_down.keep, sum_up.keep, sum_qkv.keep):
        keep.wait()


def padded(rows, devices):
    unit = 16 * devices
    return (rows + unit - 1) // unit * unit


def finish_kernel(
    states_hbm, grads_hbm, extra_hbm, down_hbm, up_hbm, qkv_hbm, small_hbm,
    loop_out, grad_out, embed_out, n1g, n1b, gqkv, qb, vb, gout, ob, n2g, n2b, gup, ub, gdown, db,
    states, grads, extra, down, up, qkv, small, grad_v, embed_v, gqkv_v, gout_v, gup_v, gdown_v, sems,
):
    part = lax.axis_index("section")
    length, width = grads.shape[1:]

    def copy(at, src, dst):
        return pltpu.make_async_copy(src, dst, sems.at[at])

    passed = copy(0, states_hbm, states)
    loads = [
        copy(1, grads_hbm, grads), copy(2, extra_hbm, extra), copy(3, up_hbm, up), copy(4, down_hbm, down),
        copy(12, qkv_hbm, qkv), copy(13, small_hbm, small),
    ]
    passed.start()
    for load in loads:
        load.start()
    passed.wait()
    stores = [copy(11, states, loop_out.at[0])]
    stores[-1].start()
    loads[0].wait()
    grad_v[...] = grads[...].astype(f32)
    stores.append(copy(5, grad_v, grad_out.at[0]))
    stores[-1].start()
    loads[1].wait()
    half_rows = pl.ds(pl.multiple_of(part * (length // 2), BLOCK), length // 2)
    embed_v[...] = grads[:, half_rows, :].astype(f32) + extra[...].astype(f32)
    stores.append(copy(6, embed_v, embed_out))
    stores[-1].start()
    loads[2].wait()
    for i in range(gup_v.shape[1] // 128):
        lanes = slice(i * 128, i * 128 + 128)
        gup_v[:, lanes] = up[i * width : (i + 1) * width, :].astype(f32)
    stores.append(copy(7, gup_v, gup))
    stores[-1].start()
    for i in range(width // 128):
        at = OUT_AT + i * width
        gout_v[:, i * 128 : i * 128 + 128] = up[at : at + width, :].astype(f32)
    stores.append(copy(9, gout_v, gout))
    stores[-1].start()
    loads[3].wait()
    for i in range(gup_v.shape[1] // 128):
        gdown_v[i * 128 : i * 128 + 128, :] = down[i * width : (i + 1) * width, :].T.astype(f32)
    stores.append(copy(8, gdown_v, gdown))
    stores[-1].start()
    loads[4].wait()
    for i in range(width // 128):
        turned = qkv[i * 3 * width : (i + 1) * 3 * width, :].T
        gqkv_v[i * 128 : i * 128 + 128, :] = turned.astype(f32)
    stores.append(copy(10, gqkv_v, gqkv))
    stores[-1].start()
    loads[5].wait()
    for at, ref in ((N1G, n1g), (N1B, n1b), (QB, qb), (VB, vb), (OB, ob), (N2G, n2g), (N2B, n2b), (DB, db), (UB, ub)):
        for i in range(ref.shape[0] // 128):
            ref[i * 128 : i * 128 + 128] = small[at // 128 + i]
    for store in stores:
        store.wait()


def whole_block(sections, places, *args):
    start = args[0]
    _, length, width = start.shape
    hidden = args[15].shape[0]
    vmem = pl.BlockSpec(memory_space=pltpu.VMEM)
    smem = pl.BlockSpec(memory_space=pltpu.SMEM)
    hbm = pl.BlockSpec(memory_space=pl.ANY)
    count = length // BLOCK
    devices = sections * places
    far_count = places // 4
    payloads = [padded(rows, devices) for rows in (DOWN_ROWS, UP_ROWS, QKV_ROWS)]

    def V(*shape, dtype=bf16):
        return pltpu.VMEM(shape, dtype)

    def O(*shape, dtype=f32):
        return jax.ShapeDtypeStruct(shape, dtype)

    def sum_buffers(rows):
        return [
            V(rows, 128),
            V(rows // 2, 128),
            V(3, rows // 8, 128),
            V(far_count - 1, rows // devices, 128),
            V(rows, 128),
        ]

    copies = 2 * (6 + 2 * far_count) + devices + 2 + far_count
    between = pl.pallas_call(
        partial(compute_kernel, far_count),
        name="block_both_ways",
        in_specs=[hbm, hbm, hbm, vmem, smem] + [vmem] * 13,
        out_specs=[hbm] * 7,
        out_shape=[
            O(2, length, width, dtype=bf16),
            O(2, length, width, dtype=bf16),
            O(2, length // 2, width, dtype=bf16),
            *(O(rows, 128, dtype=bf16) for rows in payloads),
            O(SUMS // 128, 128),
        ],
        scratch_shapes=[
            V(length, width),
            V(length, width),
            V(length, 128),
            V(width, width),
            V(width, 128, dtype=f32),
            V(2, 128, 128, dtype=f32),
            V(SPAN + BLOCK, BLOCK, dtype=f32),
            V(SPAN + BLOCK, BLOCK, dtype=f32),
            V(SPAN + BLOCK, BLOCK, dtype=f32),
            V(SPAN + BLOCK, BLOCK, dtype=f32),
            V(SPAN + BLOCK, BLOCK),
            V(SPAN + BLOCK, BLOCK),
            V(length, width, dtype=f32),
            V(2, length, width, dtype=f32),
            V(2, length, 128, dtype=f32),
            V(2, length, width),
            V(2, HEADS, 128, length),
            V(HEADS, length, 128),
            V(2, width, length),
            V(2, HEADS, length, 128),
            V(HEADS, 80, length),
            V(2, HEADS, blocks_of(length)[1], BLOCK),
            V(2, HEADS, 8, length, dtype=f32),
            V(2, width, length, dtype=f32),
            V(2, length, width, dtype=f32),
            V(2, length, width),
            V(2, length, hidden),
            V(2, length, hidden),
            V(length, hidden),
            V(length, width),
            V(length, width, dtype=f32),
            V(3, length, width),
            V(2, length, width),
            V(HEADS, 128, length),
            V(width, length, dtype=f32),
            V(width, length, dtype=f32),
            V(3 * width, length),
            V(3 * width, width, dtype=f32),
            V(width, width, dtype=f32),
            V(width, hidden, dtype=f32),
            V(width, hidden, dtype=f32),
            V(8, SUMS, dtype=f32),
            V(2 * width, 128, dtype=f32),
        ]
        + sum_buffers(payloads[0])
        + sum_buffers(payloads[1])
        + [
            V(payloads[2], 128),
            V(payloads[2] // 2, 128),
            V(devices // 2 - 1, payloads[2] // devices, 128),
            V(payloads[2], 128),
        ]
        + [
            V(SUMS // 128, 128, dtype=f32),
            V(2 + far_count, SUMS // 128, 128, dtype=f32),
            pltpu.SemaphoreType.DMA((7,)),
            pltpu.SemaphoreType.DMA((1 + count + count // 2,)),
            pltpu.SemaphoreType.DMA((1 + count + count // 2,)),
            pltpu.SemaphoreType.DMA((copies,)),
            pltpu.SemaphoreType.DMA((copies,)),
        ],
        compiler_params=pltpu.CompilerParams(
            vmem_limit_bytes=63 << 20, collective_id=0, has_side_effects=True
        ),
    )(*args)
    return pl.pallas_call(
        finish_kernel,
        name="widen",
        in_specs=[hbm] * 7,
        out_specs=[hbm, hbm, hbm, vmem, vmem, hbm, vmem, vmem, hbm, vmem, vmem, vmem, hbm, vmem, hbm, vmem],
        out_shape=[
            O(1, 2, length, width, dtype=bf16),
            O(1, 2, length, width),
            O(2, length // 2, width),
            O(width), O(width), O(width, 3 * width), O(width), O(width), O(width, width), O(width),
            O(width), O(width), O(width, hidden), O(hidden), O(hidden, width), O(width),
        ],
        scratch_shapes=[
            V(2, length, width),
            V(2, length, width),
            V(2, length // 2, width),
            V(payloads[0], 128),
            V(payloads[1], 128),
            V(payloads[2], 128),
            V(SUMS // 128, 128, dtype=f32),
            V(2, length, width, dtype=f32),
            V(2, length // 2, width, dtype=f32),
            V(width, 3 * width, dtype=f32),
            V(width, width, dtype=f32),
            V(width, hidden, dtype=f32),
            V(hidden, width, dtype=f32),
            pltpu.SemaphoreType.DMA((14,)),
        ],
        compiler_params=pltpu.CompilerParams(vmem_limit_bytes=63 << 20),
    )(*between)


def solution(mesh):
    rows = P("dp", None, None)
    return jax.shard_map(
        partial(whole_block, mesh.shape["section"], mesh.shape["dp"]),
        mesh=mesh,
        in_specs=(rows, rows, rows, P("dp", None), P("dp")) + (P(),) * 13,
        out_specs=(
            P("section", "dp", None, None),
            P("section", "dp", None, None),
            P("dp", "section", None),
        )
        + (P(),) * 13,
        check_vma=False,
    )
```

```python
from functools import partial

import jax
import jax.numpy as jnp
from jax import lax
from jax.experimental import pallas as pl
from jax.experimental.pallas import tpu as pltpu
from jax.sharding import PartitionSpec as P

HEADS = 4
HEAD_DIM = 64
BLOCK = 256
SPAN = 512
norm_eps = 1e-05
masked_score = -1e30
bf16 = jnp.bfloat16
f32 = jnp.float32


def mul(left, right):
    return jnp.dot(left, right, preferred_element_type=f32)


def mul_rows(left, right):
    return lax.dot_general(left, right, (((1,), (1,)), ((), ())), preferred_element_type=f32)


def mul_columns(left, right):
    return lax.dot_general(left, right, (((0,), (0,)), ((), ())), preferred_element_type=f32)


def row_of(ref):
    return ref[...].reshape(1, ref.shape[0])


def eight_sums(values):
    rows, width = values.shape
    return jnp.sum(values.reshape(rows // 8, 8, width), axis=0)


def normalise(x):
    average = jnp.mean(x, axis=-1, keepdims=True)
    centred = x - average
    spread = jnp.mean(centred * centred, axis=-1, keepdims=True)
    scale = lax.rsqrt(spread + norm_eps)
    return centred * scale, scale


def norm_back(cotangent, gain, hat, scale):
    scaled = cotangent * gain
    first = jnp.mean(scaled, axis=-1, keepdims=True)
    second = jnp.mean(scaled * hat, axis=-1, keepdims=True)
    return scale * (scaled - first - hat * second)


def blocks_of(length):
    result, store = [], 0
    for b in range(length // BLOCK):
        first = max(0, b - SPAN // BLOCK)
        result.append((b, first, store))
        store += (b + 1 - first) * BLOCK
    return result, store


def reach(half, distance, wide):
    low = 128 if half == 1 and distance == SPAN // BLOCK else 0
    return low, wide - (128 if half == 0 else 0)


HOOKS = {"a3": "DU", "f2": "Q32", "f1": "D", "f0": "U10"}
N1G, N1B, QB, VB, OB, N2G, N2B, DB, UB = (256 * i for i in range(9))
SUMS = 256 * 12
DOWN_ROWS, OUT_AT, UP_ROWS, QKV_ROWS = 2048, 2048, 2560, 1536
MESH = pl.DeviceIdType.MESH


def compute_kernel(
    far_count,
    start_hbm, emb_hbm, cot_hbm, seg_ref, pad_ref,
    g1_ref, b1_ref, wqkv_ref, qb_ref, vb_ref, wout_ref, ob_ref, g2_ref, b2_ref, wup_ref, ub_ref,
    wdown_ref, db_ref,
    states_hbm, grads_hbm, extra_hbm, down_hbm, up_hbm, qkv_hbm, small_hbm,
    start_v, emb_v, kx, wq_t, qb_t, edge, score_a, score_b, score_c, score_d, slope_a, slope_b, slope_c, slope_d,
    xbuf, hat1, scales, normed1, qa, ka, kt, va, vt, expo, inverse,
    outcome, hat2, normed2, active, slope, hgrad, branch, mgrad, grads, states, goa,
    dkt, dvt, pgrad, gqkv, gout, gup, gdown, sums, qv_sums,
    down, down_core, down_plane, down_far, down_all,
    up, up_core, up_plane, up_far, up_all,
    qkv, qkv_core, qkv_chip, qkv_all,
    small, small_there, in_sem, swap_send, swap_recv, sum_send, sum_recv,
):
    length, width = xbuf.shape
    count = length // BLOCK
    part = lax.axis_index("section")
    place = lax.axis_index("dp")
    core, near, far = place % 2, (place // 2) % 2, place // 4

    across_peer = (1 - part, place)
    core_peer = (part, place + 1 - 2 * core)
    near_peer = (part, place + 2 - 4 * near)

    plane = 2 * part + near

    def plane_peer(step):
        there = (plane + step) % 4
        return (there // 2, 4 * far + 2 * (there % 2) + core)

    def far_peer(step):
        return (part, 4 * ((far + step) % far_count) + 2 * near + core)

    chips = lax.axis_size("section") * lax.axis_size("dp") // 2
    chip = part * (chips // 2) + place // 2

    def chip_peer(step):
        there = (chip + step) % chips
        return (there // (chips // 2), 2 * (there % (chips // 2)) + core)

    peers = [core_peer] + [chip_peer(step) for step in range(1, chips)]
    barrier = pltpu.get_barrier_semaphore()
    for peer in peers:
        pl.semaphore_signal(barrier, inc=1, device_id=peer, device_id_type=MESH)

    def remote(src, dst, sems, at, peer):
        return pltpu.make_async_remote_copy(
            src_ref=src, dst_ref=dst, send_sem=sems[0].at[at], recv_sem=sems[1].at[at],
            device_id=peer, device_id_type=MESH,
        )

    class Sum:
        def __init__(self, first_sem, own, by_core, by_plane, by_far, result, result_hbm):
            self.first_sem, self.own, self.result = first_sem, own, result
            self.by_core, self.by_plane, self.by_far = by_core, by_plane, by_far
            half = own.shape[0] // 2
            quarter = half // 4
            piece = quarter // far_count
            core_at = core * half
            plane_at = core_at + plane * quarter
            self.sizes = (half, quarter, piece)
            self.starts = (core_at, plane_at, plane_at + far * piece)
            self.result_hbm = result_hbm
            rows = self.rows(core_at, half)
            self.keep = pltpu.make_async_copy(result.at[rows], result_hbm.at[rows], in_sem.at[4 + (first_sem > 0)])
            self.stage = 0

        def rows(self, at, size):
            return pl.ds(pl.multiple_of(at, 16), size)

        def copy(self, at, src, dst, peer):
            return remote(src, dst, (sum_send, sum_recv), self.first_sem + at, peer)

        def out(self, level):
            if level == 0:
                rows = self.rows((1 - core) * self.sizes[0], self.sizes[0])
                return [self.copy(0, self.own.at[rows], self.by_core, core_peer)]
            copies = []
            size = self.sizes[level]
            if level == 1:
                for step in range(1, 4):
                    rows = self.rows(self.starts[0] + (plane + step) % 4 * size, size)
                    copies.append(self.copy(step, self.own.at[rows], self.by_plane.at[step - 1], plane_peer(step)))
            else:
                for step in range(1, far_count):
                    rows = self.rows(self.starts[1] + (far + step) % far_count * size, size)
                    copies.append(self.copy(3 + step, self.own.at[rows], self.by_far.at[step - 1], far_peer(step)))
            return copies

        def back(self, level):
            src = self.result.at[self.rows(self.starts[level], self.sizes[level])]
            first = 2 + far_count
            if level == 2:
                return [self.copy(first + step, src, src, far_peer(step)) for step in range(1, far_count)]
            if level == 1:
                return [self.copy(first + far_count - 1 + step, src, src, plane_peer(step)) for step in range(1, 4)]
            rows = self.rows(self.starts[0], self.sizes[0])
            return [self.copy(first + far_count + 3, src, self.result_hbm.at[rows], core_peer)]

        def add(self, level):
            rows = self.rows(self.starts[level], self.sizes[level])
            total = self.own[rows, :].astype(f32)
            if level == 0:
                total = total + self.by_core[...].astype(f32)
            else:
                others = self.by_plane if level == 1 else self.by_far
                for step in range(others.shape[0]):
                    total = total + others[step].astype(f32)
            target = self.result if level == 2 else self.own
            target[rows, :] = total.astype(bf16)

        def step(self):
            stage = self.stage
            self.stage += 1
            if 1 <= stage <= 3:
                finish(self.out(stage - 1))
                self.add(stage - 1)
            if stage >= 4:
                finish(self.back(6 - stage))
            if stage <= 2:
                start(self.out(stage))
            elif stage <= 5:
                start(self.back(5 - stage))
            if stage == 5:
                self.keep.start()

    class ShortSum:
        def __init__(self, first_sem, own, by_core, by_chip, result, result_hbm):
            self.first_sem, self.own, self.result = first_sem, own, result
            self.by_core, self.by_chip = by_core, by_chip
            self.half = own.shape[0] // 2
            self.piece = self.half // chips
            self.core_at = core * self.half
            self.chip_at = self.core_at + chip * self.piece
            self.result_hbm = result_hbm
            rows = self.rows(self.core_at, self.half)
            self.keep = pltpu.make_async_copy(result.at[rows], result_hbm.at[rows], in_sem.at[6])
            self.stage = 0

        def rows(self, at, size):
            return pl.ds(pl.multiple_of(at, 16), size)

        def copy(self, at, src, dst, peer):
            return remote(src, dst, (sum_send, sum_recv), self.first_sem + at, peer)

        def core_out(self):
            rows = self.rows((1 - core) * self.half, self.half)
            return [self.copy(0, self.own.at[rows], self.by_core, core_peer)]

        def chip_out(self):
            copies = []
            for step in range(1, chips):
                rows = self.rows(self.core_at + (chip + step) % chips * self.piece, self.piece)
                copies.append(self.copy(step, self.own.at[rows], self.by_chip.at[step - 1], chip_peer(step)))
            return copies

        def chip_back(self):
            src = self.result.at[self.rows(self.chip_at, self.piece)]
            return [self.copy(chips - 1 + step, src, src, chip_peer(step)) for step in range(1, chips)]

        def core_back(self):
            rows = self.rows(self.core_at, self.half)
            return [self.copy(2 * chips - 1, self.result.at[rows], self.result_hbm.at[rows], core_peer)]

        def step(self):
            stage = self.stage
            self.stage += 1
            if stage == 0:
                start(self.core_out())
            elif stage == 1:
                finish(self.core_out())
                rows = self.rows(self.core_at, self.half)
                total = self.own[rows, :].astype(f32) + self.by_core[...].astype(f32)
                self.own[rows, :] = total.astype(bf16)
                start(self.chip_out())
            elif stage == 2:
                finish(self.chip_out())
                rows = self.rows(self.chip_at, self.piece)
                total = self.own[rows, :].astype(f32)
                for step in range(chips - 1):
                    total = total + self.by_chip[step].astype(f32)
                self.result[rows, :] = total.astype(bf16)
                start(self.chip_back())
            elif stage == 3:
                finish(self.chip_back())
                start(self.core_back())
                self.keep.start()
            else:
                finish(self.core_back())

    class Small:
        def __init__(self, first_sem):
            self.first_sem, self.stage = first_sem, 0
            self.keep = pltpu.make_async_copy(small, small_hbm, in_sem.at[3])

        def copies(self, level):
            first = (0, 1, 2, 1 + far_count)[level]
            peers = ([core_peer], [near_peer], [far_peer(step) for step in range(1, far_count)], [across_peer])[level]
            return [
                remote(small, small_there.at[first + i], (sum_send, sum_recv), self.first_sem + first + i, peer)
                for i, peer in enumerate(peers)
            ]

        def step(self):
            stage = self.stage
            self.stage += 1
            if stage > 0:
                copies = self.copies(stage - 1)
                finish(copies)
                first = (0, 1, 2, 1 + far_count)[stage - 1]
                total = small[...]
                for i in range(len(copies)):
                    total = total + small_there[first + i]
                small[...] = total
            if stage < 4:
                start(self.copies(stage))
            else:
                self.keep.start()

    def start(copies):
        for copy in copies:
            copy.start()

    def finish(copies):
        for copy in copies:
            copy.wait()

    sems = 6 + 2 * far_count
    sum_down = Sum(0, down, down_core, down_plane, down_far, down_all, down_hbm)
    sum_up = Sum(sems, up, up_core, up_plane, up_far, up_all, up_hbm)
    sum_qkv = ShortSum(2 * sems, qkv, qkv_core, qkv_chip, qkv_all, qkv_hbm)
    sum_small = Small(2 * sems + 2 * chips)

    def pack(target, at, source):
        height = source.shape[0]
        for i in range(source.shape[1] // 128):
            target[at + i * height : at + (i + 1) * height, :] = source[:, i * 128 : i * 128 + 128].astype(bf16)

    def clear(target, used):
        if target.shape[0] > used:
            target[used:, :] = jnp.zeros((target.shape[0] - used, 128), bf16)

    def state_copy():
        return remote(states.at[1 - part], states_hbm.at[part], (swap_send, swap_recv), 0, across_peer)

    def main_copy(t, b):
        rows = slice(b * BLOCK, b * BLOCK + BLOCK)
        return remote(grads.at[t, rows], grads_hbm.at[part, rows], (swap_send, swap_recv), 1 + b, across_peer)

    def extra_copy(t, b):
        rows = slice(b * BLOCK, b * BLOCK + BLOCK)
        there = b % (count // 2)
        half_rows = slice(there * BLOCK, there * BLOCK + BLOCK)
        return remote(
            grads.at[t, rows], extra_hbm.at[part, half_rows], (swap_send, swap_recv), 1 + count + there, across_peer
        )

    loads = [
        pltpu.make_async_copy(hbm.at[part], dest, in_sem.at[i])
        for i, (hbm, dest) in enumerate(((start_hbm, start_v), (emb_hbm, emb_v), (cot_hbm, grads.at[2])))
    ]
    for load in loads:
        load.start()

    lane = lax.broadcasted_iota(jnp.int32, (128, 128), 1) & 63
    ids = jnp.where(part == 0, seg_ref[0:1, :], seg_ref[1:2, :])
    for c in range(length // 128):
        tokens = slice(c * 128, c * 128 + 128)
        turned = jnp.broadcast_to(ids[:, tokens].astype(f32), (128, 128)).T.astype(jnp.int32)
        kx[tokens, :] = jnp.where(turned == lane, 1.0, 0.0).astype(bf16)
    code = lax.broadcasted_iota(jnp.int32, (16, length), 0)
    unlike = jnp.where((code < 8) & (code != ids), masked_score, 0.0).astype(bf16)
    for h in range(HEADS):
        spare = 64 - h % 2 * 64
        for t in range(2):
            qa[t, h, spare : spare + 64, :] = jnp.zeros((64, length), bf16)
            qa[t, h, spare : spare + 16, :] = unlike
        goa[h, spare : spare + 64, :] = jnp.zeros((64, length), bf16)
        vt[h, 64:80, :] = jnp.ones((16, length), bf16)
    key_at = lax.broadcasted_iota(jnp.int32, (128, 128), 0)
    query_at = lax.broadcasted_iota(jnp.int32, (128, 128), 1)
    edge[0] = jnp.where(key_at <= query_at, 0.0, masked_score)
    live = key_at + (length - 128) < length - pad_ref[part]
    edge[1] = jnp.where((key_at == query_at) | ((key_at < query_at) & live), 0.0, masked_score)
    wq_t[...] = wqkv_ref[:, :width].T
    qb_t[...] = jnp.broadcast_to(row_of(qb_ref), (128, width)).T

    for load in loads:
        load.wait()
    xbuf[...] = start_v[...].astype(f32) + emb_v[...].astype(f32)

    low_half = lax.broadcasted_iota(jnp.int32, (BLOCK, 128), 1) < 64
    ones = jnp.ones((BLOCK, 128), bf16)

    def rows_at(b):
        return pl.ds(pl.multiple_of(b * BLOCK, BLOCK), BLOCK)

    def forward(t):
        def project(b, _):
            rows = rows_at(b)
            hat, scale = normalise(xbuf[rows, :])
            normed = (hat * row_of(g1_ref) + row_of(b1_ref)).astype(bf16)
            hat1[t, rows, :] = hat
            scales[t, rows, 0:1] = scale
            normed1[t, rows, :] = normed
            bias = jnp.concatenate([qb_t[...], qb_t[...]], axis=1)
            q = (mul_rows(wq_t[...], normed) + bias).astype(bf16) * jnp.asarray(HEAD_DIM**-0.5, bf16)
            k = mul(normed, wqkv_ref[:, width : 2 * width]).astype(bf16)
            v = (mul(normed, wqkv_ref[:, 2 * width :]) + row_of(vb_ref)).astype(bf16)
            kt[t, :, rows] = k.T
            turned = v.T
            for h in range(HEADS):
                lanes = slice(h // 2 * 128, h // 2 * 128 + 128)
                own = h % 2 * 64
                head = slice(h * HEAD_DIM, h * HEAD_DIM + HEAD_DIM)
                mine = low_half if h % 2 == 0 else jnp.logical_not(low_half)
                qa[t, h, own : own + 64, rows] = q[head]
                ka[h, rows, :] = jnp.where(mine, k[:, lanes], kx[rows, :])
                va[t, h, rows, :] = jnp.where(mine, v[:, lanes], ones)
                vt[h, 0:64, rows] = turned[head]
            return 0

        lax.fori_loop(0, count, project, 0, unroll=4)

        def attend(pair, _):
            units = [(parity, *block) for block in blocks_of(length)[0] for parity in range(2)]
            buffers = (score_a, score_b, score_c, score_d)

            def score(i):
                parity, b, first, store = units[i]
                h, wide = 2 * pair + parity, (b + 1 - first) * BLOCK
                rows = slice(b * BLOCK, b * BLOCK + BLOCK)
                keys = slice(first * BLOCK, b * BLOCK + BLOCK)
                buffers[i % 4][0:wide, :] = mul(ka[h, keys, :], qa[t, h, :, rows])

            def weigh(i):
                parity, b, first, store = units[i]
                h, wide = 2 * pair + parity, (b + 1 - first) * BLOCK
                rows = slice(b * BLOCK, b * BLOCK + BLOCK)
                keys = slice(first * BLOCK, b * BLOCK + BLOCK)
                for half in range(2):
                    low, high = reach(half, b - first, wide)
                    lanes = slice(half * 128, half * 128 + 128)
                    last = edge[1 if b == count - 1 and half == 1 else 0]
                    scores = buffers[i % 4][low : high - 128, lanes]
                    border = buffers[i % 4][high - 128 : high, lanes] + last
                    peak = jnp.max(border, axis=0, keepdims=True)
                    if high - 128 > low:
                        peak = jnp.maximum(peak, jnp.max(scores, axis=0, keepdims=True))
                        expo[t, h, store + low : store + high - 128, lanes] = jnp.exp(scores - peak).astype(bf16)
                    expo[t, h, store + high - 128 : store + high, lanes] = jnp.exp(border - peak).astype(bf16)
                    if low > 0:
                        expo[t, h, store : store + low, lanes] = jnp.zeros((low, 128), bf16)
                    if high < wide:
                        expo[t, h, store + high : store + wide, lanes] = jnp.zeros((wide - high, 128), bf16)
                result = mul(vt[h, :, keys], expo[t, h, store : store + wide, :])
                inv = 1.0 / result[64:72]
                inverse[t, h, :, rows] = inv
                head_rows = pl.ds(pl.multiple_of(h * HEAD_DIM, HEAD_DIM), HEAD_DIM)
                outcome[t, head_rows, rows] = result[0:64] * inv[0:1]

            score(0)
            score(1)
            for i in range(0, len(units), 2):
                if i + 2 < len(units):
                    score(i + 2)
                    score(i + 3)
                weigh(i)
                weigh(i + 1)
            return 0

        lax.fori_loop(0, HEADS // 2, attend, 0, unroll=2)

        def feed(b, _):
            rows = rows_at(b)
            turned = outcome[t, :, rows].astype(bf16).T
            middle = xbuf[rows, :] + row_of(ob_ref) + mul(turned, wout_ref[...])
            hat, scale = normalise(middle)
            normed = (hat * row_of(g2_ref) + row_of(b2_ref)).astype(bf16)
            hat2[t, rows, :] = hat
            scales[t, rows, 1:2] = scale
            normed2[t, rows, :] = normed
            for c in range(wup_ref.shape[1] // 256):
                columns = slice(c * 256, c * 256 + 256)
                hidden = mul(normed, wup_ref[:, columns]) + row_of(ub_ref)[:, columns]
                inner = hidden * 0.7071067811865476
                phi = 0.5 * lax.erf(inner) + 0.5
                bell = jnp.exp2(inner * -1.4426950408889634 * inner)
                active[t, rows, columns] = (hidden * phi).astype(bf16)
                slope[t, rows, columns] = (phi + hidden * bell * 0.3989422804014327).astype(bf16)
            total = middle + row_of(db_ref) + mul(active[t, rows, :], wdown_ref[...])
            state = total.astype(bf16)
            states[t, rows, :] = state
            xbuf[rows, :] = state.astype(f32) + emb_v[rows, :].astype(f32)
            return 0

        lax.fori_loop(0, count, feed, 0, unroll=4)
    forward(0)
    forward(1)

    for total in (sums, qv_sums):
        total[...] = jnp.zeros_like(total)
    pl.semaphore_wait(barrier, len(peers))
    state_copy().start()
    keep_state = pltpu.make_async_copy(states.at[part], states_hbm.at[part], in_sem.at[0])
    keep_state.start()

    def add_to(total, term, t):
        if t == 1:
            total[...] = term
        else:
            total[...] += term

    def add_sums(at, values):
        columns = slice(at, at + values.shape[1])
        sums[:, columns] += eight_sums(values)

    def send(now, blocks):
        @pl.when(part == 1 - now)
        def _():
            for b in blocks:
                main_copy(now, b).start()

        extra = [b for b in blocks if b // (count // 2) == 1 - now]
        if extra:
            @pl.when(part == now)
            def _():
                for b in extra:
                    extra_copy(now, b).start()

    totals = {"D": sum_down, "U": sum_up, "Q": sum_qkv, "S": sum_small}

    def perform(action):
        if action in totals:
            totals[action].step()
        else:
            send(0, [int(action)])

    def backward(t):
        def hook(point):
            if t == 0:
                for action in HOOKS.get(point, ()):
                    perform(action)

        def feed_back(b, _):
            rows = rows_at(b)
            down = grads[t + 1, rows, :]
            down_wide = down.astype(f32)
            add_sums(DB, down_wide)
            for c in range(wup_ref.shape[1] // 256):
                columns = slice(c * 256, c * 256 + 256)
                up_grad = mul_rows(down, wdown_ref[columns, :]) * slope[t, rows, columns].astype(f32)
                hgrad[rows, columns] = up_grad.astype(bf16)
                add_sums(UB + c * 256, up_grad)
            cotangent = mul_rows(hgrad[rows, :], wup_ref[...])
            hat = hat2[t, rows, :]
            add_sums(N2G, cotangent * hat)
            add_sums(N2B, cotangent)
            middle = down_wide + norm_back(cotangent, row_of(g2_ref), hat, scales[t, rows, 1:2])
            mgrad[rows, :] = middle
            low = middle.astype(bf16)
            branch[rows, :] = low
            add_sums(OB, middle)
            attended_grad = mul_rows(wout_ref[...], low).astype(bf16).astype(f32)
            line = lax.broadcasted_iota(jnp.int32, (16, BLOCK), 0)
            for h in range(HEADS):
                own = h % 2 * 64
                head = slice(h * HEAD_DIM, h * HEAD_DIM + HEAD_DIM)
                scaled = (attended_grad[head] * inverse[t, h, 0:1, rows]).astype(bf16)
                inner = -jnp.sum(scaled.astype(f32) * outcome[t, head, rows], axis=0, keepdims=True)
                high = inner.astype(bf16).astype(f32)
                extra = jnp.where(line == 0, high, jnp.where(line == 1, inner - high, 0.0))
                goa[h, own : own + 64, rows] = scaled
                goa[h, 64 - own : 80 - own, rows] = extra.astype(bf16)
            return 0

        lax.fori_loop(0, count, feed_back, 0, unroll=4)

        add_to(gdown, mul_columns(grads[t + 1], active[t]), t)
        if t == 0:
            pack(down, 0, gdown)
            clear(down, DOWN_ROWS)
            sum_down.step()

        add_to(gup, mul_columns(normed2[t], hgrad[...]), t)
        add_to(gout, mul(outcome[t].astype(bf16), branch[...]), t)

        if t == 0:
            pack(up, 0, gup)
            pack(up, OUT_AT, gout)
            clear(up, UP_ROWS)
            sum_up.step()

        buffers = (slope_a, slope_b, slope_c, slope_d)

        def slopes(i):
            b, first, store, h = units[i]
            rows = slice(b * BLOCK, b * BLOCK + BLOCK)
            keys = slice(first * BLOCK, b * BLOCK + BLOCK)
            wide = (b + 1 - first) * BLOCK
            values = mul(va[t, h, keys, :], goa[h, :, rows])
            values = expo[t, h, store : store + wide, :].astype(f32) * values
            buffers[i % 4][0:wide, :] = values.astype(bf16)

        def spread(i):
            b, first, store, h = units[i]
            rows = slice(b * BLOCK, b * BLOCK + BLOCK)
            keys = slice(first * BLOCK, b * BLOCK + BLOCK)
            wide = (b + 1 - first) * BLOCK
            head = slice(h * HEAD_DIM, h * HEAD_DIM + HEAD_DIM)
            own = slice(h % 2 * 64, h % 2 * 64 + 64)
            score_grad = buffers[i % 4][0:wide, :]
            query_part = mul(kt[t, head, keys], score_grad)
            pgrad[head, rows] = (query_part * HEAD_DIM**-0.5).astype(bf16)
            key_part = mul_rows(qa[t, h, own, rows], score_grad)
            value_part = mul_rows(goa[h, own, rows], expo[t, h, store : store + wide, :])
            for kb in range(first, b + 1):
                mine = slice((kb - first) * BLOCK, (kb - first) * BLOCK + BLOCK)
                there = slice(kb * BLOCK, kb * BLOCK + BLOCK)
                if b == min(count - 1, kb + SPAN // BLOCK):
                    dkt[head, there] = key_part[:, mine]
                    dvt[head, there] = value_part[:, mine]
                else:
                    dkt[head, there] += key_part[:, mine]
                    dvt[head, there] += value_part[:, mine]

        def input_back(b):
            rows = slice(b * BLOCK, b * BLOCK + BLOCK)
            if t == 1:
                pgrad[width : 2 * width, rows] = dkt[:, rows].astype(bf16)
                pgrad[2 * width :, rows] = dvt[:, rows].astype(bf16)
            part_grad = pgrad[:, rows]
            for lanes in (slice(0, 128), slice(128, 256)):
                qv_sums[0:width, :] += part_grad[:width, lanes].astype(f32)
                qv_sums[width:, :] += part_grad[2 * width :, lanes].astype(f32)
            cotangent = mul(wqkv_ref[...], part_grad).T
            hat = hat1[t, rows, :]
            add_sums(N1G, cotangent * hat)
            add_sums(N1B, cotangent)
            x_grad = mgrad[rows, :] + norm_back(cotangent, row_of(g1_ref), hat, scales[t, rows, 0:1])
            grads[t, rows, :] = x_grad.astype(bf16)

        last = t == 0
        units = [(*block, h) for block in reversed(blocks_of(length)[0]) for h in range(HEADS)]
        slopes(0)
        slopes(1)
        for i in range(0, len(units), 2):
            if i + 2 < len(units):
                slopes(i + 2)
                slopes(i + 3)
            spread(i)
            spread(i + 1)
            b = units[i][0]
            if units[i + 1][3] < HEADS - 1:
                continue
            if b + 1 < count and (False or not last):
                input_back(b + 1)
                if not last and True:
                    send(1, [b + 1])
            hook(f"a{b}")
        pgrad[width : 2 * width, 0:BLOCK] = dkt[:, 0:BLOCK].astype(bf16)
        pgrad[2 * width :, 0:BLOCK] = dvt[:, 0:BLOCK].astype(bf16)
        if last and not False:
            for b in range(1, count):
                rows = slice(b * BLOCK, b * BLOCK + BLOCK)
                pgrad[width : 2 * width, rows] = dkt[:, rows].astype(bf16)
                pgrad[2 * width :, rows] = dvt[:, rows].astype(bf16)
        add_to(gqkv, mul(pgrad[...], normed1[t]), t)
        if last:
            pack(qkv, 0, gqkv)
            clear(qkv, QKV_ROWS)
            sum_qkv.step()
            hook("q")
        for b in reversed(range(1 if False or not last else count)):
            input_back(b)
            hook(f"f{b}")
        if not last:
            send(1, [0] if True else range(count))

    backward(1)
    backward(0)

    sums[0:1, QB : QB + width] = jnp.sum(qv_sums[0:width, :].T, axis=0, keepdims=True)
    sums[0:1, VB : VB + width] = jnp.sum(qv_sums[width:, :].T, axis=0, keepdims=True)
    total = jnp.sum(sums[...], axis=0, keepdims=True)
    small[...] = jnp.concatenate([total[:, i * 128 : i * 128 + 128] for i in range(SUMS // 128)], axis=0)
    sum_small.step()
    half_rows = pl.ds(pl.multiple_of(part * (length // 2), BLOCK), length // 2)
    keep_grad = pltpu.make_async_copy(grads.at[part], grads_hbm.at[part], in_sem.at[1])
    keep_extra = pltpu.make_async_copy(grads.at[1 - part, half_rows], extra_hbm.at[part], in_sem.at[2])
    keep_grad.start()
    keep_extra.start()
    for action in "SDUSQDUSQDUSQDU":
        perform(action)

    state_copy().wait()
    for b in range(count):
        main_copy(0, b).wait()
    for b in range(count // 2):
        extra_copy(0, b).wait()
    for keep in (keep_state, keep_grad, keep_extra, sum_small.keep, sum_down.keep, sum_up.keep, sum_qkv.keep):
        keep.wait()


def padded(rows, devices):
    unit = 16 * devices
    return (rows + unit - 1) // unit * unit


def finish_kernel(
    states_hbm, grads_hbm, extra_hbm, down_hbm, up_hbm, qkv_hbm, small_hbm,
    loop_out, grad_out, embed_out, n1g, n1b, gqkv, qb, vb, gout, ob, n2g, n2b, gup, ub, gdown, db,
    states, grads, extra, down, up, qkv, small, grad_v, embed_v, gqkv_v, gout_v, gup_v, gdown_v, sems,
):
    part = lax.axis_index("section")
    length, width = grads.shape[1:]

    def copy(at, src, dst):
        return pltpu.make_async_copy(src, dst, sems.at[at])

    passed = copy(0, states_hbm, states)
    loads = [
        copy(1, grads_hbm, grads), copy(2, extra_hbm, extra), copy(3, up_hbm, up), copy(4, down_hbm, down),
        copy(12, qkv_hbm, qkv), copy(13, small_hbm, small),
    ]
    passed.start()
    for load in loads:
        load.start()
    passed.wait()
    stores = [copy(11, states, loop_out.at[0])]
    stores[-1].start()
    loads[0].wait()
    grad_v[...] = grads[...].astype(f32)
    stores.append(copy(5, grad_v, grad_out.at[0]))
    stores[-1].start()
    loads[1].wait()
    half_rows = pl.ds(pl.multiple_of(part * (length // 2), BLOCK), length // 2)
    embed_v[...] = grads[:, half_rows, :].astype(f32) + extra[...].astype(f32)
    stores.append(copy(6, embed_v, embed_out))
    stores[-1].start()
    loads[2].wait()
    for i in range(gup_v.shape[1] // 128):
        lanes = slice(i * 128, i * 128 + 128)
        gup_v[:, lanes] = up[i * width : (i + 1) * width, :].astype(f32)
    stores.append(copy(7, gup_v, gup))
    stores[-1].start()
    for i in range(width // 128):
        at = OUT_AT + i * width
        gout_v[:, i * 128 : i * 128 + 128] = up[at : at + width, :].astype(f32)
    stores.append(copy(9, gout_v, gout))
    stores[-1].start()
    loads[3].wait()
    for i in range(gup_v.shape[1] // 128):
        gdown_v[i * 128 : i * 128 + 128, :] = down[i * width : (i + 1) * width, :].T.astype(f32)
    stores.append(copy(8, gdown_v, gdown))
    stores[-1].start()
    loads[4].wait()
    for i in range(width // 128):
        turned = qkv[i * 3 * width : (i + 1) * 3 * width, :].T
        gqkv_v[i * 128 : i * 128 + 128, :] = turned.astype(f32)
    stores.append(copy(10, gqkv_v, gqkv))
    stores[-1].start()
    loads[5].wait()
    for at, ref in ((N1G, n1g), (N1B, n1b), (QB, qb), (VB, vb), (OB, ob), (N2G, n2g), (N2B, n2b), (DB, db), (UB, ub)):
        for i in range(ref.shape[0] // 128):
            ref[i * 128 : i * 128 + 128] = small[at // 128 + i]
    for store in stores:
        store.wait()


def whole_block(sections, places, *args):
    start = args[0]
    _, length, width = start.shape
    hidden = args[15].shape[0]
    vmem = pl.BlockSpec(memory_space=pltpu.VMEM)
    smem = pl.BlockSpec(memory_space=pltpu.SMEM)
    hbm = pl.BlockSpec(memory_space=pl.ANY)
    count = length // BLOCK
    devices = sections * places
    far_count = places // 4
    payloads = [padded(rows, devices) for rows in (DOWN_ROWS, UP_ROWS, QKV_ROWS)]

    def V(*shape, dtype=bf16):
        return pltpu.VMEM(shape, dtype)

    def O(*shape, dtype=f32):
        return jax.ShapeDtypeStruct(shape, dtype)

    def sum_buffers(rows):
        return [
            V(rows, 128),
            V(rows // 2, 128),
            V(3, rows // 8, 128),
            V(far_count - 1, rows // devices, 128),
            V(rows, 128),
        ]

    copies = 2 * (6 + 2 * far_count) + devices + 2 + far_count
    between = pl.pallas_call(
        partial(compute_kernel, far_count),
        name="block_both_ways",
        in_specs=[hbm, hbm, hbm, vmem, smem] + [vmem] * 13,
        out_specs=[hbm] * 7,
        out_shape=[
            O(2, length, width, dtype=bf16),
            O(2, length, width, dtype=bf16),
            O(2, length // 2, width, dtype=bf16),
            *(O(rows, 128, dtype=bf16) for rows in payloads),
            O(SUMS // 128, 128),
        ],
        scratch_shapes=[
            V(length, width),
            V(length, width),
            V(length, 128),
            V(width, width),
            V(width, 128, dtype=f32),
            V(2, 128, 128, dtype=f32),
            V(SPAN + BLOCK, BLOCK, dtype=f32),
            V(SPAN + BLOCK, BLOCK, dtype=f32),
            V(SPAN + BLOCK, BLOCK, dtype=f32),
            V(SPAN + BLOCK, BLOCK, dtype=f32),
            V(SPAN + BLOCK, BLOCK),
            V(SPAN + BLOCK, BLOCK),
            V(SPAN + BLOCK, BLOCK),
            V(SPAN + BLOCK, BLOCK),
            V(length, width, dtype=f32),
            V(2, length, width, dtype=f32),
            V(2, length, 128, dtype=f32),
            V(2, length, width),
            V(2, HEADS, 128, length),
            V(HEADS, length, 128),
            V(2, width, length),
            V(2, HEADS, length, 128),
            V(HEADS, 80, length),
            V(2, HEADS, blocks_of(length)[1], BLOCK),
            V(2, HEADS, 8, length, dtype=f32),
            V(2, width, length, dtype=f32),
            V(2, length, width, dtype=f32),
            V(2, length, width),
            V(2, length, hidden),
            V(2, length, hidden),
            V(length, hidden),
            V(length, width),
            V(length, width, dtype=f32),
            V(3, length, width),
            V(2, length, width),
            V(HEADS, 128, length),
            V(width, length, dtype=f32),
            V(width, length, dtype=f32),
            V(3 * width, length),
            V(3 * width, width, dtype=f32),
            V(width, width, dtype=f32),
            V(width, hidden, dtype=f32),
            V(width, hidden, dtype=f32),
            V(8, SUMS, dtype=f32),
            V(2 * width, 128, dtype=f32),
        ]
        + sum_buffers(payloads[0])
        + sum_buffers(payloads[1])
        + [
            V(payloads[2], 128),
            V(payloads[2] // 2, 128),
            V(devices // 2 - 1, payloads[2] // devices, 128),
            V(payloads[2], 128),
        ]
        + [
            V(SUMS // 128, 128, dtype=f32),
            V(2 + far_count, SUMS // 128, 128, dtype=f32),
            pltpu.SemaphoreType.DMA((7,)),
            pltpu.SemaphoreType.DMA((1 + count + count // 2,)),
            pltpu.SemaphoreType.DMA((1 + count + count // 2,)),
            pltpu.SemaphoreType.DMA((copies,)),
            pltpu.SemaphoreType.DMA((copies,)),
        ],
        compiler_params=pltpu.CompilerParams(
            vmem_limit_bytes=63 << 20, collective_id=0, has_side_effects=True
        ),
    )(*args)
    return pl.pallas_call(
        finish_kernel,
        name="widen",
        in_specs=[hbm] * 7,
        out_specs=[hbm, hbm, hbm, vmem, vmem, hbm, vmem, vmem, hbm, vmem, vmem, vmem, hbm, vmem, hbm, vmem],
        out_shape=[
            O(1, 2, length, width, dtype=bf16),
            O(1, 2, length, width),
            O(2, length // 2, width),
            O(width), O(width), O(width, 3 * width), O(width), O(width), O(width, width), O(width),
            O(width), O(width), O(width, hidden), O(hidden), O(hidden, width), O(width),
        ],
        scratch_shapes=[
            V(2, length, width),
            V(2, length, width),
            V(2, length // 2, width),
            V(payloads[0], 128),
            V(payloads[1], 128),
            V(payloads[2], 128),
            V(SUMS // 128, 128, dtype=f32),
            V(2, length, width, dtype=f32),
            V(2, length // 2, width, dtype=f32),
            V(width, 3 * width, dtype=f32),
            V(width, width, dtype=f32),
            V(width, hidden, dtype=f32),
            V(hidden, width, dtype=f32),
            pltpu.SemaphoreType.DMA((14,)),
        ],
        compiler_params=pltpu.CompilerParams(vmem_limit_bytes=63 << 20),
    )(*between)


def solution(mesh):
    rows = P("dp", None, None)
    return jax.shard_map(
        partial(whole_block, mesh.shape["section"], mesh.shape["dp"]),
        mesh=mesh,
        in_specs=(rows, rows, rows, P("dp", None), P("dp")) + (P(),) * 13,
        out_specs=(
            P("section", "dp", None, None),
            P("section", "dp", None, None),
            P("dp", "section", None),
        )
        + (P(),) * 13,
        check_vma=False,
    )
```
